128 devices in a mesh: seq: 64 (over y, z, x_hi, core), rep: 2 (over x_lo).
Axes of the slice: x: 4 (x_hi: 2, x_lo: 2; x = x_hi * 2 + x_lo), y: 4, z: 4, core: 2. Of those that a mesh axis runs over, the one named last changes fastest.
Arguments:
- inputs: bfloat16 [2, 8192, 1152], P('rep', 'seq'), may hold values from -6 to 6
- out_grad: bfloat16 [2, 8192, 1152], P('rep', 'seq'), may hold values from -6 to 6
- doc_ids: int32 [2, 128], P('rep'), may hold values from 0 to 2, as said below
- owners: int32 [91], replicated, may hold values from 0 to 127, as said below
- masters: float32 [128, 1152, 256], P(('seq', 'rep')), may hold values from -0.1875 to 0.1875
- first_old: float32 [128, 1152, 256], P(('seq', 'rep'))
- second_old: float32 [128, 1152, 256], P(('seq', 'rep')), as said below
- left_basis: float32 [128, 1152, 1152], P(('seq', 'rep')), may hold values from -1 to 1, as said below
- right_basis: float32 [128, 256, 256], P(('seq', 'rep')), may hold values from -1 to 1, as said below
- gains: float32 [5120], replicated, may hold values from 0.5 to 1.5
- gain_first: float32 [5120], replicated, may hold values from -384 to 384
- gain_second: float32 [5120], replicated, may hold values from 16384 to 65536
Outputs:
- layer_out: bfloat16 [2, 8192, 1152], P('rep', 'seq')
- input_grad: float32 [2, 8192, 1152], P('rep', 'seq')
- new_masters: float32 [128, 1152, 256], P(('seq', 'rep'))
- new_first: float32 [128, 1152, 256], P(('seq', 'rep'))
- new_second: float32 [128, 1152, 256], P(('seq', 'rep'))
- new_gains: float32 [5120], replicated
- new_gain_first: float32 [5120], replicated
- new_gain_second: float32 [5120], replicated
The draws below stay inside these ranges and needn't reach their ends.
Inputs may be any that keep to these rules, and one draw needn't show every extreme that they name: `doc_ids`: along each sequence the ids never fall; they start at 0 and end at 2. `owners`: no two tiles share a slot. `second_old`: Positive. `left_basis`: each slot's matrix is orthogonal. `right_basis`: each slot's matrix is orthogonal.
All inputs are finite; a program needn't handle non-finite values.
Results may differ from the reference program's by a relative error of at most 0.02.
Values may be sent and summed in bfloat16 or wider, within the bound.
A program may use at most 512 MiB of HBM per device.

```python
import math
import jax
import jax.numpy as jnp
from jax import lax

D = 1152
FF = 6912
HEADS = 4
HD = 256
WINDOW = 512
BLK = 64
DOCS = 3
STEP = 10
LENGTH = 8192
SEQS = 2
TOKENS = 16384
NB = 128
TILES = 91
SLOTS_ALL = 128
GAINS = 5120


def owner_table(key):
    middle = jax.random.permutation(jax.random.fold_in(key, 101), SLOTS_ALL - 2).astype(jnp.int32) + 1
    chosen = jnp.concatenate([middle[:TILES - 2], jnp.array([0, SLOTS_ALL - 1], dtype=jnp.int32)])
    order = jax.random.permutation(jax.random.fold_in(key, 102), TILES)
    return chosen[order].astype(jnp.int32)


def slot_scale(key):
    table = owner_table(key)
    tile_index = jnp.arange(TILES, dtype=jnp.int32)
    per_tile = jnp.where(tile_index < HEADS + 2, 0.7, jnp.where(tile_index < 2 * HEADS + 2, 1.0, 0.4)).astype(jnp.float32)
    per_slot = jnp.full((SLOTS_ALL,), 0.4, jnp.float32).at[table].set(per_tile)
    return per_slot * math.sqrt(TOKENS)


def orthogonal_table(key, order_size):
    row_perm = jax.random.permutation(jax.random.fold_in(key, 1), order_size).astype(jnp.int32)
    col_perm = jax.random.permutation(jax.random.fold_in(key, 2), order_size).astype(jnp.int32)
    row_sign = jnp.where(jax.random.bernoulli(jax.random.fold_in(key, 3), 0.5, (order_size,)), 1.0, -1.0)
    col_sign = jnp.where(jax.random.bernoulli(jax.random.fold_in(key, 4), 0.5, (order_size,)), 1.0, -1.0)
    product = (2 * row_perm[:, None] + 1) * (2 * col_perm[None, :] + 1) % (8 * order_size)
    angle = math.pi * product.astype(jnp.float32) / (4.0 * order_size)
    wave = jnp.cos(angle)
    return (row_sign[:, None] * col_sign[None, :] * math.sqrt(2.0 / order_size) * wave).astype(jnp.float32)


def draw_owners(key, part):
    table = owner_table(key)
    return table


def draw_doc_ids(key, part):
    key = jax.random.fold_in(key, 7)

    def one_sequence(seq_key):
        picks = jax.random.permutation(seq_key, NB - 1)[:DOCS - 1].astype(jnp.int32) + 1
        starts = jnp.zeros((NB,), jnp.int32).at[picks].set(1)
        return jnp.cumsum(starts).astype(jnp.int32)
    return jax.vmap(one_sequence)(jax.random.split(key, SEQS))


def draw_first_old(key, part):
    scales = slot_scale(key)
    key = jax.random.fold_in(key, 3)
    base = jax.random.truncated_normal(key, -3.0, 3.0, (SLOTS_ALL, D, HD), jnp.float32)
    return base * scales[:, None, None]


def draw_second_old(key, part):
    scales = slot_scale(key)
    key = jax.random.fold_in(key, 4)
    base = jnp.exp(jax.random.uniform(key, (SLOTS_ALL, D, HD), jnp.float32, 0.0, math.log(4.0)))
    return base * (scales * scales)[:, None, None]


def draw_left_basis(key, part):
    key = jax.random.fold_in(key, 5)
    keys = jax.random.split(key, SLOTS_ALL)
    return jax.vmap(lambda one_key: orthogonal_table(one_key, D))(keys)


def draw_right_basis(key, part):
    key = jax.random.fold_in(key, 6)
    keys = jax.random.split(key, SLOTS_ALL)
    return jax.vmap(lambda one_key: orthogonal_table(one_key, HD))(keys)


def steps_of(own_key, dims, cuts, least, top_value):
    loudness = 1.0
    for axis_at, blocks in cuts:
        heights = jax.random.uniform(jax.random.fold_in(jax.random.fold_in(own_key, 6), axis_at), (blocks,), jnp.float32, least / len(cuts), top_value / len(cuts))
        loudness = loudness * jnp.repeat(jnp.exp(heights), dims[axis_at] // blocks).reshape((-1,) + (1,) * (len(dims) - 1 - axis_at))
    return loudness


def normal_values(stream_key, extent, width, limit, pieces=(), kind=jnp.bfloat16):
    values = jax.random.normal(stream_key, extent, jnp.float32) * width
    if len(pieces) > 0:
        values = steps_of(stream_key, extent, pieces, -0.22, 0.18) * values
    return jnp.clip(values, min=-limit, max=limit).astype(kind)


def setup_inputs(seed: int = 0) -> dict:
    key_of = jax.random.split(jax.random.key(seed), 13)
    inputs = normal_values(key_of[0], (SEQS, LENGTH, D), 1.0, 6.0, ((0, 2), (1, 64)))
    out_grad = normal_values(key_of[1], (SEQS, LENGTH, D), 1.0, 6.0, ((0, 2), (1, 64)))
    doc_ids = draw_doc_ids(jax.random.fold_in(key_of[12], 71), 0)
    owners = draw_owners(jax.random.fold_in(key_of[12], 71), 0)
    masters = normal_values(key_of[4], (SLOTS_ALL, D, HD), D ** -0.5, 0.1875, ((0, 128),), jnp.float32)
    first_old = draw_first_old(jax.random.fold_in(key_of[12], 71), 0)
    second_old = draw_second_old(jax.random.fold_in(key_of[12], 71), 0)
    left_basis = draw_left_basis(jax.random.fold_in(key_of[12], 71), 0)
    right_basis = draw_right_basis(jax.random.fold_in(key_of[12], 71), 0)
    gains = jnp.clip(1.0 + 0.1 * jax.random.normal(key_of[9], (GAINS,), jnp.float32), 0.5, 1.5)
    gain_first = normal_values(key_of[10], (GAINS,), (TOKENS ** 0.5), 384.0, (), jnp.float32)
    gain_second = jnp.clip(jnp.exp(jax.random.uniform(key_of[11], (GAINS,), jnp.float32, math.log(16384.0), math.log(65536.0))), 16384.0, 65536.0)
    return {"inputs": inputs, "out_grad": out_grad, "doc_ids": doc_ids, "owners": owners, "masters": masters, "first_old": first_old, "second_old": second_old, "left_basis": left_basis, "right_basis": right_basis, "gains": gains, "gain_first": gain_first, "gain_second": gain_second}


@jax.custom_vjp
def low(v):
    return lax.optimization_barrier(v.astype(jnp.bfloat16)).astype(jnp.float32)

@jax.custom_vjp
def low_back(v):
    return v

def low_keep(v):
    return (low(v), None)

def low_pass(kept, grad):
    return (grad,)

def back_keep(v):
    return (v, None)

def back_low(kept, grad):
    return (low(grad),)
low.defvjp(low_keep, low_pass)
low_back.defvjp(back_keep, back_low)
NORM_EPS = 1e-06
THETA = 10000.0
BETA_ONE = 0.5
BETA_TWO = 0.5
RATE = 0.02
GAIN_RATE = 0.4
DECAY = 0.01
ADAM_EPS = 1e-08
HIGH = lax.Precision.HIGHEST

def rms_norm(values, gain):
    return values * lax.rsqrt(lax.optimization_barrier(jnp.mean(values * values, axis=-1, keepdims=True)) + NORM_EPS) * gain

def rotary(values, positions):
    half = values.shape[-1] // 2
    freq = jnp.exp(-jnp.log(THETA) * jnp.arange(half, dtype=jnp.float32) * 2.0 / values.shape[-1])
    angle = positions.astype(jnp.float32)[:, None] * freq[None, :]
    shape = (values.shape[0],) + (1,) * (values.ndim - 2) + (half,)
    cosine = jnp.cos(angle).reshape(shape)
    sine = jnp.sin(angle).reshape(shape)
    first = values[..., :half]
    second = values[..., half:]
    return jnp.concatenate([first * cosine - second * sine, second * cosine + first * sine], axis=-1)

def layer(inputs, tiles, gains, docs):
    model_width = inputs.shape[1]
    length = inputs.shape[0]
    head_dim = tiles.shape[2]
    ff_tiles = FF // head_dim
    g_apre = gains[0:model_width]
    g_apost = gains[model_width:2 * model_width]
    g_fpre = gains[2 * model_width:3 * model_width]
    g_fpost = gains[3 * model_width:4 * model_width]
    g_query = gains[4 * model_width:4 * model_width + head_dim]
    g_key = gains[4 * model_width + head_dim:]
    w_query = tiles[0:HEADS]
    w_key = tiles[HEADS]
    w_value = tiles[HEADS + 1]
    w_out = tiles[HEADS + 2:2 * HEADS + 2]
    base = 2 * HEADS + 2
    w_gate = tiles[base:base + ff_tiles]
    w_up = tiles[base + ff_tiles:base + 2 * ff_tiles]
    w_down = tiles[base + 2 * ff_tiles:base + 3 * ff_tiles]
    positions = jnp.arange(length, dtype=jnp.int32)
    normed_in = low(rms_norm(inputs, g_apre))
    queries_raw = low_back(jnp.einsum('td,hdc->thc', normed_in, w_query, precision=HIGH))
    keys_raw = low_back(jnp.dot(normed_in, w_key, precision=HIGH))
    values_raw = low_back(jnp.dot(normed_in, w_value, precision=HIGH))
    queries = low(rotary(rms_norm(queries_raw, g_query), positions))
    keys = low(rotary(rms_norm(keys_raw, g_key), positions))
    values = low(values_raw)
    key_pad = jnp.concatenate([jnp.zeros((WINDOW, head_dim), jnp.float32), keys])
    value_pad = jnp.concatenate([jnp.zeros((WINDOW, head_dim), jnp.float32), values])
    doc_pad = jnp.concatenate([jnp.full((WINDOW,), -1, jnp.int32), docs.astype(jnp.int32)])
    score_scale = head_dim ** (-0.5)

    def block(index):
        first_row = (index * WINDOW).astype(jnp.int32)
        query_block = lax.dynamic_slice_in_dim(queries, first_row, WINDOW, 0)
        key_block = lax.dynamic_slice_in_dim(key_pad, first_row, 2 * WINDOW, 0)
        value_block = lax.dynamic_slice_in_dim(value_pad, first_row, 2 * WINDOW, 0)
        query_docs = lax.dynamic_slice_in_dim(docs.astype(jnp.int32), first_row, WINDOW, 0)
        key_docs = lax.dynamic_slice_in_dim(doc_pad, first_row, 2 * WINDOW, 0)
        query_pos = first_row + jnp.arange(WINDOW, dtype=jnp.int32)
        key_pos = first_row - WINDOW + jnp.arange(2 * WINDOW, dtype=jnp.int32)
        visible = (key_docs[None, :] == query_docs[:, None]) & (key_pos[None, :] <= query_pos[:, None])
        visible = visible & (query_pos[:, None] - key_pos[None, :] < WINDOW) & (key_pos[None, :] >= 0)
        scores = low_back(jnp.einsum('thc,kc->thk', query_block, key_block, precision=HIGH)) * score_scale
        scores = jnp.where(visible[:, None, :], scores, -1e+30)
        row_top = lax.optimization_barrier(jnp.max(scores, axis=-1, keepdims=True))
        expo = jnp.exp(scores - row_top)
        probs = expo / lax.optimization_barrier(jnp.sum(expo, axis=-1, keepdims=True))
        return low(low_back(jnp.einsum('thk,kc->thc', low(probs), value_block, precision=HIGH)))
    block_count = length // WINDOW
    mixed = lax.map(jax.checkpoint(block), jnp.arange(block_count, dtype=jnp.int32))
    mixed = mixed.reshape(length, HEADS, head_dim)
    projected = low_back(jnp.einsum('thc,hdc->td', mixed, w_out, precision=HIGH))
    residual_one = inputs + rms_norm(projected, g_apost)
    normed_ffn = low(rms_norm(residual_one, g_fpre))
    gate_pre = low_back(jnp.einsum('td,kdc->tkc', normed_ffn, w_gate, precision=HIGH))
    up_pre = low_back(jnp.einsum('td,kdc->tkc', normed_ffn, w_up, precision=HIGH))
    hidden = low(jax.nn.gelu(gate_pre, approximate=True) * up_pre)
    down = low_back(jnp.einsum('tkc,kdc->td', hidden, w_down, precision=HIGH))
    return residual_one + rms_norm(down, g_fpost)

def reference(inputs, out_grad, doc_ids, owners, masters, first_old, second_old, left_basis, right_basis, gains, gain_first, gain_second):
    tiles = lax.optimization_barrier(masters[owners].astype(jnp.bfloat16)).astype(jnp.float32)

    def one_sequence(carry, item):
        tile_sum, gain_sum = carry
        seq_in, seq_grad, seq_docs = item
        docs = jnp.repeat(seq_docs.astype(jnp.int32), BLK, total_repeat_length=LENGTH)
        result, pull = jax.vjp(lambda x_in, t_in, g_in: layer(x_in, t_in, g_in, docs), seq_in.astype(jnp.float32), tiles, gains)
        d_in, d_tiles, d_gains = pull(seq_grad.astype(jnp.float32))
        return ((tile_sum + d_tiles, gain_sum + d_gains), (result.astype(jnp.bfloat16), d_in))
    start_sums = (jnp.zeros_like(tiles), jnp.zeros_like(gains))
    (tile_grads, gain_grads), (layer_out, input_grad) = lax.scan(one_sequence, start_sums, (inputs, out_grad, doc_ids))

    def update(item):
        grad, slot = item
        left = left_basis[slot]
        right = right_basis[slot]
        rotated = jnp.dot(jnp.dot(left.T, grad, precision=HIGH), right, precision=HIGH)
        first = BETA_ONE * first_old[slot] + (1.0 - BETA_ONE) * rotated
        second = BETA_TWO * second_old[slot] + (1.0 - BETA_TWO) * rotated * rotated
        normed = first / (1.0 - BETA_ONE ** STEP) / (jnp.sqrt(second / (1.0 - BETA_TWO ** STEP)) + ADAM_EPS)
        back = jnp.dot(jnp.dot(left, normed, precision=HIGH), right.T, precision=HIGH)
        weight = masters[slot]
        return (first, second, weight - RATE * (back + DECAY * weight))
    firsts, seconds, weights = lax.map(update, (tile_grads, owners))
    new_masters = masters.at[owners].set(weights)
    new_first = first_old.at[owners].set(firsts)
    new_second = second_old.at[owners].set(seconds)
    new_gain_first = BETA_ONE * gain_first + (1.0 - BETA_ONE) * gain_grads
    new_gain_second = BETA_TWO * gain_second + (1.0 - BETA_TWO) * gain_grads * gain_grads
    gain_step = new_gain_first / (1.0 - BETA_ONE ** STEP) / (jnp.sqrt(new_gain_second / (1.0 - BETA_TWO ** STEP)) + ADAM_EPS)
    new_gains = gains - GAIN_RATE * gain_step
    return (layer_out, input_grad, new_masters, new_first, new_second, new_gains, new_gain_first, new_gain_second)
```

```python
import functools

import jax
import jax.numpy as jnp
from jax import lax
from jax.experimental import pallas as pl
from jax.experimental.pallas import tpu as pltpu
from jax.sharding import Mesh
from jax.sharding import PartitionSpec as P

FF = 6912
HEADS = 4
WINDOW = 512
BLK = 64
STEP = 10
D = 1152
HD = 256
TOK = 128
GROUP = 8
SLICE = HD // GROUP
ATT = 2 * HEADS + 2
FFT = FF // HD

NORM_EPS = 1e-06
THETA = 10000.0
BETA_ONE = 0.5
BETA_TWO = 0.5
RATE = 0.02
GAIN_RATE = 0.4
DECAY = 0.01
ADAM_EPS = 1e-08

MESH = pl.DeviceIdType.MESH
AXES = ("y", "z", "xh", "core", "xl")
VMEM_LIMIT = 56 * 1024 * 1024
BF = jnp.bfloat16
F32 = jnp.float32


def here():
    y, z, xh, c, xl = [lax.axis_index(a) for a in AXES]
    return y, z, xh * 2 + xl, c


def place(y, z, x, c):
    return (y, z, x // 2, c, lax.rem(x, 2))


def member(x, c):
    return (x // 2) * 4 + c * 2 + lax.rem(x, 2)


def of_member(q):
    return (q // 4) * 2 + q % 2, (q // 2) % 2


def turn(a, d):
    return lax.rem(a + d, 4)


def greet(places):
    sem = pltpu.get_barrier_semaphore()
    for p in places:
        pl.semaphore_signal(sem, inc=1, device_id=p, device_id_type=MESH)
    pl.semaphore_wait(sem, len(places))


def remote(src, dst, send, recv, where):
    return pltpu.make_async_remote_copy(src, dst, send, recv, device_id=where, device_id_type=MESH)


def params(cid):
    return pltpu.CompilerParams(
        collective_id=cid, has_side_effects=True, vmem_limit_bytes=VMEM_LIMIT
    )


ANY = pl.BlockSpec(memory_space=pl.ANY)
INV = pl.BlockSpec(memory_space=pltpu.VMEM)
DMA = pltpu.SemaphoreType.DMA


def gather_body(x_ref, o_ref, own_sem, xs, xr, cs, cr):
    y, z, x, c = here()
    peers = [place(y, z, turn(x, d), c) for d in (1, 2, 3)]
    twin = place(y, z, x, 1 - c)
    greet(peers + [twin])
    mine = o_ref.at[:, member(x, c)]
    own = pltpu.make_async_copy(x_ref, mine, own_sem)
    far = [remote(x_ref, mine, xs.at[i], xr.at[i], p) for i, p in enumerate(peers)]
    for i in (1, 0, 2):
        far[i].start()
    near = [remote(x_ref, mine, cs.at[3], cr.at[3], twin)]
    near[0].start()
    own.start()
    for i in (0, 2, 1):
        far[i].wait_recv()
        src = o_ref.at[:, member(turn(x, 3 - i), c)]
        step = remote(src, src, cs.at[i], cr.at[i], twin)
        step.start()
        near.append(step)
    own.wait()
    for step in near:
        step.wait()
    for step in far:
        step.wait_send()


def gather_group(x, cid):
    n, r, w = x.shape
    return pl.pallas_call(
        gather_body,
        out_shape=jax.ShapeDtypeStruct((n, GROUP, r, w), x.dtype),
        in_specs=[ANY],
        out_specs=ANY,
        scratch_shapes=[DMA, DMA((3,)), DMA((3,)), DMA((4,)), DMA((4,))],
        compiler_params=params(cid),
    )(x)


def sum_body(x_ref, o_ref, own, near, part, far, own_sem, cs, cr, xs, xr):
    y, z, x, c = here()
    peers = [place(y, z, turn(x, d), c) for d in (1, 2, 3)]
    twin = place(y, z, x, 1 - c)
    greet(peers + [twin])
    n = x_ref.shape[0]
    swap, load = [], []
    for k, d in enumerate((2, 1, 3, 0)):
        xd = turn(x, d)
        swap.append(remote(x_ref.at[:, xd // 2, 1 - c, lax.rem(xd, 2)], near.at[k], cs.at[k], cr.at[k], twin))
        load.append(pltpu.make_async_copy(x_ref.at[:, xd // 2, c, lax.rem(xd, 2)], own.at[k], own_sem.at[k]))
        swap[-1].start()
        load[-1].start()
    sends = []
    for k, d in enumerate((2, 1, 3, 0)):
        load[k].wait()
        swap[k].wait_recv()

        def add(i, carry, k=k):
            part[k, i] = (own[k, i].astype(F32) + near[k, i].astype(F32)).astype(BF)
            return carry

        if d:
            lax.fori_loop(0, n, add, 0)
            step = remote(part.at[k], far.at[k], xs.at[k], xr.at[k], peers[d - 1])
            step.start()
            sends.append(step)
    for step in sends:
        step.wait_recv()

    def total(i, carry):
        first = own[3, i].astype(F32) + near[3, i].astype(F32)
        o_ref[i] = ((first + far[0, i].astype(F32)) + far[1, i].astype(F32)) + far[2, i].astype(F32)
        return carry

    lax.fori_loop(0, n, total, 0)
    for step in swap + sends:
        step.wait_send()


def sum_group(x, cid):
    n, _, r, w = x.shape
    blk = (n, r, w)
    return pl.pallas_call(
        sum_body,
        out_shape=jax.ShapeDtypeStruct(blk, F32),
        in_specs=[ANY],
        out_specs=INV,
        scratch_shapes=[
            pltpu.VMEM((4,) + blk, BF),
            pltpu.VMEM((4,) + blk, BF),
            pltpu.VMEM((3,) + blk, BF),
            pltpu.VMEM((3,) + blk, BF),
            DMA((4,)),
            DMA((4,)),
            DMA((4,)),
            DMA((3,)),
            DMA((3,)),
        ],
        compiler_params=params(cid),
    )(x.reshape(n, 2, 2, 2, r, w))


def weights_body(t_ref, o_ref, own_sem, gs, gr, s1, r1, s2, r2):
    y, z, x, c = here()
    me = member(x, c)
    friends = []
    for dx in range(4):
        for dc in range(2):
            if dx or dc:
                friends.append((turn(x, dx), lax.rem(c + dc, 2)))
    ring_z = [place(y, turn(z, d), x, c) for d in (1, 2, 3)]
    ring_y = [place(turn(y, d), z, x, c) for d in (1, 2, 3)]
    greet([place(y, z, *f) for f in friends] + ring_z + ring_y)
    mine = o_ref.at[y, z, me // 4, lax.rem(me, 4)]
    spread = []
    for i, f in enumerate(friends):
        step = remote(t_ref.at[member(*f)], mine, gs.at[i], gr.at[i], place(y, z, *f))
        step.start()
        spread.append(step)
    own = pltpu.make_async_copy(t_ref.at[me], mine, own_sem)
    own.start()
    own.wait()
    for step in spread:
        step.wait_recv()
    first = []
    for i in (1, 0, 2):
        a = remote(o_ref.at[y, z, 0], o_ref.at[y, z, 0], s1.at[0, i], r1.at[0, i], ring_z[i])
        b = remote(o_ref.at[y, z, 1], o_ref.at[y, z, 1], s1.at[1, i], r1.at[1, i], ring_y[i])
        a.start()
        b.start()
        first.append((i, a, b))
    second = []

    def onward(j, yy, zz):
        for i in (1, 0, 2):
            ra = o_ref.at[y, zz, 0]
            rb = o_ref.at[yy, z, 1]
            a = remote(ra, ra, s2.at[0, j, i], r2.at[0, j, i], ring_y[i])
            b = remote(rb, rb, s2.at[1, j, i], r2.at[1, j, i], ring_z[i])
            a.start()
            b.start()
            second.extend([a, b])

    onward(3, y, z)
    order = sorted(first, key=lambda f: (f[0] == 1, f[0]))
    for i, a, b in order:
        a.wait_recv()
        b.wait_recv()
        onward(i, turn(y, 3 - i), turn(z, 3 - i))
    for step in second:
        step.wait()
    for i, a, b in first:
        a.wait_send()
        b.wait_send()
    for step in spread:
        step.wait_send()


def gather_slices(tile, cid):
    return pl.pallas_call(
        weights_body,
        out_shape=jax.ShapeDtypeStruct((4, 4, 2, 4, SLICE, D), BF),
        in_specs=[ANY],
        out_specs=ANY,
        scratch_shapes=[
            DMA,
            DMA((7,)),
            DMA((7,)),
            DMA((2, 3)),
            DMA((2, 3)),
            DMA((2, 4, 3)),
            DMA((2, 4, 3)),
        ],
        compiler_params=params(cid),
    )(tile)


def grads_body(
    d_ref, g_ref, o_ref, go_ref,
    own1, in1, mid, in2, fin, gin, gmid, gin2,
    own_sem, s1, r1, s2, r2, gs, gr, gas, gar, gbs, gbr,
):
    y, z, x, c = here()
    me = member(x, c)
    friends = []
    for dx in range(4):
        for dc in range(2):
            if dx or dc:
                friends.append((turn(x, dx), lax.rem(c + dc, 2)))
    ring_z = [place(y, turn(z, d), x, c) for d in (1, 2, 3)]
    ring_y = [place(turn(y, d), z, x, c) for d in (1, 2, 3)]
    group = [place(y, z, *f) for f in friends]
    greet(group + ring_z + ring_y)
    first = []
    for i in (1, 0, 2):
        a = remote(d_ref.at[turn(y, i + 1), :, 0], in1.at[0, i], s1.at[0, i], r1.at[0, i], ring_y[i])
        b = remote(d_ref.at[:, turn(z, i + 1), 1], in1.at[1, i], s1.at[1, i], r1.at[1, i], ring_z[i])
        a.start()
        b.start()
        first.extend([a, b])
    la = pltpu.make_async_copy(d_ref.at[y, :, 0], own1.at[0], own_sem.at[0])
    lb = pltpu.make_async_copy(d_ref.at[:, z, 1], own1.at[1], own_sem.at[1])
    la.start()
    lb.start()
    gains = []
    for i, p in enumerate(group):
        step = remote(g_ref, gin.at[i], gas.at[i], gar.at[i], p)
        step.start()
        gains.append(step)
    for step in gains:
        step.wait_recv()
    acc = g_ref[...]
    for i in range(7):
        acc = acc + gin[i]
    gmid[0] = acc
    more = []
    for i, p in enumerate(ring_z):
        step = remote(gmid.at[0], gin2.at[0, i], gbs.at[0, i], gbr.at[0, i], p)
        step.start()
        more.append(step)
    for step in more:
        step.wait_recv()
    gmid[1] = gmid[0] + gin2[0, 0] + gin2[0, 1] + gin2[0, 2]
    for i, p in enumerate(ring_y):
        step = remote(gmid.at[1], gin2.at[1, i], gbs.at[1, i], gbr.at[1, i], p)
        step.start()
        more.append(step)
    for step in more[3:]:
        step.wait_recv()
    go_ref[...] = gmid[1] + gin2[1, 0] + gin2[1, 1] + gin2[1, 2]
    la.wait()
    lb.wait()
    for step in first:
        step.wait_recv()
    second = []
    for i in (1, 0, 2, 3):
        za = turn(z, i + 1)
        yb = turn(y, i + 1)
        for half, at in ((0, za), (1, yb)):
            def add(k, carry, half=half, at=at, i=i):
                t = own1[half, at, k].astype(F32) + in1[half, 0, at, k].astype(F32)
                t = t + in1[half, 1, at, k].astype(F32)
                mid[half, i, k] = (t + in1[half, 2, at, k].astype(F32)).astype(BF)
                return carry

            lax.fori_loop(0, 4, add, 0)
        if i < 3:
            a = remote(mid.at[0, i], in2.at[0, i], s2.at[0, i], r2.at[0, i], ring_z[i])
            b = remote(mid.at[1, i], in2.at[1, i], s2.at[1, i], r2.at[1, i], ring_y[i])
            a.start()
            b.start()
            second.extend([a, b])
    for step in second:
        step.wait_recv()
    for half in range(2):
        def add(k, carry, half=half):
            t = mid[half, 3, k].astype(F32) + in2[half, 0, k].astype(F32)
            t = t + in2[half, 1, k].astype(F32)
            fin[half * 4 + k] = (t + in2[half, 2, k].astype(F32)).astype(BF)
            return carry

        lax.fori_loop(0, 4, add, 0)
    spread = []
    for i, f in enumerate(friends):
        step = remote(fin.at[member(*f)], o_ref.at[me], gs.at[i], gr.at[i], place(y, z, *f))
        step.start()
        spread.append(step)
    last = pltpu.make_async_copy(fin.at[me], o_ref.at[me], own_sem.at[2])
    last.start()
    last.wait()
    for step in spread:
        step.wait()
    for step in first + second + gains + more:
        step.wait_send()


def sum_slices(slices, gains, cid):
    return pl.pallas_call(
        grads_body,
        out_shape=(
            jax.ShapeDtypeStruct((GROUP, SLICE, D), BF),
            jax.ShapeDtypeStruct(gains.shape, F32),
        ),
        in_specs=[ANY, INV],
        out_specs=(INV, INV),
        scratch_shapes=[
            pltpu.VMEM((2, 4, 4, SLICE, D), BF),
            pltpu.VMEM((2, 3, 4, 4, SLICE, D), BF),
            pltpu.VMEM((2, 4, 4, SLICE, D), BF),
            pltpu.VMEM((2, 3, 4, SLICE, D), BF),
            pltpu.VMEM((8, SLICE, D), BF),
            pltpu.VMEM((7,) + gains.shape, F32),
            pltpu.VMEM((2,) + gains.shape, F32),
            pltpu.VMEM((2, 3) + gains.shape, F32),
            DMA((3,)),
            DMA((2, 3)),
            DMA((2, 3)),
            DMA((2, 3)),
            DMA((2, 3)),
            DMA((7,)),
            DMA((7,)),
            DMA((7,)),
            DMA((7,)),
            DMA((2, 3)),
            DMA((2, 3)),
        ],
        compiler_params=params(cid),
    )(slices, gains)


def seq_place(s):
    return (s // 16, lax.rem(s // 4, 4), lax.rem(s // 2, 2), lax.rem(s, 2), lax.axis_index("xl"))


def seq_index():
    y, z, xh, c, xl = [lax.axis_index(a) for a in AXES]
    return ((y * 4 + z) * 2 + xh) * 2 + c


def ahead_body(x_ref, o_ref, own_sem, ss, rs):
    s = seq_index()
    sem = pltpu.get_barrier_semaphore()
    for d in range(1, 5):
        pl.semaphore_signal(sem, inc=1, device_id=seq_place(lax.rem(s + 64 - d, 64)), device_id_type=MESH)
    pl.semaphore_wait(sem, 4)
    steps = []
    for d in (4, 3, 2, 1):
        step = remote(x_ref, o_ref.at[4 - d], ss.at[d - 1], rs.at[d - 1], seq_place(lax.rem(s + d, 64)))
        step.start()
        steps.append(step)
    own = pltpu.make_async_copy(x_ref, o_ref.at[4], own_sem)
    own.start()
    own.wait()
    for step in steps:
        step.wait()


def send_ahead(kv, cid):
    return pl.pallas_call(
        ahead_body,
        out_shape=jax.ShapeDtypeStruct((5,) + kv.shape, kv.dtype),
        in_specs=[ANY],
        out_specs=ANY,
        scratch_shapes=[DMA, DMA((4,)), DMA((4,))],
        compiler_params=params(cid),
    )(kv)


def back_body(x_ref, o_ref, ss, rs):
    s = seq_index()
    sem = pltpu.get_barrier_semaphore()
    for d in range(1, 5):
        pl.semaphore_signal(sem, inc=1, device_id=seq_place(lax.rem(s + d, 64)), device_id_type=MESH)
    pl.semaphore_wait(sem, 4)
    steps = []
    for d in (4, 3, 2, 1):
        step = remote(x_ref.at[4 - d], o_ref.at[d - 1], ss.at[d - 1], rs.at[d - 1], seq_place(lax.rem(s + 64 - d, 64)))
        step.start()
        steps.append(step)
    for step in steps:
        step.wait()


def send_back(pieces, cid):
    return pl.pallas_call(
        back_body,
        out_shape=jax.ShapeDtypeStruct((4,) + pieces.shape[1:], pieces.dtype),
        in_specs=[ANY],
        out_specs=ANY,
        scratch_shapes=[DMA((4,)), DMA((4,))],
        compiler_params=params(cid),
    )(pieces)


def rms_norm(values, gain):
    return values * lax.rsqrt(jnp.mean(values * values, axis=-1, keepdims=True) + NORM_EPS) * gain


def rotary(values, positions):
    half = values.shape[-1] // 2
    freq = jnp.exp(-jnp.log(THETA) * jnp.arange(half, dtype=F32) * 2.0 / values.shape[-1])
    angle = positions.astype(F32)[:, None] * freq[None, :]
    shape = (values.shape[0],) + (1,) * (values.ndim - 2) + (half,)
    cosine = jnp.cos(angle).reshape(shape)
    sine = jnp.sin(angle).reshape(shape)
    first = values[..., :half]
    second = values[..., half:]
    return jnp.concatenate(
        [first * cosine - second * sine, second * cosine + first * sine], axis=-1
    )


def gate_product(gate_pre, up_pre):
    return jax.nn.gelu(gate_pre, approximate=True) * up_pre


def doc_lookup(table, positions):
    block_index = jnp.clip(positions // BLK, 0, table.shape[0] - 1)
    match = jnp.arange(table.shape[0], dtype=jnp.int32)[None, :] == block_index[:, None]
    return jnp.sum(jnp.where(match, table[None, :], 0), axis=1)


def dot(a, b, da, db):
    return lax.dot_general(a, b, (((da,), (db,)), ((), ())), preferred_element_type=F32)


def local(
    inputs,
    out_grad,
    doc_ids,
    owners,
    masters,
    first_old,
    second_old,
    left_basis,
    right_basis,
    gains,
    gain_first,
    gain_second,
):
    g_apre = gains[0:D]
    g_apost = gains[D : 2 * D]
    g_fpre = gains[2 * D : 3 * D]
    g_fpost = gains[3 * D : 4 * D]
    g_query = gains[4 * D : 4 * D + HD]
    g_key = gains[4 * D + HD :]
    my_seq = seq_index()
    my_slot = my_seq * 2 + lax.axis_index("xl")

    tile = masters[0].T.astype(BF).reshape(GROUP, SLICE, D)
    slots = gather_slices(tile, 1).reshape(128, SLICE, D)
    w_att = gather_group(jnp.take(slots, owners[:ATT], axis=0), 2).reshape(ATT, HD, D)
    w_ffn = jnp.take(slots, owners[ATT:], axis=0).reshape(3, FFT * SLICE, D)
    w_gate, w_up, w_down = w_ffn[0], w_ffn[1], w_ffn[2]
    w_qkv = w_att[: HEADS + 2].reshape((HEADS + 2) * HD, D)
    w_out = w_att[HEADS + 2 :].reshape(HEADS * HD, D)

    activ = inputs[0].astype(F32)
    local_pos = my_seq * TOK + jnp.arange(TOK, dtype=jnp.int32)
    normed_in = rms_norm(activ, g_apre).astype(BF)
    raw = dot(normed_in, w_qkv, 1, 1)
    queries_raw = raw[:, : HEADS * HD].reshape(TOK, HEADS, HD)
    keys_raw = raw[:, HEADS * HD : HEADS * HD + HD]
    values_raw = raw[:, HEADS * HD + HD :]

    def query_path(values, gain):
        return rotary(rms_norm(values, gain), local_pos)

    queries_low = query_path(queries_raw, g_query).astype(BF)
    keys_low = query_path(keys_raw, g_key).astype(BF)
    values_low = values_raw.astype(BF)
    pairs = send_ahead(jnp.stack([keys_low, values_low]), 3)
    all_keys = pairs[:, 0].reshape(WINDOW + TOK, HD)
    all_values = pairs[:, 1].reshape(WINDOW + TOK, HD)
    key_pos = my_seq * TOK - WINDOW + jnp.arange(WINDOW + TOK, dtype=jnp.int32)
    doc_table = doc_ids[0]
    query_docs = doc_lookup(doc_table, local_pos)
    key_docs = doc_lookup(doc_table, key_pos)
    visible = (key_docs[None, :] == query_docs[:, None]) & (key_pos[None, :] <= local_pos[:, None])
    visible = visible & (local_pos[:, None] - key_pos[None, :] < WINDOW) & (key_pos[None, :] >= 0)
    score_scale = HD ** (-0.5)
    scores = (
        jnp.einsum("thc,kc->thk", queries_low, all_keys, preferred_element_type=F32) * score_scale
    )
    scores = jnp.where(visible[:, None, :], scores, -1e30)
    row_top = jnp.max(scores, axis=-1, keepdims=True)
    expo = jnp.exp(scores - row_top)
    probs = expo / jnp.sum(expo, axis=-1, keepdims=True)
    probs_low = probs.astype(BF)
    attended = jnp.einsum("thk,kc->thc", probs_low, all_values, preferred_element_type=F32)
    attended = attended.astype(BF).reshape(TOK, HEADS * HD)
    projected = dot(attended, w_out, 1, 0)
    residual_one = activ + rms_norm(projected, g_apost)
    normed_ffn = rms_norm(residual_one, g_fpre).astype(BF)

    xf = gather_group(normed_ffn[None], 4).reshape(GROUP * TOK, D)
    gate_pre = dot(xf, w_gate, 1, 1)
    up_pre = dot(xf, w_up, 1, 1)
    hidden = gate_product(gate_pre, up_pre).astype(BF)
    down_part = dot(hidden, w_down, 1, 0).astype(BF)
    down = sum_group(down_part.reshape(1, GROUP, TOK, D), 5)[0]
    result = residual_one + rms_norm(down, g_fpost)
    layer_out = result.astype(BF)[None]
    cotangent = out_grad[0].astype(F32)
    unused, pull = jax.vjp(rms_norm, down, g_fpost)
    d_down, d_gfpost = pull(cotangent)
    d_down_all = gather_group(d_down.astype(BF)[None], 6).reshape(GROUP * TOK, D)
    d_hidden = dot(d_down_all, w_down, 1, 1)
    unused, pull = jax.vjp(gate_product, gate_pre, up_pre)
    d_gate, d_up = pull(d_hidden)
    d_gate_low = d_gate.astype(BF)
    d_up_low = d_up.astype(BF)
    d_xf_part = (dot(d_gate_low, w_gate, 1, 0) + dot(d_up_low, w_up, 1, 0)).astype(BF)
    d_normed_ffn = sum_group(d_xf_part.reshape(1, GROUP, TOK, D), 7)[0]
    t_gate = dot(d_gate_low, xf, 0, 0).astype(BF)
    t_up = dot(d_up_low, xf, 0, 0).astype(BF)
    t_down = dot(hidden, d_down_all, 0, 0).astype(BF)

    unused, pull = jax.vjp(rms_norm, residual_one, g_fpre)
    d_res_part, d_gfpre = pull(d_normed_ffn)
    d_residual = cotangent + d_res_part
    unused, pull = jax.vjp(rms_norm, projected, g_apost)
    d_projected, d_gapost = pull(d_residual)
    d_proj_low = d_projected.astype(BF)
    d_mixed = dot(d_proj_low, w_out, 1, 1).astype(BF)
    d_mixed_heads = d_mixed.reshape(TOK, HEADS, HD)
    d_probs = jnp.einsum("thc,kc->thk", d_mixed_heads, all_values, preferred_element_type=F32)
    inner_sum = jnp.sum(probs * d_probs, axis=-1, keepdims=True)
    d_scores = (probs * (d_probs - inner_sum) * score_scale).astype(BF)
    d_queries = jnp.einsum("thk,kc->thc", d_scores, all_keys, preferred_element_type=F32)
    d_keys_all = jnp.einsum("thk,thc->kc", d_scores, queries_low, preferred_element_type=F32)
    d_values_all = jnp.einsum("thk,thc->kc", probs_low, d_mixed_heads, preferred_element_type=F32)
    d_pairs = jnp.stack([d_keys_all.reshape(5, TOK, HD), d_values_all.reshape(5, TOK, HD)], axis=1)
    others = send_back(d_pairs[:4].astype(BF), 8)
    d_local = d_pairs[4] + jnp.sum(others.astype(F32), axis=0)
    unused, pull = jax.vjp(query_path, keys_raw, g_key)
    d_keys_raw, d_gkey = pull(d_local[0])
    unused, pull = jax.vjp(query_path, queries_raw, g_query)
    d_queries_raw, d_gquery = pull(d_queries)
    d_qkv = jnp.concatenate(
        [d_queries_raw.reshape(TOK, HEADS * HD), d_keys_raw, d_local[1]], axis=1
    ).astype(BF)
    d_normed_in = dot(d_qkv, w_qkv, 1, 0)
    unused, pull = jax.vjp(rms_norm, activ, g_apre)
    d_in_part, d_gapre = pull(d_normed_in)
    input_grad = (d_residual + d_in_part)[None]

    t_att = jnp.concatenate(
        [dot(d_qkv, normed_in, 0, 0).astype(BF), dot(attended, d_proj_low, 0, 0).astype(BF)]
    )
    t_att = sum_group(t_att.reshape(ATT, GROUP, SLICE, D), 9).astype(BF)
    by_tile = jnp.concatenate(
        [
            t_att,
            t_gate.reshape(FFT, SLICE, D),
            t_up.reshape(FFT, SLICE, D),
            t_down.reshape(FFT, SLICE, D),
        ]
    )
    match = owners[None, :] == jnp.arange(128, dtype=jnp.int32)[:, None]
    tile_of = jnp.sum(jnp.where(match, jnp.arange(owners.shape[0], dtype=jnp.int32)[None, :], 0), axis=1)
    by_slot = jnp.take(by_tile, tile_of, axis=0).reshape(4, 4, 2, 4, SLICE, D)
    gain_local = jnp.concatenate([d_gapre, d_gapost, d_gfpre, d_gfpost, d_gquery, d_gkey])
    grad, gain_grads = sum_slices(by_slot, gain_local.reshape(40, 128), 10)
    grad = grad.reshape(HD, D)
    gain_grads = gain_grads.reshape(-1)

    owned = jnp.any(owners == my_slot)
    left = left_basis[0].astype(BF)
    right = right_basis[0].astype(BF)
    rotated = dot(left, grad, 0, 1)
    rotated = dot(rotated.astype(BF), right, 1, 0)
    first_new = BETA_ONE * first_old[0] + (1.0 - BETA_ONE) * rotated
    second_new = BETA_TWO * second_old[0] + (1.0 - BETA_TWO) * rotated * rotated
    normed_step = (
        first_new
        / (1.0 - BETA_ONE**STEP)
        / (jnp.sqrt(second_new / (1.0 - BETA_TWO**STEP)) + ADAM_EPS)
    )
    back = dot(normed_step.astype(BF), right, 1, 1)
    back = dot(left, back.astype(BF), 1, 0)
    weight_new = masters[0] - RATE * (back + DECAY * masters[0])
    new_masters = jnp.where(owned, weight_new, masters[0])[None]
    new_first = jnp.where(owned, first_new, first_old[0])[None]
    new_second = jnp.where(owned, second_new, second_old[0])[None]
    new_gain_first = BETA_ONE * gain_first + (1.0 - BETA_ONE) * gain_grads
    new_gain_second = BETA_TWO * gain_second + (1.0 - BETA_TWO) * gain_grads * gain_grads
    gain_step = (
        new_gain_first
        / (1.0 - BETA_ONE**STEP)
        / (jnp.sqrt(new_gain_second / (1.0 - BETA_TWO**STEP)) + ADAM_EPS)
    )
    new_gains = gains - GAIN_RATE * gain_step
    return (
        layer_out,
        input_grad,
        new_masters,
        new_first,
        new_second,
        new_gains,
        new_gain_first,
        new_gain_second,
    )


def solution(mesh):
    wide = Mesh(mesh.devices.reshape(4, 4, 2, 2, 2), AXES)
    tokens = P("xl", ("y", "z", "xh", "core"), None)
    held = P(AXES, None, None)
    return jax.shard_map(
        local,
        mesh=wide,
        in_specs=(tokens, tokens, P("xl", None), P(), held, held, held, held, held, P(), P(), P()),
        out_specs=(tokens, tokens, held, held, held, P(), P(), P()),
        check_vma=False,
    )
```

```python
import functools

import jax
import jax.numpy as jnp
from jax import lax
from jax.experimental import pallas as pl
from jax.experimental.pallas import tpu as pltpu
from jax.sharding import Mesh
from jax.sharding import PartitionSpec as P

FF = 6912
HEADS = 4
WINDOW = 512
BLK = 64
STEP = 10
D = 1152
HD = 256
TOK = 128
GROUP = 8
SLICE = HD // GROUP
ATT = 2 * HEADS + 2
FFT = FF // HD

NORM_EPS = 1e-06
THETA = 10000.0
BETA_ONE = 0.5
BETA_TWO = 0.5
RATE = 0.02
GAIN_RATE = 0.4
DECAY = 0.01
ADAM_EPS = 1e-08

MESH = pl.DeviceIdType.MESH
AXES = ("y", "z", "xh", "core", "xl")
VMEM_LIMIT = 63 * 1024 * 1024
BF = jnp.bfloat16
F32 = jnp.float32


def here():
    y, z, xh, c, xl = [lax.axis_index(a) for a in AXES]
    return y, z, xh * 2 + xl, c


def place(y, z, x, c):
    return (y, z, x // 2, c, lax.rem(x, 2))


def member(x, c):
    return (x // 2) * 4 + c * 2 + lax.rem(x, 2)


def of_member(q):
    return (q // 4) * 2 + q % 2, (q // 2) % 2


def turn(a, d):
    return lax.rem(a + d, 4)


def greet(places):
    sem = pltpu.get_barrier_semaphore()
    for p in places:
        pl.semaphore_signal(sem, inc=1, device_id=p, device_id_type=MESH)
    pl.semaphore_wait(sem, len(places))


def remote(src, dst, send, recv, where):
    return pltpu.make_async_remote_copy(src, dst, send, recv, device_id=where, device_id_type=MESH)


def params(cid):
    return pltpu.CompilerParams(
        collective_id=cid, has_side_effects=True, vmem_limit_bytes=VMEM_LIMIT
    )


ANY = pl.BlockSpec(memory_space=pl.ANY)
INV = pl.BlockSpec(memory_space=pltpu.VMEM)
DMA = pltpu.SemaphoreType.DMA


def gather_body(x_ref, o_ref, own_sem, xs, xr, cs, cr):
    y, z, x, c = here()
    peers = [place(y, z, turn(x, d), c) for d in (1, 2, 3)]
    twin = place(y, z, x, 1 - c)
    greet(peers + [twin])
    mine = o_ref.at[:, member(x, c)]
    own = pltpu.make_async_copy(x_ref, mine, own_sem)
    far = [remote(x_ref, mine, xs.at[i], xr.at[i], p) for i, p in enumerate(peers)]
    for i in (1, 0, 2):
        far[i].start()
    near = [remote(x_ref, mine, cs.at[3], cr.at[3], twin)]
    near[0].start()
    own.start()
    for i in (0, 2, 1):
        far[i].wait_recv()
        src = o_ref.at[:, member(turn(x, 3 - i), c)]
        step = remote(src, src, cs.at[i], cr.at[i], twin)
        step.start()
        near.append(step)
    own.wait()
    for step in near:
        step.wait()
    for step in far:
        step.wait_send()


def gather_group(x, cid):
    n, r, w = x.shape
    return pl.pallas_call(
        gather_body,
        out_shape=jax.ShapeDtypeStruct((n, GROUP, r, w), x.dtype),
        in_specs=[ANY],
        out_specs=ANY,
        scratch_shapes=[DMA, DMA((3,)), DMA((3,)), DMA((4,)), DMA((4,))],
        compiler_params=params(cid),
    )(x)


def sum_body(x_ref, o_ref, own, near, part, far, own_sem, cs, cr, xs, xr):
    y, z, x, c = here()
    peers = [place(y, z, turn(x, d), c) for d in (1, 2, 3)]
    twin = place(y, z, x, 1 - c)
    greet(peers + [twin])
    n = x_ref.shape[0]
    swap, load = [], []
    for k, d in enumerate((2, 1, 3, 0)):
        xd = turn(x, d)
        swap.append(remote(x_ref.at[:, xd // 2, 1 - c, lax.rem(xd, 2)], near.at[k], cs.at[k], cr.at[k], twin))
        load.append(pltpu.make_async_copy(x_ref.at[:, xd // 2, c, lax.rem(xd, 2)], own.at[k], own_sem.at[k]))
        swap[-1].start()
        load[-1].start()
    sends = []
    for k, d in enumerate((2, 1, 3, 0)):
        load[k].wait()
        swap[k].wait_recv()

        def add(i, carry, k=k):
            part[k, i] = (own[k, i].astype(F32) + near[k, i].astype(F32)).astype(BF)
            return carry

        if d:
            lax.fori_loop(0, n, add, 0)
            step = remote(part.at[k], far.at[k], xs.at[k], xr.at[k], peers[d - 1])
            step.start()
            sends.append(step)
    for step in sends:
        step.wait_recv()

    def total(i, carry):
        first = own[3, i].astype(F32) + near[3, i].astype(F32)
        o_ref[i] = ((first + far[0, i].astype(F32)) + far[1, i].astype(F32)) + far[2, i].astype(F32)
        return carry

    lax.fori_loop(0, n, total, 0)
    for step in swap + sends:
        step.wait_send()


def sum_group(x, cid):
    n, _, r, w = x.shape
    blk = (n, r, w)
    return pl.pallas_call(
        sum_body,
        out_shape=jax.ShapeDtypeStruct(blk, F32),
        in_specs=[ANY],
        out_specs=INV,
        scratch_shapes=[
            pltpu.VMEM((4,) + blk, BF),
            pltpu.VMEM((4,) + blk, BF),
            pltpu.VMEM((3,) + blk, BF),
            pltpu.VMEM((3,) + blk, BF),
            DMA((4,)),
            DMA((4,)),
            DMA((4,)),
            DMA((3,)),
            DMA((3,)),
        ],
        compiler_params=params(cid),
    )(x.reshape(n, 2, 2, 2, r, w))


def weights_body(t_ref, o_ref, own_sem, gs, gr, s1, r1, s2, r2):
    y, z, x, c = here()
    me = member(x, c)
    friends = []
    for dx in range(4):
        for dc in range(2):
            if dx or dc:
                friends.append((turn(x, dx), lax.rem(c + dc, 2)))
    ring_z = [place(y, turn(z, d), x, c) for d in (1, 2, 3)]
    ring_y = [place(turn(y, d), z, x, c) for d in (1, 2, 3)]
    greet([place(y, z, *f) for f in friends] + ring_z + ring_y)
    mine = o_ref.at[y, z, me // 4, lax.rem(me, 4)]
    spread = []
    for i, f in enumerate(friends):
        step = remote(t_ref.at[f[0] * 2 + f[1]], mine, gs.at[i], gr.at[i], place(y, z, *f))
        step.start()
        spread.append(step)
    own = pltpu.make_async_copy(t_ref.at[x * 2 + c], mine, own_sem)
    own.start()
    own.wait()
    for step in spread:
        step.wait_recv()
    first = []
    for i in (1, 0, 2):
        a = remote(o_ref.at[y, z, 0], o_ref.at[y, z, 0], s1.at[0, i], r1.at[0, i], ring_z[i])
        b = remote(o_ref.at[y, z, 1], o_ref.at[y, z, 1], s1.at[1, i], r1.at[1, i], ring_y[i])
        a.start()
        b.start()
        first.append((i, a, b))
    second = []

    def onward(j, yy, zz):
        for i in (1, 0, 2):
            ra = o_ref.at[y, zz, 0]
            rb = o_ref.at[yy, z, 1]
            a = remote(ra, ra, s2.at[0, j, i], r2.at[0, j, i], ring_y[i])
            b = remote(rb, rb, s2.at[1, j, i], r2.at[1, j, i], ring_z[i])
            a.start()
            b.start()
            second.extend([a, b])

    onward(3, y, z)
    order = sorted(first, key=lambda f: (f[0] == 1, f[0]))
    for i, a, b in order:
        a.wait_recv()
        b.wait_recv()
        onward(i, turn(y, 3 - i), turn(z, 3 - i))
    for step in second:
        step.wait()
    for i, a, b in first:
        a.wait_send()
        b.wait_send()
    for step in spread:
        step.wait_send()


def gather_slices(tile, cid):
    return pl.pallas_call(
        weights_body,
        out_shape=jax.ShapeDtypeStruct((4, 4, 2, 4, SLICE, D), BF),
        in_specs=[ANY],
        out_specs=ANY,
        scratch_shapes=[
            DMA,
            DMA((7,)),
            DMA((7,)),
            DMA((2, 3)),
            DMA((2, 3)),
            DMA((2, 4, 3)),
            DMA((2, 4, 3)),
        ],
        compiler_params=params(cid),
    )(tile)


def grads_body(
    d_ref, g_ref, o_ref, go_ref,
    own1, in1, mid, in2, fin, gin, gmid, gin2,
    own_sem, s1, r1, s2, r2, gs, gr, gas, gar, gbs, gbr,
):
    y, z, x, c = here()
    me = member(x, c)
    friends = []
    for dx in range(4):
        for dc in range(2):
            if dx or dc:
                friends.append((turn(x, dx), lax.rem(c + dc, 2)))
    ring_z = [place(y, turn(z, d), x, c) for d in (1, 2, 3)]
    ring_y = [place(turn(y, d), z, x, c) for d in (1, 2, 3)]
    group = [place(y, z, *f) for f in friends]
    greet(group + ring_z + ring_y)
    first = []
    for i in (1, 0, 2):
        a = remote(d_ref.at[turn(y, i + 1), :, 0], in1.at[0, i], s1.at[0, i], r1.at[0, i], ring_y[i])
        b = remote(d_ref.at[:, turn(z, i + 1), 1], in1.at[1, i], s1.at[1, i], r1.at[1, i], ring_z[i])
        a.start()
        b.start()
        first.extend([a, b])
    la = pltpu.make_async_copy(d_ref.at[y, :, 0], own1.at[0], own_sem.at[0])
    lb = pltpu.make_async_copy(d_ref.at[:, z, 1], own1.at[1], own_sem.at[1])
    la.start()
    lb.start()
    gains = []
    for i, p in enumerate(group):
        step = remote(g_ref, gin.at[i], gas.at[i], gar.at[i], p)
        step.start()
        gains.append(step)
    for step in gains:
        step.wait_recv()
    acc = g_ref[...]
    for i in range(7):
        acc = acc + gin[i]
    gmid[0] = acc
    more = []
    for i, p in enumerate(ring_z):
        step = remote(gmid.at[0], gin2.at[0, i], gbs.at[0, i], gbr.at[0, i], p)
        step.start()
        more.append(step)
    for step in more:
        step.wait_recv()
    gmid[1] = gmid[0] + gin2[0, 0] + gin2[0, 1] + gin2[0, 2]
    for i, p in enumerate(ring_y):
        step = remote(gmid.at[1], gin2.at[1, i], gbs.at[1, i], gbr.at[1, i], p)
        step.start()
        more.append(step)
    for step in more[3:]:
        step.wait_recv()
    go_ref[...] = gmid[1] + gin2[1, 0] + gin2[1, 1] + gin2[1, 2]
    la.wait()
    lb.wait()
    for step in first:
        step.wait_recv()
    second = []
    for i in (1, 0, 2, 3):
        za = turn(z, i + 1)
        yb = turn(y, i + 1)
        for half, at in ((0, za), (1, yb)):
            def add(k, carry, half=half, at=at, i=i):
                t = own1[half, at, k].astype(F32) + in1[half, 0, at, k].astype(F32)
                t = t + in1[half, 1, at, k].astype(F32)
                mid[half, i, k] = (t + in1[half, 2, at, k].astype(F32)).astype(BF)
                return carry

            lax.fori_loop(0, 4, add, 0)
        if i < 3:
            a = remote(mid.at[0, i], in2.at[0, i], s2.at[0, i], r2.at[0, i], ring_z[i])
            b = remote(mid.at[1, i], in2.at[1, i], s2.at[1, i], r2.at[1, i], ring_y[i])
            a.start()
            b.start()
            second.extend([a, b])
    for step in second:
        step.wait_recv()
    for half in range(2):
        def add(k, carry, half=half):
            t = mid[half, 3, k].astype(F32) + in2[half, 0, k].astype(F32)
            t = t + in2[half, 1, k].astype(F32)
            fin[half * 4 + k] = (t + in2[half, 2, k].astype(F32)).astype(BF)
            return carry

        lax.fori_loop(0, 4, add, 0)
    spread = []
    for i, f in enumerate(friends):
        step = remote(fin.at[member(*f)], o_ref.at[x * 2 + c], gs.at[i], gr.at[i], place(y, z, *f))
        step.start()
        spread.append(step)
    last = pltpu.make_async_copy(fin.at[me], o_ref.at[x * 2 + c], own_sem.at[2])
    last.start()
    last.wait()
    for step in spread:
        step.wait()
    for step in first + second + gains + more:
        step.wait_send()


def sum_slices(slices, gains, cid):
    return pl.pallas_call(
        grads_body,
        out_shape=(
            jax.ShapeDtypeStruct((GROUP, SLICE, D), BF),
            jax.ShapeDtypeStruct(gains.shape, F32),
        ),
        in_specs=[ANY, INV],
        out_specs=(INV, INV),
        scratch_shapes=[
            pltpu.VMEM((2, 4, 4, SLICE, D), BF),
            pltpu.VMEM((2, 3, 4, 4, SLICE, D), BF),
            pltpu.VMEM((2, 4, 4, SLICE, D), BF),
            pltpu.VMEM((2, 3, 4, SLICE, D), BF),
            pltpu.VMEM((8, SLICE, D), BF),
            pltpu.VMEM((7,) + gains.shape, F32),
            pltpu.VMEM((2,) + gains.shape, F32),
            pltpu.VMEM((2, 3) + gains.shape, F32),
            DMA((3,)),
            DMA((2, 3)),
            DMA((2, 3)),
            DMA((2, 3)),
            DMA((2, 3)),
            DMA((7,)),
            DMA((7,)),
            DMA((7,)),
            DMA((7,)),
            DMA((2, 3)),
            DMA((2, 3)),
        ],
        compiler_params=params(cid),
    )(slices, gains)


def seq_place(s):
    return (s // 16, lax.rem(s // 4, 4), lax.rem(s // 2, 2), lax.rem(s, 2), lax.axis_index("xl"))


def seq_index():
    y, z, xh, c, xl = [lax.axis_index(a) for a in AXES]
    return ((y * 4 + z) * 2 + xh) * 2 + c


def ahead_body(x_ref, o_ref, own_sem, ss, rs):
    s = seq_index()
    sem = pltpu.get_barrier_semaphore()
    for d in range(1, 5):
        pl.semaphore_signal(sem, inc=1, device_id=seq_place(lax.rem(s + 64 - d, 64)), device_id_type=MESH)
    pl.semaphore_wait(sem, 4)
    steps = []
    for d in (4, 3, 2, 1):
        step = remote(x_ref, o_ref.at[4 - d], ss.at[d - 1], rs.at[d - 1], seq_place(lax.rem(s + d, 64)))
        step.start()
        steps.append(step)
    own = pltpu.make_async_copy(x_ref, o_ref.at[4], own_sem)
    own.start()
    own.wait()
    for step in steps:
        step.wait()


def send_ahead(kv, cid):
    return pl.pallas_call(
        ahead_body,
        out_shape=jax.ShapeDtypeStruct((5,) + kv.shape, kv.dtype),
        in_specs=[ANY],
        out_specs=ANY,
        scratch_shapes=[DMA, DMA((4,)), DMA((4,))],
        compiler_params=params(cid),
    )(kv)


def back_body(x_ref, o_ref, ss, rs):
    s = seq_index()
    sem = pltpu.get_barrier_semaphore()
    for d in range(1, 5):
        pl.semaphore_signal(sem, inc=1, device_id=seq_place(lax.rem(s + d, 64)), device_id_type=MESH)
    pl.semaphore_wait(sem, 4)
    steps = []
    for d in (4, 3, 2, 1):
        step = remote(x_ref.at[4 - d], o_ref.at[d - 1], ss.at[d - 1], rs.at[d - 1], seq_place(lax.rem(s + 64 - d, 64)))
        step.start()
        steps.append(step)
    for step in steps:
        step.wait()


def send_back(pieces, cid):
    return pl.pallas_call(
        back_body,
        out_shape=jax.ShapeDtypeStruct((4,) + pieces.shape[1:], pieces.dtype),
        in_specs=[ANY],
        out_specs=ANY,
        scratch_shapes=[DMA((4,)), DMA((4,))],
        compiler_params=params(cid),
    )(pieces)


def norm_of(v, g):
    return v * lax.rsqrt(jnp.mean(v * v, axis=-1, keepdims=True) + NORM_EPS) * g


def norm_back(v, g, w):
    r = lax.rsqrt(jnp.mean(v * v, axis=-1, keepdims=True) + NORM_EPS)
    u = w * g
    dg = jnp.sum(w * (v * r), axis=0, keepdims=True)
    dv = r * u - v * (r * r * r * jnp.mean(u * v, axis=-1, keepdims=True))
    return dv, dg


def rope_norm(v, g, cos, sin):
    n = v * lax.rsqrt(jnp.mean(v * v, axis=0, keepdims=True) + NORM_EPS) * g
    a, b = n[: HD // 2], n[HD // 2 :]
    return jnp.concatenate([a * cos - b * sin, b * cos + a * sin], axis=0)


def gelu_parts(g):
    k, a = 0.7978845608028654, 0.044715
    sq = g * g
    th = jnp.tanh(k * g * (1.0 + a * sq))
    half = 0.5 * (1.0 + th)
    slope = half + 0.5 * g * (1.0 - th * th) * (k * (1.0 + 3.0 * a * sq))
    return g * half, slope


def nn(a, b):
    return jnp.dot(a, b, preferred_element_type=F32)


def nt(a, b):
    return lax.dot_general(a, b, (((1,), (1,)), ((), ())), preferred_element_type=F32)


ORDER = (0, 3, 1, 2)


def layer_body(
    doc_ref, own_ref, wall_ref, xa_ref, x_ref, y_ref, g4_ref, gqk_ref, cos_ref, sin_ref,
    lo_ref, dr1_ref, dap_ref, gg_ref, raw_ref, qt_ref, k_ref, vt_ref, pt_ref, wo_ref, osl_ref, tg_ref,
    wall, wg, wu, wd, xa, sq, xf, dd, gb, ub, hb, dgb, dub, pbuf, sbuf, near, far, ptl, oto, dgt,
    load_sem, as_, ar, wxs, wxr, wcs, wcr, hs, hr, os_, or_, fxs, fxr, fcs, fcr, bxs, bxr, bcs, bcr,
    ss, sr, rs_, rr, out_sem,
):
    y, z, x, c = here()
    me = x * 2 + c
    twin = place(y, z, x, 1 - c)
    s = seq_index()
    chips = {d: turn(x, d) for d in range(4)}
    peers = {d: place(y, z, chips[d], c) for d in (1, 2, 3)}
    others = [(d, cc) for d in (1, 2, 3) for cc in range(2)]
    greet(
        [place(y, z, chips[d], cc) for d, cc in others]
        + [twin]
        + [seq_place(lax.rem(s + 64 + d, 64)) for d in (-4, -3, -2, -1, 1, 2, 3, 4)]
    )
    load_w = pltpu.make_async_copy(wall_ref, wall, load_sem.at[0])
    load_x = pltpu.make_async_copy(xa_ref, xa, load_sem.at[1])
    load_w.start()
    load_x.start()
    load_w.wait()

    for h in range(HEADS):
        wo_ref[h, me] = wall[own_ref[HEADS + 2 + h]]
    w_far = {}
    w_near = {}
    mine = wo_ref.at[:, me]
    for d in (1, 3, 2):
        w_far[d] = remote(mine, mine, wxs.at[d - 1], wxr.at[d - 1], peers[d])
    w_near[0] = remote(mine, mine, wcs.at[0], wcr.at[0], twin)

    watt = [wall[own_ref[t]] for t in range(HEADS + 2)]
    watt = jnp.concatenate(watt, axis=0)
    load_x.wait()
    qkv = []
    for d in (2, 1, 3, 0):
        part = nt(watt, xa[chips[d]].reshape(2 * TOK, D)).astype(BF)
        for cc in range(2):
            sq[d, cc] = part[:, cc * TOK : (cc + 1) * TOK].reshape(HEADS + 2, SLICE, TOK)
        if d:
            for cc in range(2):
                step = remote(
                    sq.at[d, cc], raw_ref.at[:, me], as_.at[d, cc], ar.at[d, c], place(y, z, chips[d], cc)
                )
                step.start()
                qkv.append(step)
    step = remote(sq.at[0, 1 - c], raw_ref.at[:, me], as_.at[0, 0], ar.at[0, c], twin)
    step.start()
    qkv.append(step)
    raw_ref[:, me] = sq[0, c]
    for d in (1, 3, 2):
        w_far[d].start()
    w_near[0].start()

    def pack(t, carry):
        rows = pl.ds(pl.multiple_of(t * SLICE, SLICE), SLICE)
        wg[rows] = wall[own_ref[ATT + t]]
        wu[rows] = wall[own_ref[ATT + FFT + t]]
        wd[rows] = wall[own_ref[ATT + 2 * FFT + t]]
        return carry

    lax.fori_loop(0, FFT, pack, 0)
    for d in (1, 2, 3):
        for cc in range(2):
            remote(sq.at[d, cc], raw_ref.at[:, me], as_.at[d, cc], ar.at[d, cc], twin).wait_recv()
    remote(sq.at[0, 0], raw_ref.at[:, me], as_.at[0, 0], ar.at[0, 1 - c], twin).wait_recv()

    cos, sin = cos_ref[...], sin_ref[...]
    kt = rope_norm(
        raw_ref[HEADS].reshape(HD, TOK).astype(F32), gqk_ref[:, 1:2], cos, sin
    )
    k_ref[4] = kt.T.astype(BF)
    vt_ref[:, 4 * TOK :] = raw_ref[HEADS + 1].reshape(HD, TOK)
    halo = []
    for d in (4, 3, 2, 1):
        to = seq_place(lax.rem(s + d, 64))
        a = remote(k_ref.at[4], k_ref.at[4 - d], hs.at[0, d - 1], hr.at[0, d - 1], to)
        b = remote(
            vt_ref.at[:, 4 * TOK :], vt_ref.at[:, (4 - d) * TOK : (5 - d) * TOK], hs.at[1, d - 1], hr.at[1, d - 1], to
        )
        a.start()
        b.start()
        halo.extend([a, b])
    for h in range(HEADS):
        q = rope_norm(raw_ref[h].reshape(HD, TOK).astype(F32), gqk_ref[:, 0:1], cos, sin)
        qt_ref[:, h * TOK : (h + 1) * TOK] = q.astype(BF)
    row = lax.broadcasted_iota(jnp.int32, (WINDOW + TOK, TOK), 0)
    col = lax.broadcasted_iota(jnp.int32, (WINDOW + TOK, TOK), 1)
    seen = (row <= col + WINDOW) & (row > col) & (row >= WINDOW - s * TOK)
    half = lax.broadcasted_iota(jnp.int32, (BLK, TOK), 1) < BLK
    q_doc = jnp.where(half, doc_ref[0, 2 * s], doc_ref[0, 2 * s + 1])
    k_doc = jnp.concatenate(
        [
            jnp.full((BLK, TOK), doc_ref[0, jnp.maximum(2 * s - 8 + b, 0)], jnp.int32)
            for b in range(10)
        ],
        axis=0,
    )
    seen = seen & (k_doc == jnp.concatenate([q_doc] * 10, axis=0))
    for step in halo:
        step.wait_recv()
    keys = k_ref[...].reshape(WINDOW + TOK, HD)
    for h in range(HEADS):
        lanes = slice(h * TOK, (h + 1) * TOK)
        sc = nn(keys, qt_ref[:, lanes]) * (HD**-0.5)
        sc = jnp.where(seen, sc, -1e30)
        ex = jnp.exp(sc - jnp.max(sc, axis=0, keepdims=True))
        pr = ex / jnp.sum(ex, axis=0, keepdims=True)
        pt_ref[:, lanes] = pr
        ptl[:, lanes] = pr.astype(BF)
    ot = nn(vt_ref[...], ptl[...])
    oto[...] = ot.astype(BF)
    o_steps = []
    for d, cc in others:
        to = chips[d] * 2 + cc
        rows = pl.ds(pl.multiple_of(to * SLICE, SLICE), SLICE)
        step = remote(
            oto.at[rows], osl_ref.at[me], os_.at[d, cc], or_.at[d, c], place(y, z, chips[d], cc)
        )
        step.start()
        o_steps.append(step)
    rows = pl.ds(pl.multiple_of((x * 2 + 1 - c) * SLICE, SLICE), SLICE)
    step = remote(oto.at[rows], osl_ref.at[me], os_.at[0, 0], or_.at[0, c], twin)
    step.start()
    o_steps.append(step)
    osl_ref[me] = oto[pl.ds(pl.multiple_of(me * SLICE, SLICE), SLICE)]

    for d in (1, 3, 2):
        w_far[d].wait_recv()
        src = wo_ref.at[:, chips[4 - d] * 2 + c]
        w_near[d] = remote(src, src, wcs.at[d], wcr.at[d], twin)
        w_near[d].start()
    for step in w_near.values():
        step.wait()
    ap = jnp.zeros((TOK, D), F32)
    for h in range(HEADS):
        o = ot[:, h * TOK : (h + 1) * TOK].T.astype(BF)
        ap = ap + nn(o, wo_ref[h].reshape(HD, D))
    act = x_ref[...].astype(F32)
    r1 = act + norm_of(ap, g4_ref[1:2])
    xf[x, c] = norm_of(r1, g4_ref[2:3]).astype(BF)

    def gather_start(buf, xs, xr, cs, cr):
        own = buf.at[x, c]
        sends = {d: remote(own, own, xs.at[d - 1], xr.at[d - 1], peers[d]) for d in (1, 3, 2)}
        near_ = {0: remote(own, own, cs.at[0], cr.at[0], twin)}
        near_[0].start()
        for d in (1, 3, 2):
            sends[d].start()
        return sends, near_

    def gather_wait(buf, e, sends, near_, cs, cr):
        if e:
            d = 4 - e
            sends[d].wait_recv()
            src = buf.at[chips[e], c]
            near_[d] = remote(src, src, cs.at[d], cr.at[d], twin)
            near_[d].start()
            near_[d].wait_recv()
        else:
            near_[0].wait_recv()

    def gather_end(sends, near_):
        for step in list(sends.values()) + list(near_.values()):
            step.wait_send()

    def sum_swap(ph, e):
        step = remote(pbuf.at[e, 1 - c], near.at[ph, e], ss.at[ph, e], sr.at[ph, e], twin)
        step.start()
        return step

    def sum_send(ph, e, swap):
        swap.wait_recv()
        both = pbuf[e, c].astype(F32) + near[ph, e].astype(F32)
        if not e:
            return None, both
        sbuf[e - 1] = both.astype(BF)
        step = remote(sbuf.at[e - 1], far.at[ph, e - 1], rs_.at[ph, e - 1], rr.at[ph, e - 1], peers[e])
        step.start()
        return step, None

    def pipeline(ph, buf, xs, xr, cs, cr, block):
        sends, near_ = gather_start(buf, xs, xr, cs, cr)
        swaps, outs = {}, []
        for n, e in enumerate(ORDER):
            gather_wait(buf, e, sends, near_, cs, cr)
            pbuf[e] = block(e).astype(BF).reshape(2, TOK, D)
            swaps[e] = sum_swap(ph, e)
            if n >= 2:
                outs.append(sum_send(ph, ORDER[n - 1], swaps[ORDER[n - 1]])[0])
        outs.append(sum_send(ph, ORDER[3], swaps[ORDER[3]])[0])
        return sends, near_, swaps, outs

    def finish(ph, sends, near_, swaps, outs):
        _, total = sum_send(ph, 0, swaps[0])
        for step in outs:
            step.wait_recv()
        total = ((total + far[ph, 0].astype(F32)) + far[ph, 1].astype(F32)) + far[ph, 2].astype(F32)
        gather_end(sends, near_)
        for step in list(swaps.values()) + outs:
            step.wait_send()
        return total

    def forward(e):
        v = xf[chips[e]].reshape(2 * TOK, D)
        g = nt(v, wg[...])
        u = nt(v, wu[...])
        at = chips[e]
        gb[at] = g
        ub[at] = u
        h, _ = gelu_parts(g)
        hb[at] = (h * u).astype(BF)
        return nn(hb[at], wd[...])

    state = pipeline(0, xf, fxs, fxr, fcs, fcr, forward)
    dn = finish(0, *state)
    lo_ref[...] = (r1 + norm_of(dn, g4_ref[3:4])).astype(BF)
    cot = y_ref[...].astype(F32)
    ddn, d_fpost = norm_back(dn, g4_ref[3:4], cot)
    dd[x, c] = ddn.astype(BF)

    def backward(e):
        v = dd[chips[e]].reshape(2 * TOK, D)
        dh = nt(v, wd[...])
        at = chips[e]
        h, slope = gelu_parts(gb[at])
        dgb[at] = (dh * ub[at] * slope).astype(BF)
        dub[at] = (dh * h).astype(BF)
        return nn(dgb[at], wg[...]) + nn(dub[at], wu[...])

    state = pipeline(1, dd, bxs, bxr, bcs, bcr, backward)
    for i, (lhs, rhs) in enumerate(((dgb, xf), (dub, xf), (hb, dd))):
        for e in range(4):
            dgt[:, e * 2 * TOK : (e + 1) * 2 * TOK] = lhs[e].T
        for n in range(3):
            cols = slice(n * 384, (n + 1) * 384)
            g = nn(dgt[...], rhs[:, :, :, cols].reshape(GROUP * TOK, 384)).astype(BF)
            wall[i * FFT : (i + 1) * FFT, :, cols] = g.reshape(FFT, SLICE, 384)
    out = pltpu.make_async_copy(wall.at[0 : 3 * FFT], tg_ref, out_sem)
    out.start()
    dxf = finish(1, *state)
    e1, d_fpre = norm_back(r1, g4_ref[2:3], dxf)
    dr1 = cot + e1
    dr1_ref[...] = dr1
    dap, d_apost = norm_back(ap, g4_ref[1:2], dr1)
    dap_ref[...] = dap.astype(BF)
    gg_ref[0:1] = d_apost
    gg_ref[1:2] = d_fpre
    gg_ref[2:3] = d_fpost
    for d in (1, 2, 3):
        for cc in range(2):
            remote(oto.at[0:SLICE], osl_ref.at[me], os_.at[d, cc], or_.at[d, cc], twin).wait_recv()
    remote(oto.at[0:SLICE], osl_ref.at[me], os_.at[0, 0], or_.at[0, 1 - c], twin).wait_recv()
    for step in qkv + halo + o_steps + list(w_far.values()):
        step.wait_send()
    out.wait()


def run_layer(doc, owners, slots, xa, x, y, g4, gqk, cos, sin, cid):
    f = jax.ShapeDtypeStruct
    smem = pl.BlockSpec(memory_space=pltpu.SMEM)
    vm = pltpu.VMEM
    ffw = FFT * SLICE
    outs = [
        (f((TOK, D), BF), INV),
        (f((TOK, D), F32), INV),
        (f((TOK, D), BF), INV),
        (f((3, D), F32), INV),
        (f((HEADS + 2, GROUP, SLICE, TOK), BF), INV),
        (f((HD, HEADS * TOK), BF), INV),
        (f((5, TOK, HD), BF), INV),
        (f((HD, WINDOW + TOK), BF), INV),
        (f((WINDOW + TOK, HEADS * TOK), F32), INV),
        (f((HEADS, GROUP, SLICE, D), BF), INV),
        (f((GROUP, SLICE, HEADS * TOK), BF), INV),
        (f((3 * FFT, SLICE, D), BF), ANY),
    ]
    return pl.pallas_call(
        layer_body,
        out_shape=tuple(o[0] for o in outs),
        in_specs=[smem, smem, ANY, ANY, INV, INV, INV, INV, INV, INV],
        out_specs=tuple(o[1] for o in outs),
        scratch_shapes=[
            vm((128, SLICE, D), BF),
            vm((ffw, D), BF),
            vm((ffw, D), BF),
            vm((ffw, D), BF),
            vm((4, 2, TOK, D), BF),
            vm((4, 2, HEADS + 2, SLICE, TOK), BF),
            vm((4, 2, TOK, D), BF),
            vm((4, 2, TOK, D), BF),
            vm((4, 2 * TOK, ffw), F32),
            vm((4, 2 * TOK, ffw), F32),
            vm((4, 2 * TOK, ffw), BF),
            vm((4, 2 * TOK, ffw), BF),
            vm((4, 2 * TOK, ffw), BF),
            vm((4, 2, TOK, D), BF),
            vm((3, TOK, D), BF),
            vm((2, 4, TOK, D), BF),
            vm((2, 3, TOK, D), BF),
            vm((WINDOW + TOK, HEADS * TOK), BF),
            vm((HD, HEADS * TOK), BF),
            vm((ffw, GROUP * TOK), BF),
            DMA((2,)),
            DMA((4, 2)), DMA((4, 2)),
            DMA((3,)), DMA((3,)), DMA((4,)), DMA((4,)),
            DMA((2, 4)), DMA((2, 4)),
            DMA((4, 2)), DMA((4, 2)),
            DMA((3,)), DMA((3,)), DMA((4,)), DMA((4,)),
            DMA((3,)), DMA((3,)), DMA((4,)), DMA((4,)),
            DMA((2, 4)), DMA((2, 4)), DMA((2, 3)), DMA((2, 3)),
            DMA,
        ],
        compiler_params=params(cid),
    )(doc, owners, slots, xa, x, y, g4, gqk, cos, sin)


def rms_norm(values, gain):
    return values * lax.rsqrt(jnp.mean(values * values, axis=-1, keepdims=True) + NORM_EPS) * gain


def rotary(values, positions):
    half = values.shape[-1] // 2
    freq = jnp.exp(-jnp.log(THETA) * jnp.arange(half, dtype=F32) * 2.0 / values.shape[-1])
    angle = positions.astype(F32)[:, None] * freq[None, :]
    shape = (values.shape[0],) + (1,) * (values.ndim - 2) + (half,)
    cosine = jnp.cos(angle).reshape(shape)
    sine = jnp.sin(angle).reshape(shape)
    first = values[..., :half]
    second = values[..., half:]
    return jnp.concatenate(
        [first * cosine - second * sine, second * cosine + first * sine], axis=-1
    )


def gate_product(gate_pre, up_pre):
    return jax.nn.gelu(gate_pre, approximate=True) * up_pre


def doc_lookup(table, positions):
    block_index = jnp.clip(positions // BLK, 0, table.shape[0] - 1)
    match = jnp.arange(table.shape[0], dtype=jnp.int32)[None, :] == block_index[:, None]
    return jnp.sum(jnp.where(match, table[None, :], 0), axis=1)


def dot(a, b, da, db):
    return lax.dot_general(a, b, (((da,), (db,)), ((), ())), preferred_element_type=F32)


def local(
    inputs,
    out_grad,
    doc_ids,
    owners,
    masters,
    first_old,
    second_old,
    left_basis,
    right_basis,
    gains,
    gain_first,
    gain_second,
):
    g_apre = gains[0:D]
    g_apost = gains[D : 2 * D]
    g_fpre = gains[2 * D : 3 * D]
    g_fpost = gains[3 * D : 4 * D]
    g_query = gains[4 * D : 4 * D + HD]
    g_key = gains[4 * D + HD :]
    my_seq = seq_index()
    my_slot = my_seq * 2 + lax.axis_index("xl")

    tile = masters[0].T.astype(BF).reshape(GROUP, SLICE, D)
    slots = gather_slices(tile, 1).reshape(128, SLICE, D)
    activ = inputs[0].astype(F32)
    local_pos = my_seq * TOK + jnp.arange(TOK, dtype=jnp.int32)
    normed_in = rms_norm(activ, g_apre).astype(BF)
    xa_all = gather_group(normed_in[None], 2)[0]
    xa_all = xa_all.reshape(2, 2, 2, TOK, D).transpose(0, 2, 1, 3, 4).reshape(4, 2, TOK, D)
    freq = jnp.exp(-jnp.log(THETA) * jnp.arange(HD // 2, dtype=F32) * 2.0 / HD)
    angle = freq[:, None] * local_pos.astype(F32)[None, :]
    g4 = jnp.stack([g_apre, g_apost, g_fpre, g_fpost])
    gqk = jnp.stack([g_query, g_key], axis=1)
    (layer_out, d_residual, d_proj_low, gg, raw, qt, k_all, vt, pt, wo, osl, t_ffn) = run_layer(
        doc_ids, owners, slots, xa_all, inputs[0], out_grad[0], g4, gqk, jnp.cos(angle), jnp.sin(angle), 3
    )
    layer_out = layer_out[None]
    w_att = gather_group(jnp.take(slots, owners[:ATT], axis=0), 12)
    w_att = w_att.reshape(ATT, 2, 2, 2, SLICE, D).transpose(0, 1, 3, 2, 4, 5).reshape(ATT, HD, D)
    w_qkv = w_att[: HEADS + 2].reshape((HEADS + 2) * HD, D)
    w_out = wo.reshape(HEADS * HD, D)
    raw = raw.reshape(6, HD, TOK).astype(F32)
    queries_raw = raw[:HEADS].transpose(2, 0, 1)
    keys_raw = raw[HEADS].T
    queries_low = qt.reshape(HD, HEADS, TOK).transpose(2, 1, 0)
    all_keys = k_all.reshape(WINDOW + TOK, HD)
    all_values = vt.T
    probs = pt.reshape(WINDOW + TOK, HEADS, TOK).transpose(2, 1, 0)
    probs_low = probs.astype(BF)
    attended = jnp.einsum("thk,kc->thc", probs_low, all_values, preferred_element_type=F32)
    attended = attended.astype(BF).reshape(TOK, HEADS * HD)
    score_scale = HD ** (-0.5)

    def query_path(values, gain):
        return rotary(rms_norm(values, gain), local_pos)

    d_gapost, d_gfpre, d_gfpost = gg[0], gg[1], gg[2]
    d_mixed = dot(d_proj_low, w_out, 1, 1).astype(BF)
    d_mixed_heads = d_mixed.reshape(TOK, HEADS, HD)
    d_probs = jnp.einsum("thc,kc->thk", d_mixed_heads, all_values, preferred_element_type=F32)
    inner_sum = jnp.sum(probs * d_probs, axis=-1, keepdims=True)
    d_scores = (probs * (d_probs - inner_sum) * score_scale).astype(BF)
    d_queries = jnp.einsum("thk,kc->thc", d_scores, all_keys, preferred_element_type=F32)
    d_keys_all = jnp.einsum("thk,thc->kc", d_scores, queries_low, preferred_element_type=F32)
    d_values_all = jnp.einsum("thk,thc->kc", probs_low, d_mixed_heads, preferred_element_type=F32)
    d_pairs = jnp.stack([d_keys_all.reshape(5, TOK, HD), d_values_all.reshape(5, TOK, HD)], axis=1)
    others = send_back(d_pairs[:4].astype(BF), 8)
    d_local = d_pairs[4] + jnp.sum(others.astype(F32), axis=0)
    unused, pull = jax.vjp(query_path, keys_raw, g_key)
    d_keys_raw, d_gkey = pull(d_local[0])
    unused, pull = jax.vjp(query_path, queries_raw, g_query)
    d_queries_raw, d_gquery = pull(d_queries)
    d_qkv = jnp.concatenate(
        [d_queries_raw.reshape(TOK, HEADS * HD), d_keys_raw, d_local[1]], axis=1
    ).astype(BF)
    d_normed_in = dot(d_qkv, w_qkv, 1, 0)
    unused, pull = jax.vjp(rms_norm, activ, g_apre)
    d_in_part, d_gapre = pull(d_normed_in)
    input_grad = (d_residual + d_in_part)[None]

    t_att = jnp.concatenate(
        [dot(d_qkv, normed_in, 0, 0).astype(BF), dot(attended, d_proj_low, 0, 0).astype(BF)]
    )
    t_att = t_att.reshape(ATT, 2, 2, 2, SLICE, D).transpose(0, 1, 3, 2, 4, 5)
    t_att = sum_group(t_att.reshape(ATT, GROUP, SLICE, D), 9).astype(BF)
    by_tile = jnp.concatenate(
        [
            t_att,
            t_ffn,
        ]
    )
    match = owners[None, :] == jnp.arange(128, dtype=jnp.int32)[:, None]
    tile_of = jnp.sum(jnp.where(match, jnp.arange(owners.shape[0], dtype=jnp.int32)[None, :], 0), axis=1)
    by_slot = jnp.take(by_tile, tile_of, axis=0).reshape(4, 4, 2, 4, SLICE, D)
    gain_local = jnp.concatenate([d_gapre, d_gapost, d_gfpre, d_gfpost, d_gquery, d_gkey])
    grad, gain_grads = sum_slices(by_slot, gain_local.reshape(40, 128), 10)
    grad = grad.reshape(HD, D)
    gain_grads = gain_grads.reshape(-1)

    owned = jnp.any(owners == my_slot)
    left = left_basis[0].astype(BF)
    right = right_basis[0].astype(BF)
    rotated = dot(left, grad, 0, 1)
    rotated = dot(rotated.astype(BF), right, 1, 0)
    first_new = BETA_ONE * first_old[0] + (1.0 - BETA_ONE) * rotated
    second_new = BETA_TWO * second_old[0] + (1.0 - BETA_TWO) * rotated * rotated
    normed_step = (
        first_new
        / (1.0 - BETA_ONE**STEP)
        / (jnp.sqrt(second_new / (1.0 - BETA_TWO**STEP)) + ADAM_EPS)
    )
    back = dot(normed_step.astype(BF), right, 1, 1)
    back = dot(left, back.astype(BF), 1, 0)
    weight_new = masters[0] - RATE * (back + DECAY * masters[0])
    new_masters = jnp.where(owned, weight_new, masters[0])[None]
    new_first = jnp.where(owned, first_new, first_old[0])[None]
    new_second = jnp.where(owned, second_new, second_old[0])[None]
    new_gain_first = BETA_ONE * gain_first + (1.0 - BETA_ONE) * gain_grads
    new_gain_second = BETA_TWO * gain_second + (1.0 - BETA_TWO) * gain_grads * gain_grads
    gain_step = (
        new_gain_first
        / (1.0 - BETA_ONE**STEP)
        / (jnp.sqrt(new_gain_second / (1.0 - BETA_TWO**STEP)) + ADAM_EPS)
    )
    new_gains = gains - GAIN_RATE * gain_step
    return (
        layer_out,
        input_grad,
        new_masters,
        new_first,
        new_second,
        new_gains,
        new_gain_first,
        new_gain_second,
    )


def solution(mesh):
    wide = Mesh(mesh.devices.reshape(4, 4, 2, 2, 2), AXES)
    tokens = P("xl", ("y", "z", "xh", "core"), None)
    held = P(AXES, None, None)
    return jax.shard_map(
        local,
        mesh=wide,
        in_specs=(tokens, tokens, P("xl", None), P(), held, held, held, held, held, P(), P(), P()),
        out_specs=(tokens, tokens, held, held, held, P(), P(), P()),
        check_vma=False,
    )
```

```python
import functools

import jax
import jax.numpy as jnp
from jax import lax
from jax.experimental import pallas as pl
from jax.experimental.pallas import tpu as pltpu
from jax.sharding import Mesh
from jax.sharding import PartitionSpec as P

FF = 6912
HEADS = 4
WINDOW = 512
BLK = 64
STEP = 10
D = 1152
HD = 256
TOK = 128
GROUP = 8
SLICE = HD // GROUP
ATT = 2 * HEADS + 2
FFT = FF // HD

NORM_EPS = 1e-06
THETA = 10000.0
BETA_ONE = 0.5
BETA_TWO = 0.5
RATE = 0.02
GAIN_RATE = 0.4
DECAY = 0.01
ADAM_EPS = 1e-08

MESH = pl.DeviceIdType.MESH
AXES = ("y", "z", "xh", "core", "xl")
VMEM_LIMIT = 63 * 1024 * 1024
BF = jnp.bfloat16
F32 = jnp.float32


def here():
    y, z, xh, c, xl = [lax.axis_index(a) for a in AXES]
    return y, z, xh * 2 + xl, c


def place(y, z, x, c):
    return (y, z, x // 2, c, lax.rem(x, 2))


def member(x, c):
    return (x // 2) * 4 + c * 2 + lax.rem(x, 2)


def turn(a, d):
    return lax.rem(a + d, 4)


def greet(places):
    sem = pltpu.get_barrier_semaphore()
    for p in places:
        pl.semaphore_signal(sem, inc=1, device_id=p, device_id_type=MESH)
    pl.semaphore_wait(sem, len(places))


def remote(src, dst, send, recv, where):
    return pltpu.make_async_remote_copy(src, dst, send, recv, device_id=where, device_id_type=MESH)


def params(cid):
    return pltpu.CompilerParams(
        collective_id=cid, has_side_effects=True, vmem_limit_bytes=VMEM_LIMIT
    )


ANY = pl.BlockSpec(memory_space=pl.ANY)
INV = pl.BlockSpec(memory_space=pltpu.VMEM)
DMA = pltpu.SemaphoreType.DMA


def seq_place(s):
    return (s // 16, lax.rem(s // 4, 4), lax.rem(s // 2, 2), lax.rem(s, 2), lax.axis_index("xl"))


def seq_index():
    y, z, xh, c, xl = [lax.axis_index(a) for a in AXES]
    return ((y * 4 + z) * 2 + xh) * 2 + c


def norm_of(v, g):
    return v * lax.rsqrt(jnp.mean(v * v, axis=-1, keepdims=True) + NORM_EPS) * g


def norm_back(v, g, w):
    r = lax.rsqrt(jnp.mean(v * v, axis=-1, keepdims=True) + NORM_EPS)
    u = w * g
    dg = jnp.sum(w * (v * r), axis=0, keepdims=True)
    dv = r * u - v * (r * r * r * jnp.mean(u * v, axis=-1, keepdims=True))
    return dv, dg


def column(g_ref, i):
    row = g_ref[:, 4 * D + i * HD : 4 * D + (i + 1) * HD]
    return jnp.broadcast_to(row, (128, HD)).T[:, 0:1]


def rope_norm(v, g, cos, sin):
    n = v * lax.rsqrt(jnp.mean(v * v, axis=0, keepdims=True) + NORM_EPS) * g
    a, b = n[: HD // 2], n[HD // 2 :]
    return jnp.concatenate([a * cos - b * sin, b * cos + a * sin], axis=0)


def gelu_parts(g):
    k, a = 0.7978845608028654, 0.044715
    sq = g * g
    th = jnp.tanh(k * g * (1.0 + a * sq))
    half = 0.5 * (1.0 + th)
    slope = half + 0.5 * g * (1.0 - th * th) * (k * (1.0 + 3.0 * a * sq))
    return g * half, slope


def nn(a, b):
    return jnp.dot(a, b, preferred_element_type=F32)


def nt(a, b):
    return lax.dot_general(a, b, (((1,), (1,)), ((), ())), preferred_element_type=F32)


def start_body(
    own_ref, m_ref, x_ref, g_ref,
    o_ref, xa_ref, cos_ref, sin_ref, tile_ref,
    tile, own_sem, gs, gr, s1, r1, f1, q1, s2, r2, f2, q2, bxs, bxr, bcs, bcr,
):
    y, z, x, c = here()
    me = x * 2 + c
    mm = member(x, c)
    chips = {d: turn(x, d) for d in range(4)}
    peers = {d: place(y, z, chips[d], c) for d in (1, 2, 3)}
    twin = place(y, z, x, 1 - c)
    others = [(d, cc) for d in (1, 2, 3) for cc in range(2)]
    at = (z, y)
    ring = (
        {d: place(y, turn(z, d), x, c) for d in (1, 2, 3)},
        {d: place(turn(y, d), z, x, c) for d in (1, 2, 3)},
    )
    everyone = [place(y, z, chips[d], cc) for d, cc in others] + [twin]
    everyone = everyone + [ring[h][d] for h in (0, 1) for d in (1, 3)]
    sem = pltpu.get_barrier_semaphore()
    for p in everyone:
        pl.semaphore_signal(sem, inc=1, device_id=p, device_id_type=MESH)
    for h in range(2):
        tile[4 * h : 4 * h + 4] = m_ref[:, h * 128 : (h + 1) * 128].T.astype(BF).reshape(4, SLICE, D)
    pl.semaphore_wait(sem, len(everyone))

    sent = []

    def go(step):
        step.start()
        sent.append(step)
        return step

    mine = o_ref.at[y, z, mm // 4, lax.rem(mm, 4)]
    for d, cc in [(2, 0), (2, 1), (1, 0), (1, 1), (3, 0), (3, 1)]:
        go(remote(tile.at[chips[d] * 2 + cc], mine, gs.at[d, cc], gr.at[d, c], place(y, z, chips[d], cc)))
    go(remote(tile.at[x * 2 + 1 - c], mine, gs.at[0, 0], gr.at[0, c], twin))
    own = pltpu.make_async_copy(tile.at[me], mine, own_sem)
    own.start()
    xa_ref[x, c] = norm_of(x_ref[...].astype(F32), g_ref[:, 0:D]).astype(BF)
    mine_x = xa_ref.at[x, c]
    x_far = {d: remote(mine_x, mine_x, bxs.at[d - 1], bxr.at[d - 1], peers[d]) for d in (1, 3, 2)}
    for d in (1, 3, 2):
        go(x_far[d])
    x_near = [go(remote(mine_x, mine_x, bcs.at[0], bcr.at[0], twin))]
    own.wait()
    for d, cc in others:
        remote(tile.at[0], mine, gs.at[d, cc], gr.at[d, cc], twin).wait_recv()
    remote(tile.at[0], mine, gs.at[0, 0], gr.at[0, 1 - c], twin).wait_recv()

    def block(h, first, second):
        return o_ref.at[second, first, 0] if h == 0 else o_ref.at[first, second, 1]

    fc = {h: {d: turn(at[h], d) for d in range(4)} for h in (0, 1)}
    sc = {h: {d: turn(at[1 - h], d) for d in range(4)} for h in (0, 1)}
    ways = ((0, 1, 3), (1, 3, 1))
    one, two = {}, {}
    for h in (0, 1):
        b = block(h, fc[h][0], sc[h][0])
        for n, up, _ in ways:
            one[h, n] = go(remote(b, b, s1.at[h, n], r1.at[h, n], ring[h][up]))

    def second(k):
        for h in (0, 1):
            b = block(h, fc[h][k], sc[h][0])
            for n, up, _ in ways:
                two[h, k, n] = go(remote(b, b, s2.at[h, k, n], r2.at[h, k, n], ring[1 - h][up]))

    second(0)
    pos = (lax.axis_index("y") * 4 + z) * 4 + lax.axis_index("xh") * 2 + c
    pos = pos * TOK + lax.broadcasted_iota(jnp.int32, (HD // 2, TOK), 1)
    freq = lax.broadcasted_iota(jnp.int32, (HD // 2, TOK), 0).astype(F32)
    angle = pos.astype(F32) * jnp.exp(-jnp.log(THETA) * freq * 2.0 / HD)
    cos_ref[...] = jnp.cos(angle)
    sin_ref[...] = jnp.sin(angle)
    lane = lax.broadcasted_iota(jnp.int32, (1, 128), 1)

    def find(t, acc):
        return jnp.where(lane == own_ref[t], t, acc)

    tile_ref[...] = lax.fori_loop(0, ATT + 3 * FFT, find, jnp.zeros((1, 128), jnp.int32))
    far = {}
    for h in (0, 1):
        for n, up, down in ways:
            one[h, n].wait_recv()
            b = block(h, fc[h][down], sc[h][0]).at[2 * n : 2 * n + 2]
            far[h, n] = go(remote(b, b, f1.at[h, n], q1.at[h, n], ring[h][up]))
    second(3)
    second(1)
    for d in (1, 3, 2):
        x_far[d].wait_recv()
        src = xa_ref.at[chips[4 - d], c]
        x_near.append(go(remote(src, src, bcs.at[d], bcr.at[d], twin)))
    for h in (0, 1):
        for n in (0, 1):
            far[h, n].wait_recv()
    second(2)
    last = []
    for k in (0, 3, 1, 2):
        for h in (0, 1):
            for n, up, down in ways:
                two[h, k, n].wait_recv()
                b = block(h, fc[h][k], sc[h][down]).at[2 * n : 2 * n + 2]
                last.append(go(remote(b, b, f2.at[h, k, n], q2.at[h, k, n], ring[1 - h][up])))
    for step in x_near + last:
        step.wait_recv()
    for step in sent:
        step.wait_send()


def run_start(owners, master, x, gains, cid):
    f = jax.ShapeDtypeStruct
    smem = pl.BlockSpec(memory_space=pltpu.SMEM)
    return pl.pallas_call(
        start_body,
        out_shape=(
            f((4, 4, 2, 4, SLICE, D), BF),
            f((4, 2, TOK, D), BF),
            f((HD // 2, TOK), F32),
            f((HD // 2, TOK), F32),
            f((1, 128), jnp.int32),
        ),
        in_specs=[smem, INV, INV, INV],
        out_specs=(ANY, INV, INV, INV, INV),
        scratch_shapes=[
            pltpu.VMEM((GROUP, SLICE, D), BF),
            DMA,
            DMA((4, 2)), DMA((4, 2)),
            DMA((2, 2)), DMA((2, 2)), DMA((2, 2)), DMA((2, 2)),
            DMA((2, 4, 2)), DMA((2, 4, 2)), DMA((2, 4, 2)), DMA((2, 4, 2)),
            DMA((3,)), DMA((3,)), DMA((4,)), DMA((4,)),
        ],
        compiler_params=params(cid),
    )(owners, master, x, gains)


ORDER = (0, 3, 1, 2)


def layer_body(
    doc_ref, own_ref, wall_ref, xa_ref, x_ref, y_ref, g_ref, cos_ref, sin_ref,
    lo_ref, dr1_ref, dap_ref, gg_ref, raw_ref, qt_ref, k_ref, vt_ref, pt_ref, wo_ref, osl_ref, watt_ref, tg_ref,
    wall, wg, wu, wd, xa, sq, xf, dd, gb, ub, hb, dgb, dub, pbuf, sbuf, near, far, ptl, oto, dgt,
    load_sem, as_, ar, wxs, wxr, wcs, wcr, hs, hr, os_, or_, fxs, fxr, fcs, fcr, bxs, bxr, bcs, bcr,
    ss, sr, rs_, rr, out_sem,
):
    y, z, x, c = here()
    me = x * 2 + c
    twin = place(y, z, x, 1 - c)
    s = seq_index()
    chips = {d: turn(x, d) for d in range(4)}
    peers = {d: place(y, z, chips[d], c) for d in (1, 2, 3)}
    others = [(d, cc) for d in (1, 2, 3) for cc in range(2)]
    greet(
        [place(y, z, chips[d], cc) for d, cc in others]
        + [twin]
        + [seq_place(lax.rem(s + 64 + d, 64)) for d in (-4, -3, -2, -1, 1, 2, 3, 4)]
    )
    load_w = pltpu.make_async_copy(wall_ref, wall, load_sem.at[0])
    load_x = pltpu.make_async_copy(xa_ref, xa, load_sem.at[1])
    load_w.start()
    load_x.start()
    load_w.wait()

    for h in range(HEADS):
        wo_ref[h, me] = wall[own_ref[HEADS + 2 + h]]
    w_far = {}
    w_near = {}
    mine = wo_ref.at[:, me]
    for d in (1, 3, 2):
        w_far[d] = remote(mine, mine, wxs.at[d - 1], wxr.at[d - 1], peers[d])
    w_near[0] = remote(mine, mine, wcs.at[0], wcr.at[0], twin)

    watt = [wall[own_ref[t]] for t in range(HEADS + 2)]
    watt = jnp.concatenate(watt, axis=0)
    watt_ref[...] = watt
    load_x.wait()
    qkv = []
    for d in (2, 1, 3, 0):
        part = nt(watt, xa[chips[d]].reshape(2 * TOK, D)).astype(BF)
        for cc in range(2):
            sq[d, cc] = part[:, cc * TOK : (cc + 1) * TOK].reshape(HEADS + 2, SLICE, TOK)
        if d:
            for cc in range(2):
                step = remote(
                    sq.at[d, cc], raw_ref.at[:, me], as_.at[d, cc], ar.at[d, c], place(y, z, chips[d], cc)
                )
                step.start()
                qkv.append(step)
    step = remote(sq.at[0, 1 - c], raw_ref.at[:, me], as_.at[0, 0], ar.at[0, c], twin)
    step.start()
    qkv.append(step)
    raw_ref[:, me] = sq[0, c]
    for d in (1, 3, 2):
        w_far[d].start()
    w_near[0].start()

    def pack(t, carry):
        rows = pl.ds(pl.multiple_of(t * SLICE, SLICE), SLICE)
        wg[rows] = wall[own_ref[ATT + t]]
        wu[rows] = wall[own_ref[ATT + FFT + t]]
        wd[rows] = wall[own_ref[ATT + 2 * FFT + t]]
        return carry

    lax.fori_loop(0, FFT, pack, 0)
    for d in (1, 2, 3):
        for cc in range(2):
            remote(sq.at[d, cc], raw_ref.at[:, me], as_.at[d, cc], ar.at[d, cc], twin).wait_recv()
    remote(sq.at[0, 0], raw_ref.at[:, me], as_.at[0, 0], ar.at[0, 1 - c], twin).wait_recv()

    cos, sin = cos_ref[...], sin_ref[...]
    gain_q, gain_k = column(g_ref, 0), column(g_ref, 1)
    kt = rope_norm(
        raw_ref[HEADS].reshape(HD, TOK).astype(F32), gain_k, cos, sin
    )
    k_ref[4] = kt.T.astype(BF)
    vt_ref[:, 4 * TOK :] = raw_ref[HEADS + 1].reshape(HD, TOK)
    halo = []
    for d in (4, 3, 2, 1):
        to = seq_place(lax.rem(s + d, 64))
        a = remote(k_ref.at[4], k_ref.at[4 - d], hs.at[0, d - 1], hr.at[0, d - 1], to)
        b = remote(
            vt_ref.at[:, 4 * TOK :], vt_ref.at[:, (4 - d) * TOK : (5 - d) * TOK], hs.at[1, d - 1], hr.at[1, d - 1], to
        )
        a.start()
        b.start()
        halo.extend([a, b])
    for h in range(HEADS):
        q = rope_norm(raw_ref[h].reshape(HD, TOK).astype(F32), gain_q, cos, sin)
        qt_ref[:, h * TOK : (h + 1) * TOK] = q.astype(BF)
    row = lax.broadcasted_iota(jnp.int32, (WINDOW + TOK, TOK), 0)
    col = lax.broadcasted_iota(jnp.int32, (WINDOW + TOK, TOK), 1)
    seen = (row <= col + WINDOW) & (row > col) & (row >= WINDOW - s * TOK)
    half = lax.broadcasted_iota(jnp.int32, (BLK, TOK), 1) < BLK
    q_doc = jnp.where(half, doc_ref[0, 2 * s], doc_ref[0, 2 * s + 1])
    k_doc = jnp.concatenate(
        [
            jnp.full((BLK, TOK), doc_ref[0, jnp.maximum(2 * s - 8 + b, 0)], jnp.int32)
            for b in range(10)
        ],
        axis=0,
    )
    seen = seen & (k_doc == jnp.concatenate([q_doc] * 10, axis=0))
    for step in halo:
        step.wait_recv()
    keys = k_ref[...].reshape(WINDOW + TOK, HD)
    for h in range(HEADS):
        lanes = slice(h * TOK, (h + 1) * TOK)
        sc = nn(keys, qt_ref[:, lanes]) * (HD**-0.5)
        sc = jnp.where(seen, sc, -1e30)
        ex = jnp.exp(sc - jnp.max(sc, axis=0, keepdims=True))
        pr = ex / jnp.sum(ex, axis=0, keepdims=True)
        pt_ref[:, lanes] = pr
        ptl[:, lanes] = pr.astype(BF)
    ot = nn(vt_ref[...], ptl[...])
    oto[...] = ot.astype(BF)
    o_steps = []
    for d, cc in others:
        to = chips[d] * 2 + cc
        rows = pl.ds(pl.multiple_of(to * SLICE, SLICE), SLICE)
        step = remote(
            oto.at[rows], osl_ref.at[me], os_.at[d, cc], or_.at[d, c], place(y, z, chips[d], cc)
        )
        step.start()
        o_steps.append(step)
    rows = pl.ds(pl.multiple_of((x * 2 + 1 - c) * SLICE, SLICE), SLICE)
    step = remote(oto.at[rows], osl_ref.at[me], os_.at[0, 0], or_.at[0, c], twin)
    step.start()
    o_steps.append(step)
    osl_ref[me] = oto[pl.ds(pl.multiple_of(me * SLICE, SLICE), SLICE)]

    for d in (1, 3, 2):
        w_far[d].wait_recv()
        src = wo_ref.at[:, chips[4 - d] * 2 + c]
        w_near[d] = remote(src, src, wcs.at[d], wcr.at[d], twin)
        w_near[d].start()
    for step in w_near.values():
        step.wait()
    ap = jnp.zeros((TOK, D), F32)
    for h in range(HEADS):
        o = ot[:, h * TOK : (h + 1) * TOK].T.astype(BF)
        ap = ap + nn(o, wo_ref[h].reshape(HD, D))
    act = x_ref[...].astype(F32)
    r1 = act + norm_of(ap, g_ref[:, 1 * D : 2 * D])
    xf[x, c] = norm_of(r1, g_ref[:, 2 * D : 3 * D]).astype(BF)

    def gather_start(buf, xs, xr, cs, cr):
        own = buf.at[x, c]
        sends = {d: remote(own, own, xs.at[d - 1], xr.at[d - 1], peers[d]) for d in (1, 3, 2)}
        near_ = {0: remote(own, own, cs.at[0], cr.at[0], twin)}
        near_[0].start()
        for d in (1, 3, 2):
            sends[d].start()
        return sends, near_

    def gather_wait(buf, e, sends, near_, cs, cr):
        if e:
            d = 4 - e
            sends[d].wait_recv()
            src = buf.at[chips[e], c]
            near_[d] = remote(src, src, cs.at[d], cr.at[d], twin)
            near_[d].start()
            near_[d].wait_recv()
        else:
            near_[0].wait_recv()

    def gather_end(sends, near_):
        for step in list(sends.values()) + list(near_.values()):
            step.wait_send()

    def sum_swap(ph, e):
        step = remote(pbuf.at[e, 1 - c], near.at[ph, e], ss.at[ph, e], sr.at[ph, e], twin)
        step.start()
        return step

    def sum_send(ph, e, swap):
        swap.wait_recv()
        both = pbuf[e, c].astype(F32) + near[ph, e].astype(F32)
        if not e:
            return None, both
        sbuf[e - 1] = both.astype(BF)
        step = remote(sbuf.at[e - 1], far.at[ph, e - 1], rs_.at[ph, e - 1], rr.at[ph, e - 1], peers[e])
        step.start()
        return step, None

    def pipeline(ph, buf, xs, xr, cs, cr, block):
        sends, near_ = gather_start(buf, xs, xr, cs, cr)
        swaps, outs = {}, []
        for n, e in enumerate(ORDER):
            gather_wait(buf, e, sends, near_, cs, cr)
            pbuf[e] = block(e).astype(BF).reshape(2, TOK, D)
            swaps[e] = sum_swap(ph, e)
            if n >= 2:
                outs.append(sum_send(ph, ORDER[n - 1], swaps[ORDER[n - 1]])[0])
        outs.append(sum_send(ph, ORDER[3], swaps[ORDER[3]])[0])
        return sends, near_, swaps, outs

    def finish(ph, sends, near_, swaps, outs):
        _, total = sum_send(ph, 0, swaps[0])
        for step in outs:
            step.wait_recv()
        total = ((total + far[ph, 0].astype(F32)) + far[ph, 1].astype(F32)) + far[ph, 2].astype(F32)
        gather_end(sends, near_)
        for step in list(swaps.values()) + outs:
            step.wait_send()
        return total

    def forward(e):
        v = xf[chips[e]].reshape(2 * TOK, D)
        g = nt(v, wg[...])
        u = nt(v, wu[...])
        at = chips[e]
        gb[at] = g
        ub[at] = u
        h, _ = gelu_parts(g)
        hb[at] = (h * u).astype(BF)
        return nn(hb[at], wd[...])

    state = pipeline(0, xf, fxs, fxr, fcs, fcr, forward)
    dn = finish(0, *state)
    lo_ref[...] = (r1 + norm_of(dn, g_ref[:, 3 * D : 4 * D])).astype(BF)
    cot = y_ref[...].astype(F32)
    ddn, d_fpost = norm_back(dn, g_ref[:, 3 * D : 4 * D], cot)
    dd[x, c] = ddn.astype(BF)

    def backward(e):
        v = dd[chips[e]].reshape(2 * TOK, D)
        dh = nt(v, wd[...])
        at = chips[e]
        h, slope = gelu_parts(gb[at])
        dgb[at] = (dh * ub[at] * slope).astype(BF)
        dub[at] = (dh * h).astype(BF)
        return nn(dgb[at], wg[...]) + nn(dub[at], wu[...])

    state = pipeline(1, dd, bxs, bxr, bcs, bcr, backward)
    for i, (lhs, rhs) in enumerate(((dgb, xf), (dub, xf), (hb, dd))):
        for e in range(4):
            dgt[:, e * 2 * TOK : (e + 1) * 2 * TOK] = lhs[e].T
        for n in range(3):
            cols = slice(n * 384, (n + 1) * 384)
            g = nn(dgt[...], rhs[:, :, :, cols].reshape(GROUP * TOK, 384)).astype(BF)
            wall[i * FFT : (i + 1) * FFT, :, cols] = g.reshape(FFT, SLICE, 384)
    out = pltpu.make_async_copy(wall.at[0 : 3 * FFT], tg_ref, out_sem)
    out.start()
    dxf = finish(1, *state)
    e1, d_fpre = norm_back(r1, g_ref[:, 2 * D : 3 * D], dxf)
    dr1 = cot + e1
    dr1_ref[...] = dr1
    dap, d_apost = norm_back(ap, g_ref[:, 1 * D : 2 * D], dr1)
    dap_ref[...] = dap.astype(BF)
    gg_ref[0:1] = d_apost
    gg_ref[1:2] = d_fpre
    gg_ref[2:3] = d_fpost
    for d in (1, 2, 3):
        for cc in range(2):
            remote(oto.at[0:SLICE], osl_ref.at[me], os_.at[d, cc], or_.at[d, cc], twin).wait_recv()
    remote(oto.at[0:SLICE], osl_ref.at[me], os_.at[0, 0], or_.at[0, 1 - c], twin).wait_recv()
    for step in qkv + halo + o_steps + list(w_far.values()):
        step.wait_send()
    out.wait()


def run_layer(doc, owners, slots, xa, x, y, gains, cos, sin, cid):
    f = jax.ShapeDtypeStruct
    smem = pl.BlockSpec(memory_space=pltpu.SMEM)
    vm = pltpu.VMEM
    ffw = FFT * SLICE
    outs = [
        (f((TOK, D), BF), INV),
        (f((TOK, D), F32), INV),
        (f((TOK, D), BF), INV),
        (f((3, D), F32), INV),
        (f((HEADS + 2, GROUP, SLICE, TOK), BF), INV),
        (f((HD, HEADS * TOK), BF), INV),
        (f((5, TOK, HD), BF), INV),
        (f((HD, WINDOW + TOK), BF), INV),
        (f((WINDOW + TOK, HEADS * TOK), F32), INV),
        (f((HEADS, GROUP, SLICE, D), BF), INV),
        (f((GROUP, SLICE, HEADS * TOK), BF), INV),
        (f(((HEADS + 2) * SLICE, D), BF), INV),
        (f((3 * FFT, SLICE, D), BF), ANY),
    ]
    return pl.pallas_call(
        layer_body,
        out_shape=tuple(o[0] for o in outs),
        in_specs=[smem, smem, ANY, ANY, INV, INV, INV, INV, INV],
        out_specs=tuple(o[1] for o in outs),
        scratch_shapes=[
            vm((128, SLICE, D), BF),
            vm((ffw, D), BF),
            vm((ffw, D), BF),
            vm((ffw, D), BF),
            vm((4, 2, TOK, D), BF),
            vm((4, 2, HEADS + 2, SLICE, TOK), BF),
            vm((4, 2, TOK, D), BF),
            vm((4, 2, TOK, D), BF),
            vm((4, 2 * TOK, ffw), F32),
            vm((4, 2 * TOK, ffw), F32),
            vm((4, 2 * TOK, ffw), BF),
            vm((4, 2 * TOK, ffw), BF),
            vm((4, 2 * TOK, ffw), BF),
            vm((4, 2, TOK, D), BF),
            vm((3, TOK, D), BF),
            vm((2, 4, TOK, D), BF),
            vm((2, 3, TOK, D), BF),
            vm((WINDOW + TOK, HEADS * TOK), BF),
            vm((HD, HEADS * TOK), BF),
            vm((ffw, GROUP * TOK), BF),
            DMA((2,)),
            DMA((4, 2)), DMA((4, 2)),
            DMA((3,)), DMA((3,)), DMA((4,)), DMA((4,)),
            DMA((2, 4)), DMA((2, 4)),
            DMA((4, 2)), DMA((4, 2)),
            DMA((3,)), DMA((3,)), DMA((4,)), DMA((4,)),
            DMA((3,)), DMA((3,)), DMA((4,)), DMA((4,)),
            DMA((2, 4)), DMA((2, 4)), DMA((2, 3)), DMA((2, 3)),
            DMA,
        ],
        compiler_params=params(cid),
    )(doc, owners, slots, xa, x, y, gains, cos, sin)


def rope_norm_back(v, g, cos, sin, w):
    r = lax.rsqrt(jnp.mean(v * v, axis=0, keepdims=True) + NORM_EPS)
    a, b = w[: HD // 2], w[HD // 2 :]
    dn = jnp.concatenate([a * cos + b * sin, b * cos - a * sin], axis=0)
    dg = jnp.sum(dn * (v * r), axis=1, keepdims=True)
    u = dn * g
    dv = r * u - v * (r * r * r * jnp.mean(u * v, axis=0, keepdims=True))
    return dv, dg


def rows_add(dst, src, n):
    def step(i, carry):
        dst[i] = (dst[i].astype(F32) + src[i].astype(F32)).astype(BF)
        return carry

    lax.fori_loop(0, n, step, 0)


def back_layer_body(
    tile_ref, dap_ref, osl_ref, wo_ref, k_ref, vt_ref, pt_ref, qt_ref, raw_ref, cos_ref, sin_ref,
    dr1_ref, x_ref, g_ref, gg_ref, watt_ref, xa_ref, tg_ref, gf_ref, gs_ref,
    grad_ref, ig_ref, ng_ref, nf_ref, ns_ref,
    xa, tg, slots, t1, t2, sums, u1, u2, fin, dd, dot_, dst, ptl, hsend, hrec, dqk, drec, dsl,
    pbuf, sbuf, near, far, da, a1, amid, a2, att, gl, gin, gmid, gin2,
    load_sem, bxs, bxr, bcs, bcr, hs, hr, qs, qr, ss, sr, rs_, rr,
    g1s, g1r, g2s, g2r, k1s, k1r, k2s, k2r, a1s, a1r, a2s, a2r, b1s, b1r, b2s, b2r, fs, fr,
    gas, gar, gbs, gbr,
):
    y, z, x, c = here()
    me = x * 2 + c
    twin = place(y, z, x, 1 - c)
    s = seq_index()
    chips = {d: turn(x, d) for d in range(4)}
    peers = {d: place(y, z, chips[d], c) for d in (1, 2, 3)}
    others = [(d, cc) for d in (1, 2, 3) for cc in range(2)]
    at = (y, z)
    ring = (
        {d: place(turn(y, d), z, x, c) for d in (1, 2, 3)},
        {d: place(y, turn(z, d), x, c) for d in (1, 2, 3)},
    )
    greet(
        [place(y, z, chips[d], cc) for d, cc in others]
        + [twin]
        + [seq_place(lax.rem(s + 64 + d, 64)) for d in (-4, -3, -2, -1, 1, 2, 3, 4)]
        + list(ring[0].values())
        + list(ring[1].values())
    )
    load_t = pltpu.make_async_copy(tg_ref, tg, load_sem.at[0])
    load_x = pltpu.make_async_copy(xa_ref, xa, load_sem.at[1])
    load_t.start()
    load_x.start()
    dd[x, c] = dap_ref[...]
    own = dd.at[x, c]
    d_far = {d: remote(own, own, bxs.at[d - 1], bxr.at[d - 1], peers[d]) for d in (1, 3, 2)}
    d_near = {0: remote(own, own, bcs.at[0], bcr.at[0], twin)}
    d_near[0].start()
    for d in (1, 3, 2):
        d_far[d].start()

    load_t.wait()

    def fill(i, carry):
        t = jnp.clip(tile_ref[i] - ATT, 0, 3 * FFT - 1)
        slots[i // 32, lax.rem(i // 8, 4), lax.rem(i // 4, 2), lax.rem(i, 4)] = tg[t]
        return carry

    lax.fori_loop(0, 128, fill, 0)

    def part(h, first, second):
        return slots.at[first, second, 0] if h == 0 else slots.at[second, first, 1]

    sent = []

    def go(step):
        step.start()
        sent.append(step)
        return step

    here1 = {h: {d: turn(at[h], d) for d in range(4)} for h in (0, 1)}
    here2 = {h: {d: turn(at[1 - h], d) for d in range(4)} for h in (0, 1)}
    JS = (2, 1, 3, 0)
    s1 = {}
    for j in JS:
        for h in (0, 1):
            blk = part(h, here1[h][2], here2[h][j])
            s1[h, j, 0] = go(remote(blk.at[0:2], t1.at[h, j, 0], g1s.at[h, j, 0], g1r.at[h, j, 0], ring[h][1]))
            s1[h, j, 1] = go(remote(blk.at[2:4], t1.at[h, j, 1], g1s.at[h, j, 1], g1r.at[h, j, 1], ring[h][3]))

    wo = wo_ref[...].reshape(HEADS * HD, D)
    dmix = nt(wo, dap_ref[...]).astype(BF)
    for h in range(HEADS):
        dot_[:, h * TOK : (h + 1) * TOK] = dmix[h * HD : (h + 1) * HD]
    values = jnp.concatenate([vt_ref[:, b * TOK : (b + 1) * TOK].T for b in range(5)], axis=0)
    for h in range(HEADS):
        lanes = slice(h * TOK, (h + 1) * TOK)
        pr = pt_ref[:, lanes]
        dp = nn(values, dot_[:, lanes])
        inner = jnp.sum(pr * dp, axis=0, keepdims=True)
        dst[:, lanes] = (pr * (dp - inner) * (HD**-0.5)).astype(BF)
        ptl[:, lanes] = pr.astype(BF)
    dk = nt(qt_ref[...], dst[...])
    dv = nt(dot_[...], ptl[...])
    halo = []
    for d in (4, 3, 2, 1):
        lanes = slice((4 - d) * TOK, (5 - d) * TOK)
        hsend[d - 1, 0] = dk[:, lanes].astype(BF)
        hsend[d - 1, 1] = dv[:, lanes].astype(BF)
        step = remote(
            hsend.at[d - 1], hrec.at[d - 1], hs.at[d - 1], hr.at[d - 1], seq_place(lax.rem(s + 64 - d, 64))
        )
        halo.append(go(step))
    dk = dk[:, 4 * TOK :]
    dv = dv[:, 4 * TOK :]
    keys_t = jnp.concatenate([k_ref[b].T for b in range(5)], axis=1)
    cos, sin = cos_ref[...], sin_ref[...]
    gain_q, gain_k = column(g_ref, 0), column(g_ref, 1)
    dgq = jnp.zeros((HD, 1), F32)
    for h in range(HEADS):
        dq = nn(keys_t, dst[:, h * TOK : (h + 1) * TOK])
        raw = raw_ref[h].reshape(HD, TOK).astype(F32)
        dq, dg = rope_norm_back(raw, gain_q, cos, sin, dq)
        dqk[h] = dq.astype(BF).reshape(GROUP, SLICE, TOK)
        dgq = dgq + dg

    s2 = {}
    for j in JS:
        for h in (0, 1):
            s1[h, j, 0].wait_recv()
            blk = part(h, here1[h][1], here2[h][j])
            rows_add(blk.at[0:2], t1.at[h, j, 0], 2)
            s2[h, j, 0] = go(remote(blk, t2.at[h, j, 0], g2s.at[h, j, 0], g2r.at[h, j, 0], ring[h][1]))
            s1[h, j, 1].wait_recv()
            blk = part(h, here1[h][3], here2[h][j])
            rows_add(blk.at[2:4], t1.at[h, j, 1], 2)
            s2[h, j, 1] = go(remote(blk, t2.at[h, j, 1], g2s.at[h, j, 1], g2r.at[h, j, 1], ring[h][3]))

    for step in halo:
        step.wait_recv()
    for d in range(4):
        dk = dk + hrec[d, 0].astype(F32)
        dv = dv + hrec[d, 1].astype(F32)
    raw = raw_ref[HEADS].reshape(HD, TOK).astype(F32)
    dk, dgk = rope_norm_back(raw, gain_k, cos, sin, dk)
    dqk[HEADS] = dk.astype(BF).reshape(GROUP, SLICE, TOK)
    dqk[HEADS + 1] = dv.astype(BF).reshape(GROUP, SLICE, TOK)
    for d, cc in others:
        to = chips[d] * 2 + cc
        go(remote(dqk.at[:, to], drec.at[me], qs.at[d, cc], qr.at[d, c], place(y, z, chips[d], cc)))
    go(remote(dqk.at[:, x * 2 + 1 - c], drec.at[me], qs.at[0, 0], qr.at[0, c], twin))
    drec[me] = dqk[:, me]

    for d in (1, 3, 2):
        d_far[d].wait_recv()
        src = dd.at[chips[4 - d], c]
        d_near[d] = go(remote(src, src, bcs.at[d], bcr.at[d], twin))
    for d in (0, 1, 3, 2):
        d_near[d].wait_recv()
    da[...] = jnp.zeros_like(da)
    for h in range(HEADS):
        for p in range(GROUP):
            dsl[h * SLICE : (h + 1) * SLICE, p * TOK : (p + 1) * TOK] = osl_ref[p, :, h * TOK : (h + 1) * TOK]
    g = nn(dsl[0 : HEADS * SLICE], dd[...].reshape(GROUP * TOK, D)).astype(BF)
    for h in range(HEADS):
        da[(HEADS + 2 + h) // 4, (HEADS + 2 + h) % 4] = g[h * SLICE : (h + 1) * SLICE]

    for d, cc in others:
        remote(dqk.at[:, 0], drec.at[me], qs.at[d, cc], qr.at[d, cc], twin).wait_recv()
    remote(dqk.at[:, 0], drec.at[me], qs.at[0, 0], qr.at[0, 1 - c], twin).wait_recv()
    for p in range(GROUP):
        dsl[:, p * TOK : (p + 1) * TOK] = drec[p].reshape((HEADS + 2) * SLICE, TOK)
    load_x.wait()
    g = nn(dsl[...], xa[...].reshape(GROUP * TOK, D)).astype(BF)
    for t in range(HEADS + 2):
        da[t // 4, t % 4] = g[t * SLICE : (t + 1) * SLICE]

    v1 = []
    for i in (1, 0, 2):
        for h in (0, 1):
            src = dav(da, h, here1[h][i + 1], slice(h * 16, h * 16 + 16))
            v1.append(go(remote(src, a1.at[h, i], a1s.at[h, i], a1r.at[h, i], ring[h][i + 1])))

    swaps, outs = {}, []
    watt = watt_ref[...]

    def sum_send(e):
        swaps[e].wait_recv()
        both = pbuf[e, c].astype(F32) + near[e].astype(F32)
        if not e:
            return both
        sbuf[e - 1] = both.astype(BF)
        outs.append(go(remote(sbuf.at[e - 1], far.at[e - 1], rs_.at[e - 1], rr.at[e - 1], peers[e])))
        return None

    for n, e in enumerate(JS):
        for cc in range(2):
            block = drec[chips[e] * 2 + cc].reshape((HEADS + 2) * SLICE, TOK).T
            pbuf[e, cc] = nn(block, watt).astype(BF)
        swaps[e] = go(remote(pbuf.at[e, 1 - c], near.at[e], ss.at[e], sr.at[e], twin))
        if n:
            sum_send(JS[n - 1])

    for step in v1:
        step.wait_recv()
    v2 = []
    for i in (1, 0, 2, 3):
        for h in (0, 1):
            rows = slice(h * 16, h * 16 + 16)
            j = here2[h][(i + 1) % 4]
            mine = da[at[0], j, rows] if h == 0 else da[j, at[1], rows]
            tot = mine.astype(F32) + a1[h, 0, j].astype(F32)
            tot = (tot + a1[h, 1, j].astype(F32)) + a1[h, 2, j].astype(F32)
            amid[h, i] = tot.astype(BF)
            if i < 3:
                v2.append(go(remote(amid.at[h, i], a2.at[h, i], a2s.at[h, i], a2r.at[h, i], ring[1 - h][i + 1])))

    both = sum_send(0)
    for step in outs:
        step.wait_recv()
    dxa = ((both + far[0].astype(F32)) + far[1].astype(F32)) + far[2].astype(F32)
    act = x_ref[...].astype(F32)
    e2, d_apre = norm_back(act, g_ref[:, 0 * D : 1 * D], dxa)
    ig_ref[...] = dr1_ref[...] + e2
    for k in range(9):
        lanes = slice(k * 128, (k + 1) * 128)
        gl[k : k + 1] = d_apre[:, lanes]
        for m in range(3):
            gl[9 * (m + 1) + k : 9 * (m + 1) + k + 1] = gg_ref[m : m + 1, lanes]
    for m, dg in enumerate((dgq, dgk)):
        flat = jnp.broadcast_to(dg, (HD, 128)).T
        for k in range(2):
            gl[36 + 2 * m + k : 37 + 2 * m + k] = flat[0:1, k * 128 : (k + 1) * 128]
    for d, cc in others:
        go(remote(gl, gin.at[d, c], gas.at[d, cc], gar.at[d, c], place(y, z, chips[d], cc)))
    go(remote(gl, gin.at[0, c], gas.at[0, 0], gar.at[0, c], twin))

    for step in v2:
        step.wait_recv()
    mine = at[0] * 4 + at[1]
    for h in (0, 1):
        rows = slice(h * 16, h * 16 + 16)
        tot = amid[h, 3].astype(F32) + a2[h, 0].astype(F32)
        tot = (tot + a2[h, 1].astype(F32)) + a2[h, 2].astype(F32)
        att[mine, rows] = tot.astype(BF)
    w1 = {}
    for i in (0, 2, 1):
        for h in (0, 1):
            src = att.at[mine, h * 16 : h * 16 + 16]
            w1[h, i] = go(remote(src, src, b1s.at[h, i], b1r.at[h, i], ring[1 - h][i + 1]))
    w2 = []

    def onward(j):
        for h in (0, 1):
            k = at[0] * 4 + here2[h][j] if h == 0 else here2[h][j] * 4 + at[1]
            src = att.at[k, h * 16 : h * 16 + 16]
            for i in (0, 2, 1):
                w2.append(go(remote(src, src, b2s.at[h, j, i], b2r.at[h, j, i], ring[h][i + 1])))

    onward(0)
    for i in (0, 2, 1):
        for h in (0, 1):
            w1[h, i].wait_recv()
        onward(3 - i)

    def close(j):
        for h in (0, 1):
            s2[h, j, 0].wait_recv()
            s2[h, j, 1].wait_recv()
            blk = part(h, here1[h][0], here2[h][j])

            def step(i, carry, h=h, blk=blk):
                t = blk[i].astype(F32) + t2[h, j, 0, i].astype(F32)
                sums[h, j, i] = (t + t2[h, j, 1, i].astype(F32)).astype(BF)
                return carry

            lax.fori_loop(0, 4, step, 0)

    e1, e2_ = {}, {}
    close(2)
    for h in (0, 1):
        e1[h, 0] = go(remote(sums.at[h, 2, 0:2], u1.at[h, 0], k1s.at[h, 0], k1r.at[h, 0], ring[1 - h][1]))
        e1[h, 1] = go(remote(sums.at[h, 2, 2:4], u1.at[h, 1], k1s.at[h, 1], k1r.at[h, 1], ring[1 - h][3]))
    for n, j in ((0, 1), (1, 3)):
        close(j)
        for h in (0, 1):
            e1[h, n].wait_recv()
            rows_add(sums.at[h, j, 2 * n : 2 * n + 2], u1.at[h, n], 2)
            e2_[h, n] = go(remote(sums.at[h, j], u2.at[h, n], k2s.at[h, n], k2r.at[h, n], ring[1 - h][j]))
    close(0)

    for d, cc in others:
        remote(gl, gin.at[d, cc], gas.at[d, cc], gar.at[d, cc], twin).wait_recv()
    remote(gl, gin.at[0, 1 - c], gas.at[0, 0], gar.at[0, 1 - c], twin).wait_recv()
    gin[0, c] = gl[...]
    acc = gin[0, 0] + gin[0, 1]
    for d, cc in others:
        acc = acc + gin[d, cc]
    gmid[0] = acc
    for n in (0, 1):
        steps = [
            go(remote(gmid.at[n], gin2.at[n, d - 1], gbs.at[n, d - 1], gbr.at[n, d - 1], ring[1 - n][d]))
            for d in (1, 2, 3)
        ]
        for step in steps:
            step.wait_recv()
        acc = ((gmid[n] + gin2[n, 0]) + gin2[n, 1]) + gin2[n, 2]
        if n == 0:
            gmid[1] = acc
        else:
            first = BETA_ONE * gf_ref[...] + (1.0 - BETA_ONE) * acc
            second = BETA_TWO * gs_ref[...] + (1.0 - BETA_TWO) * acc * acc
            nf_ref[...] = first
            ns_ref[...] = second
            u = first / (1.0 - BETA_ONE**STEP) / (jnp.sqrt(second / (1.0 - BETA_TWO**STEP)) + ADAM_EPS)
            for k in range(40):
                lanes = slice(k * 128, (k + 1) * 128)
                ng_ref[k : k + 1] = g_ref[:, lanes] - GAIN_RATE * u[k : k + 1]

    for step in w2:
        step.wait_recv()
    for h in (0, 1):
        e2_[h, 0].wait_recv()
        e2_[h, 1].wait_recv()
        for i in range(4):
            t = sums[h, 0, i].astype(F32) + u2[h, 0, i].astype(F32)
            fin[h * 4 + i] = (t + u2[h, 1, i].astype(F32)).astype(BF)
    base = (y * 4 + z) * GROUP
    for q in range(GROUP):
        t = tile_ref[base + q]
        low = att[jnp.clip(t, 0, ATT - 1)]
        fin[q] = jnp.where(t < ATT, low, fin[q])
    for d, cc in others:
        go(
            remote(
                fin.at[member(chips[d], cc)], grad_ref.at[me], fs.at[d, cc], fr.at[d, c], place(y, z, chips[d], cc)
            )
        )
    go(remote(fin.at[member(x, 1 - c)], grad_ref.at[me], fs.at[0, 0], fr.at[0, c], twin))
    grad_ref[me] = fin[member(x, c)]
    for d, cc in others:
        remote(fin.at[0], grad_ref.at[me], fs.at[d, cc], fr.at[d, cc], twin).wait_recv()
    remote(fin.at[0], grad_ref.at[me], fs.at[0, 0], fr.at[0, 1 - c], twin).wait_recv()
    for step in sent + list(d_far.values()) + [d_near[0]]:
        step.wait_send()


def dav(da, h, to, rows):
    return da.at[to, :, rows] if h == 0 else da.at[:, to, rows]


def run_back(tile_of, dap, osl, wo, kk, vt, pt, qt, raw, cos, sin, dr1, x, gains, gg, watt, xa, tg, gf, gs, cid):
    f = jax.ShapeDtypeStruct
    smem = pl.BlockSpec(memory_space=pltpu.SMEM)
    vm = pltpu.VMEM
    return pl.pallas_call(
        back_layer_body,
        out_shape=(f((GROUP, SLICE, D), BF), f((TOK, D), F32)) + (f((40, 128), F32),) * 3,
        in_specs=[smem] + [INV] * 15 + [ANY, ANY, INV, INV],
        out_specs=(INV,) * 5,
        scratch_shapes=[
            vm((4, 2, TOK, D), BF),
            vm((3 * FFT, SLICE, D), BF),
            vm((4, 4, 2, 4, SLICE, D), BF),
            vm((2, 4, 2, 2, SLICE, D), BF),
            vm((2, 4, 2, 4, SLICE, D), BF),
            vm((2, 4, 4, SLICE, D), BF),
            vm((2, 2, 2, SLICE, D), BF),
            vm((2, 2, 4, SLICE, D), BF),
            vm((GROUP, SLICE, D), BF),
            vm((4, 2, TOK, D), BF),
            vm((HD, HEADS * TOK), BF),
            vm((WINDOW + TOK, HEADS * TOK), BF),
            vm((WINDOW + TOK, HEADS * TOK), BF),
            vm((4, 2, HD, TOK), BF),
            vm((4, 2, HD, TOK), BF),
            vm((HEADS + 2, GROUP, SLICE, TOK), BF),
            vm((GROUP, HEADS + 2, SLICE, TOK), BF),
            vm(((HEADS + 2) * SLICE, GROUP * TOK), BF),
            vm((4, 2, TOK, D), BF),
            vm((3, TOK, D), BF),
            vm((4, TOK, D), BF),
            vm((3, TOK, D), BF),
            vm((4, 4, SLICE, D), BF),
            vm((2, 3, 4, 16, D), BF),
            vm((2, 4, 16, D), BF),
            vm((2, 3, 16, D), BF),
            vm((16, SLICE, D), BF),
            vm((40, 128), F32),
            vm((4, 2, 40, 128), F32),
            vm((2, 40, 128), F32),
            vm((2, 3, 40, 128), F32),
            DMA((2,)),
            DMA((3,)), DMA((3,)), DMA((4,)), DMA((4,)),
            DMA((4,)), DMA((4,)),
            DMA((4, 2)), DMA((4, 2)),
            DMA((4,)), DMA((4,)), DMA((3,)), DMA((3,)),
            DMA((2, 4, 2)), DMA((2, 4, 2)), DMA((2, 4, 2)), DMA((2, 4, 2)),
            DMA((2, 2)), DMA((2, 2)), DMA((2, 2)), DMA((2, 2)),
            DMA((2, 3)), DMA((2, 3)), DMA((2, 3)), DMA((2, 3)),
            DMA((2, 3)), DMA((2, 3)), DMA((2, 4, 3)), DMA((2, 4, 3)),
            DMA((4, 2)), DMA((4, 2)),
            DMA((4, 2)), DMA((4, 2)),
            DMA((2, 3)), DMA((2, 3)),
        ],
        compiler_params=params(cid),
    )(tile_of, dap, osl, wo, kk, vt, pt, qt, raw, cos, sin, dr1, x, gains, gg, watt, xa, tg, gf, gs)


def step_body(
    own_ref, g_ref, l_hbm, r_hbm, m_hbm, f_hbm, s_hbm, mo_hbm, fo_hbm, so_hbm, lv, rv, mv, fv, sv, lb, sem
):
    y, z, x, c = here()
    slot = (y * 4 + z) * GROUP + member(x, c)
    ins = [
        pltpu.make_async_copy(a, b, sem.at[i])
        for i, (a, b) in enumerate(((l_hbm, lv), (r_hbm, rv), (f_hbm, fv), (s_hbm, sv), (m_hbm, mv)))
    ]
    for step in ins:
        step.start()
    owned = lax.fori_loop(0, ATT + 3 * FFT, lambda t, a: a + (own_ref[t] == slot).astype(jnp.int32), 0) > 0
    ins[0].wait()
    lb[...] = lv[...].astype(BF)
    rot = nn(g_ref[...].reshape(HD, D), lb[...])
    ins[1].wait()
    right = rv[...].astype(BF)
    rot = nn(rot.T.astype(BF), right)
    ins[2].wait()
    ins[3].wait()
    first = BETA_ONE * fv[...] + (1.0 - BETA_ONE) * rot
    second = BETA_TWO * sv[...] + (1.0 - BETA_TWO) * rot * rot
    u = first / (1.0 - BETA_ONE**STEP) / (jnp.sqrt(second / (1.0 - BETA_TWO**STEP)) + ADAM_EPS)
    fv[...] = jnp.where(owned, first, fv[...])
    sv[...] = jnp.where(owned, second, sv[...])
    outs = [pltpu.make_async_copy(fv, fo_hbm, sem.at[5]), pltpu.make_async_copy(sv, so_hbm, sem.at[6])]
    for step in outs:
        step.start()
    back = nn(lb[...], nt(u.astype(BF), right).astype(BF))
    ins[4].wait()
    w = mv[...]
    mv[...] = jnp.where(owned, w - RATE * (back + DECAY * w), w)
    outs.append(pltpu.make_async_copy(mv, mo_hbm, sem.at[7]))
    outs[2].start()
    for step in outs:
        step.wait()


def run_step(owners, grad, left, right, master, first, second):
    f = jax.ShapeDtypeStruct
    vm = pltpu.VMEM
    tile = f((D, HD), F32)
    return pl.pallas_call(
        step_body,
        out_shape=(tile, tile, tile),
        in_specs=[pl.BlockSpec(memory_space=pltpu.SMEM), INV, ANY, ANY, ANY, ANY, ANY],
        out_specs=(ANY, ANY, ANY),
        scratch_shapes=[
            vm((D, D), F32), vm((HD, HD), F32), vm((D, HD), F32), vm((D, HD), F32), vm((D, HD), F32), vm((D, D), BF),
            DMA((8,)),
        ],
        compiler_params=pltpu.CompilerParams(vmem_limit_bytes=VMEM_LIMIT),
    )(owners, grad, left, right, master, first, second)


def local(
    inputs,
    out_grad,
    doc_ids,
    owners,
    masters,
    first_old,
    second_old,
    left_basis,
    right_basis,
    gains,
    gain_first,
    gain_second,
):
    x = inputs[0]
    row = gains.reshape(1, 5120)
    slots, xa, cos, sin, tile_of = run_start(owners, masters[0], x, row, 1)
    (layer_out, dr1, dap, gg, raw, qt, kk, vt, pt, wo, osl, watt, t_ffn) = run_layer(
        doc_ids, owners, slots.reshape(128, SLICE, D), xa, x, out_grad[0], row, cos, sin, 2
    )
    grad, input_grad, new_gains, new_gain_first, new_gain_second = run_back(
        tile_of.reshape(128), dap, osl, wo, kk, vt, pt, qt, raw, cos, sin, dr1, x, row, gg, watt, xa, t_ffn,
        gain_first.reshape(40, 128), gain_second.reshape(40, 128), 3,
    )
    new_masters, new_first, new_second = run_step(
        owners, grad, left_basis[0], right_basis[0], masters[0], first_old[0], second_old[0]
    )
    return (
        layer_out[None],
        input_grad[None],
        new_masters[None],
        new_first[None],
        new_second[None],
        new_gains.reshape(5120),
        new_gain_first.reshape(5120),
        new_gain_second.reshape(5120),
    )


def solution(mesh):
    wide = Mesh(mesh.devices.reshape(4, 4, 2, 2, 2), AXES)
    tokens = P("xl", ("y", "z", "xh", "core"), None)
    held = P(AXES, None, None)
    return jax.shard_map(
        local,
        mesh=wide,
        in_specs=(tokens, tokens, P("xl", None), P(), held, held, held, held, held, P(), P(), P()),
        out_specs=(tokens, tokens, held, held, held, P(), P(), P()),
        check_vma=False,
    )
```

```python
import functools

import jax
import jax.numpy as jnp
from jax import lax
from jax.experimental import pallas as pl
from jax.experimental.pallas import tpu as pltpu
from jax.sharding import Mesh
from jax.sharding import PartitionSpec as P

FF = 6912
HEADS = 4
WINDOW = 512
BLK = 64
STEP = 10
D = 1152
HD = 256
TOK = 128
GROUP = 8
SLICE = HD // GROUP
ATT = 2 * HEADS + 2
FFT = FF // HD

NORM_EPS = 1e-06
THETA = 10000.0
BETA_ONE = 0.5
BETA_TWO = 0.5
RATE = 0.02
GAIN_RATE = 0.4
DECAY = 0.01
ADAM_EPS = 1e-08

MESH = pl.DeviceIdType.MESH
AXES = ("y", "z", "xh", "core", "xl")
VMEM_LIMIT = 63 * 1024 * 1024
BF = jnp.bfloat16
F32 = jnp.float32


def here():
    y, z, xh, c, xl = [lax.axis_index(a) for a in AXES]
    return y, z, xh * 2 + xl, c


def place(y, z, x, c):
    return (y, z, x // 2, c, lax.rem(x, 2))


def member(x, c):
    return (x // 2) * 4 + c * 2 + lax.rem(x, 2)


def turn(a, d):
    return lax.rem(a + d, 4)


def remote(src, dst, send, recv, where):
    return pltpu.make_async_remote_copy(src, dst, send, recv, device_id=where, device_id_type=MESH)


def params(cid):
    return pltpu.CompilerParams(
        collective_id=cid, has_side_effects=True, vmem_limit_bytes=VMEM_LIMIT
    )


ANY = pl.BlockSpec(memory_space=pl.ANY)
INV = pl.BlockSpec(memory_space=pltpu.VMEM)
DMA = pltpu.SemaphoreType.DMA


def seq_place(s):
    return (s // 16, lax.rem(s // 4, 4), lax.rem(s // 2, 2), lax.rem(s, 2), lax.axis_index("xl"))


def seq_index():
    y, z, xh, c, xl = [lax.axis_index(a) for a in AXES]
    return ((y * 4 + z) * 2 + xh) * 2 + c


def norm_of(v, g):
    return v * lax.rsqrt(jnp.mean(v * v, axis=-1, keepdims=True) + NORM_EPS) * g


def norm_back(v, g, w):
    r = lax.rsqrt(jnp.mean(v * v, axis=-1, keepdims=True) + NORM_EPS)
    u = w * g
    dg = jnp.sum(w * (v * r), axis=0, keepdims=True)
    dv = r * u - v * (r * r * r * jnp.mean(u * v, axis=-1, keepdims=True))
    return dv, dg


def column(g_ref, i):
    row = g_ref[:, 4 * D + i * HD : 4 * D + (i + 1) * HD]
    return jnp.broadcast_to(row, (128, HD)).T[:, 0:1]


def rope_norm(v, g, cos, sin):
    n = v * lax.rsqrt(jnp.mean(v * v, axis=0, keepdims=True) + NORM_EPS) * g
    a, b = n[: HD // 2], n[HD // 2 :]
    return jnp.concatenate([a * cos - b * sin, b * cos + a * sin], axis=0)


def gelu_parts(g):
    k, a = 0.7978845608028654, 0.044715
    sq = g * g
    th = jnp.tanh(k * g * (1.0 + a * sq))
    half = 0.5 * (1.0 + th)
    slope = half + 0.5 * g * (1.0 - th * th) * (k * (1.0 + 3.0 * a * sq))
    return g * half, slope


def nn(a, b):
    return jnp.dot(a, b, preferred_element_type=F32)


def nt(a, b):
    return lax.dot_general(a, b, (((1,), (1,)), ((), ())), preferred_element_type=F32)


def rope_norm_back(v, g, cos, sin, w):
    r = lax.rsqrt(jnp.mean(v * v, axis=0, keepdims=True) + NORM_EPS)
    a, b = w[: HD // 2], w[HD // 2 :]
    dn = jnp.concatenate([a * cos + b * sin, b * cos - a * sin], axis=0)
    dg = jnp.sum(dn * (v * r), axis=1, keepdims=True)
    u = dn * g
    dv = r * u - v * (r * r * r * jnp.mean(u * v, axis=0, keepdims=True))
    return dv, dg


def rows_add(dst, srcs, n):
    def step(i, carry):
        t = dst[i].astype(F32)
        for s in srcs:
            t = t + s[i].astype(F32)
        dst[i] = t.astype(BF)
        return carry

    lax.fori_loop(0, n, step, 0)


ORDER = (0, 3, 1, 2)
JS = (2, 1, 3, 0)
FFW = FFT * SLICE
ROWS = TOK // SLICE


def layer_body(
    doc_ref, own_ref, m_ref, x_ref, y_ref, g_ref,
    lo_ref, ig_ref, gsum_ref, grad_ref, xa_hbm,
    tile, grp, tile_of, tile_ref, wall, wf, xf, dd, dap_all, ab, bb, sbuf, near, far, t1, t2, u1, u2, fin,
    wo, ptl, qt, kb, vt, raw, oto, osl, sq, watt, dst, dot_, hsend, hrec, dqk, drec, dsl,
    da, a1, amid, a2, att, gl, gin, gmid, gin2,
    load_sem, ts, tr, n1s, n1r, n2s, n2r, n3s, n3r, n4s, n4r, xxs, xxr, xcs, xcr, c1s, c1r, c2s, c2r, c3s, c3r, c4s, c4r,
    as_, ar, wxs, wxr, wcs, wcr, hs, hr, os_, or_, fxs, fxr, fcs, fcr, bxs, bxr, bcs, bcr,
    ss, sr, rs_, rr, axs, axr, acs, acr, hbs, hbr, qs, qr, g1s, g1r, g2s, g2r, k1s, k1r, k2s, k2r,
    fs, fr, gas, gar, gbs, gbr,
):
    y, z, x, c = here()
    me = x * 2 + c
    twin = place(y, z, x, 1 - c)
    s = seq_index()
    chips = {d: turn(x, d) for d in range(4)}
    peers = {d: place(y, z, chips[d], c) for d in (1, 2, 3)}
    others = [(d, cc) for d in (1, 2, 3) for cc in range(2)]
    field = [(o - 1, place(turn(y, o // 4), turn(z, o % 4), x, c)) for o in range(1, 16)]
    mine_k = y * 4 + z
    at = (y, z)
    ring = (
        {d: place(turn(y, d), z, x, c) for d in (1, 2, 3)},
        {d: place(y, turn(z, d), x, c) for d in (1, 2, 3)},
    )
    partners = (
        [place(y, z, chips[d], cc) for d, cc in others]
        + [twin]
        + [seq_place(lax.rem(s + 64 + d, 64)) for d in (-4, -3, -2, -1, 1, 2, 3, 4)]
        + [f[1] for f in field]
    )
    sem = pltpu.get_barrier_semaphore()
    for p in partners:
        pl.semaphore_signal(sem, inc=1, device_id=p, device_id_type=MESH)
    for h in range(2):
        tile[4 * h : 4 * h + 4] = m_ref[:, h * 128 : (h + 1) * 128].T.astype(BF).reshape(4, SLICE, D)
    pl.semaphore_wait(sem, len(partners))
    sent = []

    def go(step):
        step.start()
        sent.append(step)
        return step

    def settle(steps):
        for step in steps:
            step.wait_send()
        sent[:] = [a for a in sent if not any(a is b for b in steps)]

    mm = member(x, c)
    base = mine_k * GROUP
    for d, cc in [(2, 0), (2, 1), (1, 0), (1, 1), (3, 0), (3, 1)]:
        go(remote(tile.at[chips[d] * 2 + cc], grp.at[mm], ts.at[d, cc], tr.at[d, c], place(y, z, chips[d], cc)))
    go(remote(tile.at[x * 2 + 1 - c], grp.at[mm], ts.at[0, 0], tr.at[0, c], twin))
    grp[mm] = tile[me]
    dd[x, c] = norm_of(x_ref[...].astype(F32), g_ref[:, 0:D]).astype(BF)
    mine = dd.at[x, c]
    x_far = {d: go(remote(mine, mine, xxs.at[d - 1], xxr.at[d - 1], peers[d])) for d in (1, 3, 2)}
    x_near = {0: go(remote(mine, mine, xcs.at[0], xcr.at[0], twin))}
    pos = s * TOK + lax.broadcasted_iota(jnp.int32, (HD // 2, TOK), 1)
    freq = lax.broadcasted_iota(jnp.int32, (HD // 2, TOK), 0).astype(F32)
    angle = pos.astype(F32) * jnp.exp(-jnp.log(THETA) * freq * 2.0 / HD)
    cos, sin = jnp.cos(angle), jnp.sin(angle)
    lane = lax.broadcasted_iota(jnp.int32, (1, 128), 1)
    tile_of[...] = lax.fori_loop(
        0,
        ATT + 3 * FFT,
        lambda t, acc: jnp.where(lane == own_ref[t], t, acc),
        jnp.zeros((1, 128), jnp.int32),
    )
    to_scalars = pltpu.make_async_copy(tile_of, tile_ref, load_sem.at[0])
    to_scalars.start()
    for d, cc in others:
        remote(tile.at[0], grp.at[mm], ts.at[d, cc], tr.at[d, cc], twin).wait_recv()
    remote(tile.at[0], grp.at[mm], ts.at[0, 0], tr.at[0, 1 - c], twin).wait_recv()
    def halves(h):
        return slice(h * 16, h * 16 + 16)

    def lay(t, v):
        for k in range(9):
            da[t * 9 + k] = v[:, k * 128 : (k + 1) * 128]

    def taken(t):
        return jnp.concatenate([att[t * 9 + k] for k in range(9)], axis=1)

    def set_out(ph):
        steps = []
        for d in (2, 1, 3):
            for h in (0, 1):
                src = da.at[pl.ds(24 * turn(at[h], d), 24), halves(h)]
                steps.append(go(remote(src, a1.at[ph, h, d - 1], c1s.at[ph, h, d - 1], c1r.at[ph, h, d - 1], ring[h][d])))
        return steps

    def add_up(ph, first):
        for step in first:
            step.wait_recv()
        for h in (0, 1):
            tot = da[pl.ds(24 * at[h], 24), halves(h)].astype(F32)
            for i in range(3):
                tot = tot + a1[ph, h, i].astype(F32)
            amid[h] = tot.astype(BF)
        steps = []
        for d in (2, 1, 3):
            for h in (0, 1):
                src = amid.at[h, pl.ds(6 * turn(at[1 - h], d), 6)]
                dst = a2.at[ph, h, d - 1]
                steps.append(go(remote(src, dst, c2s.at[ph, h, d - 1], c2r.at[ph, h, d - 1], ring[1 - h][d])))
        return steps

    def give(ph, second):
        for step in second:
            step.wait_recv()
        steps = []
        for h in (0, 1):
            tot = amid[h, pl.ds(6 * at[1 - h], 6)].astype(F32)
            for i in range(3):
                tot = tot + a2[ph, h, i].astype(F32)
            att[pl.ds(24 * at[h] + 6 * at[1 - h], 6), halves(h)] = tot.astype(BF)
            src = att.at[pl.ds(24 * at[h] + 6 * at[1 - h], 6), halves(h)]
            for d in (2, 1, 3):
                steps.append(go(remote(src, src, c3s.at[ph, h, d - 1], c3r.at[ph, h, d - 1], ring[1 - h][d])))
        return steps

    def give_on(ph, third):
        for step in third:
            step.wait_recv()
        steps = []
        for h in (0, 1):
            src = att.at[pl.ds(24 * at[h], 24), halves(h)]
            for d in (2, 1, 3):
                steps.append(go(remote(src, src, c4s.at[ph, h, d - 1], c4r.at[ph, h, d - 1], ring[h][d])))
        return steps

    for t in range(ATT):
        rel = own_ref[t] - base
        v = grp[jnp.clip(rel, 0, GROUP - 1)]
        lay(t, jnp.where((rel >= 0) & (rel < GROUP), v, jnp.zeros_like(v)))

    routed = set_out(0)
    wall[pl.ds(base, GROUP)] = grp[...]

    w_at = (z, y)
    f_at = {h: {d: turn(w_at[h], d) for d in range(4)} for h in (0, 1)}
    s_at = {h: {d: turn(w_at[1 - h], d) for d in range(4)} for h in (0, 1)}
    ways = ((0, 1, 3), (1, 3, 1))

    def block(h, first, second):
        yy, zz = (second, first) if h == 0 else (first, second)
        return wall.at[pl.ds(((yy * 4 + zz) * 2 + h) * 4, 4)]

    one, two, far1 = {}, {}, {}
    for h in (0, 1):
        for n, up, _ in ways:
            src = grp.at[4 * h : 4 * h + 4]
            one[h, n] = go(remote(src, block(h, f_at[h][0], s_at[h][0]), n1s.at[h, n], n1r.at[h, n], ring[1 - h][up]))

    def second(k):
        for h in (0, 1):
            b = block(h, f_at[h][k], s_at[h][0])
            src = b if k else grp.at[4 * h : 4 * h + 4]
            for n, up, _ in ways:
                two[h, k, n] = go(remote(src, b, n2s.at[h, k, n], n2r.at[h, k, n], ring[h][up]))

    def onward(k):
        for h in (0, 1):
            for n, up, down in ways:
                two[h, k, n].wait_recv()
                b = block(h, f_at[h][k], s_at[h][down]).at[2 * n : 2 * n + 2]
                last.append(go(remote(b, b, n4s.at[h, k, n], n4r.at[h, k, n], ring[h][up])))

    last = []
    for d in (1, 3, 2):
        x_far[d].wait_recv()
        src = dd.at[chips[4 - d], c]
        x_near[d] = go(remote(src, src, xcs.at[d], xcr.at[d], twin))
    added = add_up(0, routed)
    second(0)
    for h in (0, 1):
        for n, up, down in ways:
            one[h, n].wait_recv()
            b = block(h, f_at[h][down], s_at[h][0]).at[2 * n : 2 * n + 2]
            far1[h, n] = go(remote(b, b, n3s.at[h, n], n3r.at[h, n], ring[1 - h][up]))
    given = give(0, added)
    for step in x_near.values():
        step.wait_recv()
    save_x = pltpu.make_async_copy(dd, xa_hbm, load_sem.at[1])
    save_x.start()
    given_on = give_on(0, given)
    second(3)
    for step in given_on:
        step.wait_recv()

    for t in range(HEADS + 2):
        watt[t * SLICE : (t + 1) * SLICE] = taken(t)
    for h in range(HEADS):
        wo[h, me] = taken(HEADS + 2 + h)
    for d in (2, 1, 3, 0):
        part = nt(watt[...], dd[chips[d]].reshape(2 * TOK, D)).astype(BF)
        for cc in range(2):
            sq[d, cc] = part[:, cc * TOK : (cc + 1) * TOK].reshape(HEADS + 2, SLICE, TOK)
        if d:
            for cc in range(2):
                go(remote(sq.at[d, cc], raw.at[:, me], as_.at[d, cc], ar.at[d, c], place(y, z, chips[d], cc)))
    go(remote(sq.at[0, 1 - c], raw.at[:, me], as_.at[0, 0], ar.at[0, c], twin))
    raw[:, me] = sq[0, c]
    for d, cc in others:
        remote(sq.at[d, cc], raw.at[:, me], as_.at[d, cc], ar.at[d, cc], twin).wait_recv()
    remote(sq.at[0, 0], raw.at[:, me], as_.at[0, 0], ar.at[0, 1 - c], twin).wait_recv()

    gain_q, gain_k = column(g_ref, 0), column(g_ref, 1)
    kt = rope_norm(raw[HEADS].reshape(HD, TOK).astype(F32), gain_k, cos, sin)
    kb[4] = kt.T.astype(BF)
    vt[:, 4 * TOK :] = raw[HEADS + 1].reshape(HD, TOK)
    halo = []
    for d in (4, 3, 2, 1):
        to = seq_place(lax.rem(s + d, 64))
        lanes = slice((4 - d) * TOK, (5 - d) * TOK)
        halo.append(go(remote(kb.at[4], kb.at[4 - d], hs.at[0, d - 1], hr.at[0, d - 1], to)))
        halo.append(go(remote(vt.at[:, 4 * TOK :], vt.at[:, lanes], hs.at[1, d - 1], hr.at[1, d - 1], to)))
    mine = wo.at[:, me]
    w_far = {d: go(remote(mine, mine, wxs.at[d - 1], wxr.at[d - 1], peers[d])) for d in (1, 3, 2)}
    w_near = {0: go(remote(mine, mine, wcs.at[0], wcr.at[0], twin))}
    second(1)
    for step in far1.values():
        step.wait_recv()
    second(2)
    for h in range(HEADS):
        q = rope_norm(raw[h].reshape(HD, TOK).astype(F32), gain_q, cos, sin)
        qt[:, h * TOK : (h + 1) * TOK] = q.astype(BF)
    row = lax.broadcasted_iota(jnp.int32, (WINDOW + TOK, TOK), 0)
    col = lax.broadcasted_iota(jnp.int32, (WINDOW + TOK, TOK), 1)
    seen = (row <= col + WINDOW) & (row > col) & (row >= WINDOW - s * TOK)
    half = lax.broadcasted_iota(jnp.int32, (BLK, TOK), 1) < BLK
    q_doc = jnp.where(half, doc_ref[0, 2 * s], doc_ref[0, 2 * s + 1])
    k_doc = jnp.concatenate(
        [jnp.full((BLK, TOK), doc_ref[0, jnp.maximum(2 * s - 8 + b, 0)], jnp.int32) for b in range(10)],
        axis=0,
    )
    seen = seen & (k_doc == jnp.concatenate([q_doc] * 10, axis=0))
    onward(0)
    for step in halo:
        step.wait_recv()
    keys = kb[...].reshape(WINDOW + TOK, HD)
    for h in range(HEADS):
        lanes = slice(h * TOK, (h + 1) * TOK)
        sc = nn(keys, qt[:, lanes]) * (HD**-0.5)
        sc = jnp.where(seen, sc, -1e30)
        ex = jnp.exp(sc - jnp.max(sc, axis=0, keepdims=True))
        ptl[:, lanes] = (ex / jnp.sum(ex, axis=0, keepdims=True)).astype(BF)
    ot = nn(vt[...], ptl[...])
    oto[...] = ot.astype(BF)
    for d, cc in others:
        rows = pl.ds(pl.multiple_of((chips[d] * 2 + cc) * SLICE, SLICE), SLICE)
        go(remote(oto.at[rows], osl.at[me], os_.at[d, cc], or_.at[d, c], place(y, z, chips[d], cc)))
    rows = pl.ds(pl.multiple_of((x * 2 + 1 - c) * SLICE, SLICE), SLICE)
    go(remote(oto.at[rows], osl.at[me], os_.at[0, 0], or_.at[0, c], twin))
    osl[me] = oto[pl.ds(pl.multiple_of(me * SLICE, SLICE), SLICE)]

    onward(3)
    onward(1)
    for d in (1, 3, 2):
        w_far[d].wait_recv()
        src = wo.at[:, chips[4 - d] * 2 + c]
        w_near[d] = go(remote(src, src, wcs.at[d], wcr.at[d], twin))
    for step in w_near.values():
        step.wait_recv()
    ap = jnp.zeros((TOK, D), F32)
    for h in range(HEADS):
        o = ot[:, h * TOK : (h + 1) * TOK].T.astype(BF)
        ap = ap + nn(o, wo[h].reshape(HD, D))
    act = x_ref[...].astype(F32)
    r1 = act + norm_of(ap, g_ref[:, 1 * D : 2 * D])
    xf[x, c] = norm_of(r1, g_ref[:, 2 * D : 3 * D]).astype(BF)

    def gather_start(buf, xs, xr, cs, cr):
        own = buf.at[x, c]
        near_ = {0: go(remote(own, own, cs.at[0], cr.at[0], twin))}
        sends = {d: go(remote(own, own, xs.at[d - 1], xr.at[d - 1], peers[d])) for d in (1, 3, 2)}
        return sends, near_

    def gather_wait(buf, e, sends, near_, cs, cr):
        if e:
            d = 4 - e
            sends[d].wait_recv()
            src = buf.at[chips[e], c]
            near_[d] = go(remote(src, src, cs.at[d], cr.at[d], twin))
            near_[d].wait_recv()
        else:
            near_[0].wait_recv()

    def pbuf(ph, e, cc):
        return (wall if ph < 2 else wf).at[pl.ds((2 * e + cc) * ROWS, ROWS)]

    def sum_swap(ph, n, e):
        return go(remote(pbuf(ph, e, 1 - c), near.at[n, e], ss.at[ph, e], sr.at[ph, e], twin))

    def sum_send(ph, n, e, swap):
        swap.wait_recv()
        both = pbuf(ph, e, c)[...].astype(F32) + near[n, e].astype(F32)
        if not e:
            return None, both
        sbuf[e - 1] = both.astype(BF)
        return go(remote(sbuf.at[e - 1], far.at[n, e - 1], rs_.at[ph, e - 1], rr.at[ph, e - 1], peers[e])), None

    def finish(n, swaps, outs, ph, total=None):
        if total is None:
            _, total = sum_send(ph, n, 0, swaps[0])
            settle(list(swaps.values()))
        for step in outs:
            step.wait_recv()
        total = ((total + far[n, 0].astype(F32)) + far[n, 1].astype(F32)) + far[n, 2].astype(F32)
        settle(outs)
        return total.reshape(TOK, D)

    def pipeline(ph, order, ready, block):
        swaps, outs = {}, []
        for n, e in enumerate(order):
            ready(e)
            part = block(e).astype(BF).reshape(2, ROWS, SLICE, D)
            for cc in range(2):
                pbuf(ph, e, cc)[...] = part[cc]
            swaps[e] = sum_swap(ph, ph % 2, e)
            if n and order[n - 1]:
                outs.append(sum_send(ph, ph % 2, order[n - 1], swaps[order[n - 1]])[0])
        if order[3]:
            outs.append(sum_send(ph, ph % 2, order[3], swaps[order[3]])[0])
        return swaps, outs, ph

    def put(k, e, v):
        cols = pl.ds(pl.multiple_of(chips[e] * 2 * TOK, 2 * TOK), 2 * TOK)
        wall[32 + k * FFT : 32 + (k + 1) * FFT, :, cols] = v.T.reshape(FFT, SLICE, 2 * TOK)

    def tiles(k):
        return wf[k * FFT : (k + 1) * FFT].reshape(FFW, D)

    def forward(e):
        v = xf[chips[e]].reshape(2 * TOK, D)
        g = nt(v, tiles(0))
        u = nt(v, tiles(1))
        h, slope = gelu_parts(g)
        ab[e] = (u * slope).astype(BF)
        bb[e] = h.astype(BF)
        hid = (h * u).astype(BF)
        put(2, e, hid)
        return nn(hid, tiles(2))

    sends, near_ = gather_start(xf, fxs, fxr, fcs, fcr)
    onward(2)
    for step in last:
        step.wait_recv()

    def pack(t, carry):
        wf[t] = wall[own_ref[ATT + t]]
        return carry

    lax.fori_loop(0, 3 * FFT, pack, 0)
    settle(list(two.values()) + list(far1.values()) + last + list(x_far.values()) + list(x_near.values()))
    save_x.wait()
    to_scalars.wait()
    settle(routed + added + given + given_on)
    state = pipeline(0, ORDER, lambda e: gather_wait(xf, e, sends, near_, fcs, fcr), forward)
    dn = finish(0, *state)
    lo_ref[...] = (r1 + norm_of(dn, g_ref[:, 3 * D : 4 * D])).astype(BF)
    cot = y_ref[...].astype(F32)
    ddn, d_fpost = norm_back(dn, g_ref[:, 3 * D : 4 * D], cot)
    dd[x, c] = ddn.astype(BF)

    def backward(e):
        v = dd[chips[e]].reshape(2 * TOK, D)
        dh = nt(v, tiles(2))
        dg = (dh * ab[e].astype(F32)).astype(BF)
        du = (dh * bb[e].astype(F32)).astype(BF)
        put(0, e, dg)
        put(1, e, du)
        return nn(dg, tiles(0)) + nn(du, tiles(1))

    sends_b, near_b = gather_start(dd, bxs, bxr, bcs, bcr)
    state = pipeline(1, ORDER, lambda e: gather_wait(dd, e, sends_b, near_b, bcs, bcr), backward)

    for k, rhs in enumerate((xf, xf, dd)):
        left = wall[32 + k * FFT : 32 + (k + 1) * FFT, :, 0 : GROUP * TOK].reshape(FFW, GROUP * TOK)
        for n in range(3):
            cols = slice(n * 384, (n + 1) * 384)
            g = nn(left, rhs[:, :, :, cols].reshape(GROUP * TOK, 384)).astype(BF)
            wf[k * FFT : (k + 1) * FFT, :, cols] = g.reshape(FFT, SLICE, 384)
    _, rest = sum_send(1, 1, 0, state[0][0])
    settle(list(state[0].values()))

    def fill(i, carry):
        wall[i] = wf[jnp.clip(tile_ref[0, i] - ATT, 0, 3 * FFT - 1)]
        return carry

    lax.fori_loop(0, 128, fill, 0)

    def part(h, first, second):
        yy, zz = (first, second) if h == 0 else (second, first)
        return wall.at[pl.ds(((yy * 4 + zz) * 2 + h) * 4, 4)]

    here1 = {h: {d: turn(at[h], d) for d in range(4)} for h in (0, 1)}
    here2 = {h: {d: turn(at[1 - h], d) for d in range(4)} for h in (0, 1)}
    s1 = {}
    for j in JS:
        for h in (0, 1):
            blk = part(h, here1[h][2], here2[h][j])
            s1[h, j, 0] = go(remote(blk.at[0:2], t1.at[h, j, 0], g1s.at[h, j, 0], g1r.at[h, j, 0], ring[h][1]))
            s1[h, j, 1] = go(remote(blk.at[2:4], t1.at[h, j, 1], g1s.at[h, j, 1], g1r.at[h, j, 1], ring[h][3]))

    dxf = finish(1, *state, rest)
    e1, d_fpre = norm_back(r1, g_ref[:, 2 * D : 3 * D], dxf)
    dr1 = cot + e1
    ig_ref[...] = dr1
    dap, d_apost = norm_back(ap, g_ref[:, 1 * D : 2 * D], dr1)
    dap_all[x, c] = dap.astype(BF)
    sends_a, near_a = gather_start(dap_all, axs, axr, acs, acr)

    dmix = nt(wo[...].reshape(HEADS * HD, D), dap.astype(BF)).astype(BF)
    for h in range(HEADS):
        dot_[:, h * TOK : (h + 1) * TOK] = dmix[h * HD : (h + 1) * HD]
    values = jnp.concatenate([vt[:, b * TOK : (b + 1) * TOK].T for b in range(5)], axis=0)
    for h in range(HEADS):
        lanes = slice(h * TOK, (h + 1) * TOK)
        pr = ptl[:, lanes].astype(F32)
        dp = nn(values, dot_[:, lanes])
        inner = jnp.sum(pr * dp, axis=0, keepdims=True)
        dst[:, lanes] = (pr * (dp - inner) * (HD**-0.5)).astype(BF)
    dk = nt(qt[...], dst[...])
    dv = nt(dot_[...], ptl[...])
    back = []
    for d in (4, 3, 2, 1):
        lanes = slice((4 - d) * TOK, (5 - d) * TOK)
        hsend[d - 1, 0] = dk[:, lanes].astype(BF)
        hsend[d - 1, 1] = dv[:, lanes].astype(BF)
        to = seq_place(lax.rem(s + 64 - d, 64))
        back.append(go(remote(hsend.at[d - 1], hrec.at[d - 1], hbs.at[d - 1], hbr.at[d - 1], to)))
    dk = dk[:, 4 * TOK :]
    dv = dv[:, 4 * TOK :]
    settle(list(sends.values()) + list(near_.values()))
    load_x = pltpu.make_async_copy(xa_hbm, xf, load_sem.at[2])
    load_x.start()
    keys_t = jnp.concatenate([kb[b].T for b in range(5)], axis=1)
    dgq = jnp.zeros((HD, 1), F32)
    for h in range(HEADS):
        dq = nn(keys_t, dst[:, h * TOK : (h + 1) * TOK])
        dq, dg = rope_norm_back(raw[h].reshape(HD, TOK).astype(F32), gain_q, cos, sin, dq)
        dqk[h] = dq.astype(BF).reshape(GROUP, SLICE, TOK)
        dgq = dgq + dg

    for step in back:
        step.wait_recv()
    for d in range(4):
        dk = dk + hrec[d, 0].astype(F32)
        dv = dv + hrec[d, 1].astype(F32)
    dk, dgk = rope_norm_back(raw[HEADS].reshape(HD, TOK).astype(F32), gain_k, cos, sin, dk)
    dqk[HEADS] = dk.astype(BF).reshape(GROUP, SLICE, TOK)
    dqk[HEADS + 1] = dv.astype(BF).reshape(GROUP, SLICE, TOK)
    for d, cc in others:
        to = chips[d] * 2 + cc
        go(remote(dqk.at[:, to], drec.at[me], qs.at[d, cc], qr.at[d, c], place(y, z, chips[d], cc)))
    go(remote(dqk.at[:, x * 2 + 1 - c], drec.at[me], qs.at[0, 0], qr.at[0, c], twin))
    drec[me] = dqk[:, me]

    s2 = {}

    def pass_on(j):
        for h in (0, 1):
            s1[h, j, 0].wait_recv()
            blk = part(h, here1[h][1], here2[h][j])
            rows_add(blk.at[0:2], [t1.at[h, j, 0]], 2)
            s2[h, j, 0] = go(remote(blk, t2.at[h, j, 0], g2s.at[h, j, 0], g2r.at[h, j, 0], ring[h][1]))
            s1[h, j, 1].wait_recv()
            blk = part(h, here1[h][3], here2[h][j])
            rows_add(blk.at[2:4], [t1.at[h, j, 1]], 2)
            s2[h, j, 1] = go(remote(blk, t2.at[h, j, 1], g2s.at[h, j, 1], g2r.at[h, j, 1], ring[h][3]))

    for e in (0, 3, 1, 2):
        gather_wait(dap_all, e, sends_a, near_a, acs, acr)
    for d, cc in others:
        remote(oto.at[0:SLICE], osl.at[me], os_.at[d, cc], or_.at[d, cc], twin).wait_recv()
    remote(oto.at[0:SLICE], osl.at[me], os_.at[0, 0], or_.at[0, 1 - c], twin).wait_recv()
    for h in range(HEADS):
        for p in range(GROUP):
            dsl[h * SLICE : (h + 1) * SLICE, p * TOK : (p + 1) * TOK] = osl[p, :, h * TOK : (h + 1) * TOK]
    g = nn(dsl[0 : HEADS * SLICE], dap_all[...].reshape(GROUP * TOK, D)).astype(BF)
    for h in range(HEADS):
        lay(HEADS + 2 + h, g[h * SLICE : (h + 1) * SLICE])

    pass_on(2)
    pass_on(1)
    for d, cc in others:
        remote(dqk.at[:, 0], drec.at[me], qs.at[d, cc], qr.at[d, cc], twin).wait_recv()
    remote(dqk.at[:, 0], drec.at[me], qs.at[0, 0], qr.at[0, 1 - c], twin).wait_recv()
    for p in range(GROUP):
        dsl[:, p * TOK : (p + 1) * TOK] = drec[p].reshape((HEADS + 2) * SLICE, TOK)
    load_x.wait()
    g = nn(dsl[...], xf[...].reshape(GROUP * TOK, D)).astype(BF)
    for t in range(HEADS + 2):
        lay(t, g[t * SLICE : (t + 1) * SLICE])

    routed = set_out(1)
    pass_on(3)
    pass_on(0)

    def inputs_back(e):
        pair = [
            nn(drec[chips[e] * 2 + cc].reshape((HEADS + 2) * SLICE, TOK).T, watt[...]) for cc in range(2)
        ]
        return jnp.concatenate(pair, axis=0)

    state = pipeline(2, JS, lambda e: None, inputs_back)

    added = add_up(1, routed)

    def close(j):
        for h in (0, 1):
            s2[h, j, 0].wait_recv()
            s2[h, j, 1].wait_recv()
            rows_add(part(h, here1[h][0], here2[h][j]), [t2.at[h, j, 0], t2.at[h, j, 1]], 4)

    e1, e2 = {}, {}
    close(2)
    for h in (0, 1):
        blk = part(h, here1[h][0], here2[h][2])
        e1[h, 0] = go(remote(blk.at[0:2], u1.at[h, 0], k1s.at[h, 0], k1r.at[h, 0], ring[1 - h][1]))
        e1[h, 1] = go(remote(blk.at[2:4], u1.at[h, 1], k1s.at[h, 1], k1r.at[h, 1], ring[1 - h][3]))

    close(1)
    close(3)
    given = give(1, added)
    for n, j in ((0, 1), (1, 3)):
        for h in (0, 1):
            blk = part(h, here1[h][0], here2[h][j])
            e1[h, n].wait_recv()
            rows_add(blk.at[2 * n : 2 * n + 2], [u1.at[h, n]], 2)
            e2[h, n] = go(remote(blk, u2.at[h, n], k2s.at[h, n], k2r.at[h, n], ring[1 - h][j]))

    given_on = give_on(1, given)
    dxa = finish(0, *state)
    ein, d_apre = norm_back(x_ref[...].astype(F32), g_ref[:, 0 * D : 1 * D], dxa)
    ig_ref[...] = ig_ref[...] + ein
    for k in range(9):
        lanes = slice(k * 128, (k + 1) * 128)
        for m, dg in enumerate((d_apre, d_apost, d_fpre, d_fpost)):
            gl[9 * m + k : 9 * m + k + 1] = dg[:, lanes]
    for m, dg in enumerate((dgq, dgk)):
        flat = jnp.broadcast_to(dg, (HD, 128)).T
        for k in range(2):
            gl[36 + 2 * m + k : 37 + 2 * m + k] = flat[0:1, k * 128 : (k + 1) * 128]
    for d, cc in others:
        go(remote(gl, gin.at[x, c], gas.at[d, cc], gar.at[d, c], place(y, z, chips[d], cc)))
    go(remote(gl, gin.at[x, c], gas.at[0, 0], gar.at[0, c], twin))
    gin[x, c] = gl[...]

    for d, cc in others:
        remote(gl, gin.at[x, c], gas.at[d, cc], gar.at[d, cc], twin).wait_recv()
    remote(gl, gin.at[x, c], gas.at[0, 0], gar.at[0, 1 - c], twin).wait_recv()
    acc = gin[0, 0]
    for p in range(1, GROUP):
        acc = acc + gin[p // 2, p % 2]
    gmid[...] = acc
    gin2[mine_k] = acc
    all_gains = [go(remote(gmid, gin2.at[mine_k], gbs.at[o], gbr.at[o], to)) for o, to in field]
    close(0)

    for step in given_on:
        step.wait_recv()
    for h in (0, 1):
        e2[h, 0].wait_recv()
        e2[h, 1].wait_recv()
        blk = part(h, here1[h][0], here2[h][0])
        rows_add(blk, [u2.at[h, 0], u2.at[h, 1]], 4)
    for q in range(GROUP):
        t = tile_ref[0, base + q]
        low = taken(jnp.clip(t, 0, ATT - 1))
        fin[q] = jnp.where(t < ATT, low, wall[base + q])
    for d, cc in others:
        src = fin.at[member(chips[d], cc)]
        go(remote(src, grad_ref.at[me], fs.at[d, cc], fr.at[d, c], place(y, z, chips[d], cc)))
    go(remote(fin.at[member(x, 1 - c)], grad_ref.at[me], fs.at[0, 0], fr.at[0, c], twin))
    grad_ref[me] = fin[member(x, c)]
    for step in all_gains:
        step.wait_recv()
    acc = gin2[0]
    for k in range(1, 16):
        acc = acc + gin2[k]
    gsum_ref[...] = acc
    for d, cc in others:
        remote(fin.at[0], grad_ref.at[me], fs.at[d, cc], fr.at[d, cc], twin).wait_recv()
    remote(fin.at[0], grad_ref.at[me], fs.at[0, 0], fr.at[0, 1 - c], twin).wait_recv()
    for step in sent:
        step.wait_send()


def run_layer(doc, owners, master, x, y, gains, cid):
    f = jax.ShapeDtypeStruct
    smem = pl.BlockSpec(memory_space=pltpu.SMEM)
    vm = pltpu.VMEM
    blocks = (TOK // SLICE, SLICE, D)
    lanes = HEADS * TOK
    seen = WINDOW + TOK
    qkv = HEADS + 2
    return pl.pallas_call(
        layer_body,
        out_shape=(
            f((TOK, D), BF),
            f((TOK, D), F32),
            f((40, 128), F32),
            f((GROUP, SLICE, D), BF),
            f((4, 2, TOK, D), BF),
        ),
        in_specs=[smem, smem, INV, INV, INV, INV],
        out_specs=(INV, INV, INV, INV, ANY),
        scratch_shapes=[
            vm((GROUP, SLICE, D), BF),
            vm((GROUP, SLICE, D), BF),
            vm((1, 128), jnp.int32),
            pltpu.SMEM((1, 128), jnp.int32),
            vm((128, SLICE, D), BF),
            vm((3 * FFT, SLICE, D), BF),
            vm((4, 2, TOK, D), BF),
            vm((4, 2, TOK, D), BF),
            vm((4, 2, TOK, D), BF),
            vm((4, 2 * TOK, FFW), BF),
            vm((4, 2 * TOK, FFW), BF),
            vm((3,) + blocks, BF),
            vm((2, 4) + blocks, BF),
            vm((2, 3) + blocks, BF),
            vm((2, 4, 2, 2, SLICE, D), BF),
            vm((2, 4, 2, 4, SLICE, D), BF),
            vm((2, 2, 2, SLICE, D), BF),
            vm((2, 2, 4, SLICE, D), BF),
            vm((GROUP, SLICE, D), BF),
            vm((HEADS, GROUP, SLICE, D), BF),
            vm((seen, lanes), BF),
            vm((HD, lanes), BF),
            vm((5, TOK, HD), BF),
            vm((HD, seen), BF),
            vm((qkv, GROUP, SLICE, TOK), BF),
            vm((HD, lanes), BF),
            vm((GROUP, SLICE, lanes), BF),
            vm((4, 2, qkv, SLICE, TOK), BF),
            vm((qkv * SLICE, D), BF),
            vm((seen, lanes), BF),
            vm((HD, lanes), BF),
            vm((4, 2, HD, TOK), BF),
            vm((4, 2, HD, TOK), BF),
            vm((qkv, GROUP, SLICE, TOK), BF),
            vm((GROUP, qkv, SLICE, TOK), BF),
            vm((qkv * SLICE, GROUP * TOK), BF),
            vm((96, SLICE, 128), BF),
            vm((2, 2, 3, 24, 16, 128), BF),
            vm((2, 24, 16, 128), BF),
            vm((2, 2, 3, 6, 16, 128), BF),
            vm((96, SLICE, 128), BF),
            vm((40, 128), F32),
            vm((4, 2, 40, 128), F32),
            vm((40, 128), F32),
            vm((16, 40, 128), F32),
            DMA((3,)),
            DMA((4, 2)), DMA((4, 2)),
            DMA((2, 2)), DMA((2, 2)), DMA((2, 4, 2)), DMA((2, 4, 2)),
            DMA((2, 2)), DMA((2, 2)), DMA((2, 4, 2)), DMA((2, 4, 2)),
            DMA((3,)), DMA((3,)), DMA((4,)), DMA((4,)),
            DMA((2, 2, 3)), DMA((2, 2, 3)), DMA((2, 2, 3)), DMA((2, 2, 3)),
            DMA((2, 2, 3)), DMA((2, 2, 3)), DMA((2, 2, 3)), DMA((2, 2, 3)),
            DMA((4, 2)), DMA((4, 2)),
            DMA((3,)), DMA((3,)), DMA((4,)), DMA((4,)),
            DMA((2, 4)), DMA((2, 4)),
            DMA((4, 2)), DMA((4, 2)),
            DMA((3,)), DMA((3,)), DMA((4,)), DMA((4,)),
            DMA((3,)), DMA((3,)), DMA((4,)), DMA((4,)),
            DMA((3, 4)), DMA((3, 4)), DMA((3, 3)), DMA((3, 3)),
            DMA((3,)), DMA((3,)), DMA((4,)), DMA((4,)),
            DMA((4,)), DMA((4,)),
            DMA((4, 2)), DMA((4, 2)),
            DMA((2, 4, 2)), DMA((2, 4, 2)), DMA((2, 4, 2)), DMA((2, 4, 2)),
            DMA((2, 2)), DMA((2, 2)), DMA((2, 2)), DMA((2, 2)),
            DMA((4, 2)), DMA((4, 2)),
            DMA((4, 2)), DMA((4, 2)),
            DMA((15,)), DMA((15,)),
        ],
        compiler_params=params(cid),
    )(doc, owners, master, x, y, gains)


def step_body(
    own_ref, g_ref, gsum_ref, gain_ref, gf_ref, gs_ref, lo_ref, ig_ref, l_hbm, r_hbm, m_hbm, f_hbm, s_hbm,
    mo_hbm, fo_hbm, so_hbm, ng_ref, nf_ref, ns_ref, lo_out, ig_out, lv, rv, mv, fv, sv, lb, sem,
):
    y, z, x, c = here()
    slot = (y * 4 + z) * GROUP + member(x, c)
    ins = [
        pltpu.make_async_copy(a, b, sem.at[i])
        for i, (a, b) in enumerate(((l_hbm, lv), (r_hbm, rv), (f_hbm, fv), (s_hbm, sv), (m_hbm, mv)))
    ]
    for step in ins:
        step.start()
    lo_out[...] = lo_ref[...]
    ig_out[...] = ig_ref[...]
    acc = gsum_ref[...]
    first = BETA_ONE * gf_ref[...] + (1.0 - BETA_ONE) * acc
    second = BETA_TWO * gs_ref[...] + (1.0 - BETA_TWO) * acc * acc
    nf_ref[...] = first
    ns_ref[...] = second
    u = first / (1.0 - BETA_ONE**STEP) / (jnp.sqrt(second / (1.0 - BETA_TWO**STEP)) + ADAM_EPS)
    ng_ref[...] = gain_ref[...] - GAIN_RATE * u
    owned = lax.fori_loop(0, ATT + 3 * FFT, lambda t, a: a + (own_ref[t] == slot).astype(jnp.int32), 0) > 0
    ins[0].wait()
    lb[...] = lv[...].astype(BF)
    rot = nn(g_ref[...].reshape(HD, D), lb[...])
    ins[1].wait()
    right = rv[...].astype(BF)
    rot = nn(rot.T.astype(BF), right)
    ins[2].wait()
    ins[3].wait()
    first = BETA_ONE * fv[...] + (1.0 - BETA_ONE) * rot
    second = BETA_TWO * sv[...] + (1.0 - BETA_TWO) * rot * rot
    u = first / (1.0 - BETA_ONE**STEP) / (jnp.sqrt(second / (1.0 - BETA_TWO**STEP)) + ADAM_EPS)
    fv[...] = jnp.where(owned, first, fv[...])
    sv[...] = jnp.where(owned, second, sv[...])
    outs = [pltpu.make_async_copy(fv, fo_hbm, sem.at[5]), pltpu.make_async_copy(sv, so_hbm, sem.at[6])]
    for step in outs:
        step.start()
    back = nn(lb[...], nt(u.astype(BF), right).astype(BF))
    ins[4].wait()
    w = mv[...]
    mv[...] = jnp.where(owned, w - RATE * (back + DECAY * w), w)
    outs.append(pltpu.make_async_copy(mv, mo_hbm, sem.at[7]))
    outs[2].start()
    for step in outs:
        step.wait()


def run_step(owners, grad, gsum, gains, gain_first, gain_second, lo, ig, left, right, master, first, second):
    f = jax.ShapeDtypeStruct
    vm = pltpu.VMEM
    tile = f((D, HD), F32)
    row = f((40, 128), F32)
    return pl.pallas_call(
        step_body,
        out_shape=(tile, tile, tile, row, row, row, f((TOK, D), BF), f((TOK, D), F32)),
        in_specs=[pl.BlockSpec(memory_space=pltpu.SMEM)] + [INV] * 7 + [ANY] * 5,
        out_specs=(ANY, ANY, ANY, INV, INV, INV, INV, INV),
        scratch_shapes=[
            vm((D, D), F32), vm((HD, HD), F32), vm((D, HD), F32), vm((D, HD), F32), vm((D, HD), F32), vm((D, D), BF),
            DMA((8,)),
        ],
        compiler_params=pltpu.CompilerParams(vmem_limit_bytes=VMEM_LIMIT),
    )(owners, grad, gsum, gains, gain_first, gain_second, lo, ig, left, right, master, first, second)


def local(
    inputs,
    out_grad,
    doc_ids,
    owners,
    masters,
    first_old,
    second_old,
    left_basis,
    right_basis,
    gains,
    gain_first,
    gain_second,
):
    x = inputs[0]
    row = gains.reshape(1, 5120)
    lo, ig, gsum, grad, _ = run_layer(doc_ids, owners, masters[0], x, out_grad[0], row, 1)
    square = [a.reshape(40, 128) for a in (gains, gain_first, gain_second)]
    new_masters, new_first, new_second, new_gains, new_gain_first, new_gain_second, layer_out, input_grad = run_step(
        owners, grad, gsum, *square, lo, ig, left_basis[0], right_basis[0], masters[0], first_old[0], second_old[0]
    )
    return (
        layer_out[None],
        input_grad[None],
        new_masters[None],
        new_first[None],
        new_second[None],
        new_gains.reshape(5120),
        new_gain_first.reshape(5120),
        new_gain_second.reshape(5120),
    )


def solution(mesh):
    wide = Mesh(mesh.devices.reshape(4, 4, 2, 2, 2), AXES)
    tokens = P("xl", ("y", "z", "xh", "core"), None)
    held = P(AXES, None, None)
    return jax.shard_map(
        local,
        mesh=wide,
        in_specs=(tokens, tokens, P("xl", None), P(), held, held, held, held, held, P(), P(), P()),
        out_specs=(tokens, tokens, held, held, held, P(), P(), P()),
        check_vma=False,
    )
```

```python
import functools

import jax
import jax.numpy as jnp
from jax import lax
from jax.experimental import pallas as pl
from jax.experimental.pallas import tpu as pltpu
from jax.sharding import Mesh
from jax.sharding import PartitionSpec as P

FF = 6912
HEADS = 4
WINDOW = 512
BLK = 64
STEP = 10
D = 1152
HD = 256
TOK = 128
GROUP = 8
SLICE = HD // GROUP
ATT = 2 * HEADS + 2
FFT = FF // HD

NORM_EPS = 1e-06
THETA = 10000.0
BETA_ONE = 0.5
BETA_TWO = 0.5
RATE = 0.02
GAIN_RATE = 0.4
DECAY = 0.01
ADAM_EPS = 1e-08

MESH = pl.DeviceIdType.MESH
AXES = ("y", "z", "xh", "core", "xl")
VMEM_LIMIT = 63 * 1024 * 1024
BF = jnp.bfloat16
F32 = jnp.float32


def here():
    y, z, xh, c, xl = [lax.axis_index(a) for a in AXES]
    return y, z, xh * 2 + xl, c


def place(y, z, x, c):
    return (y, z, x // 2, c, lax.rem(x, 2))


def member(x, c):
    return (x // 2) * 4 + c * 2 + lax.rem(x, 2)


def turn(a, d):
    return lax.rem(a + d, 4)


def remote(src, dst, send, recv, where):
    return pltpu.make_async_remote_copy(src, dst, send, recv, device_id=where, device_id_type=MESH)


def params(cid):
    return pltpu.CompilerParams(
        collective_id=cid, has_side_effects=True, vmem_limit_bytes=VMEM_LIMIT
    )


ANY = pl.BlockSpec(memory_space=pl.ANY)
INV = pl.BlockSpec(memory_space=pltpu.VMEM)
DMA = pltpu.SemaphoreType.DMA


def seq_place(s):
    return (s // 16, lax.rem(s // 4, 4), lax.rem(s // 2, 2), lax.rem(s, 2), lax.axis_index("xl"))


def seq_index():
    y, z, xh, c, xl = [lax.axis_index(a) for a in AXES]
    return ((y * 4 + z) * 2 + xh) * 2 + c


def norm_of(v, g):
    return v * lax.rsqrt(jnp.mean(v * v, axis=-1, keepdims=True) + NORM_EPS) * g


def norm_back(v, g, w):
    r = lax.rsqrt(jnp.mean(v * v, axis=-1, keepdims=True) + NORM_EPS)
    u = w * g
    dg = jnp.sum(w * (v * r), axis=0, keepdims=True)
    dv = r * u - v * (r * r * r * jnp.mean(u * v, axis=-1, keepdims=True))
    return dv, dg


def column(g_ref, i):
    row = g_ref[:, 4 * D + i * HD : 4 * D + (i + 1) * HD]
    return jnp.broadcast_to(row, (128, HD)).T[:, 0:1]


def rope_norm(v, g, cos, sin):
    n = v * lax.rsqrt(jnp.mean(v * v, axis=0, keepdims=True) + NORM_EPS) * g
    a, b = n[: HD // 2], n[HD // 2 :]
    return jnp.concatenate([a * cos - b * sin, b * cos + a * sin], axis=0)


def gelu_parts(g):
    k, a = 0.7978845608028654, 0.044715
    sq = g * g
    th = jnp.tanh(k * g * (1.0 + a * sq))
    half = 0.5 * (1.0 + th)
    slope = half + 0.5 * g * (1.0 - th * th) * (k * (1.0 + 3.0 * a * sq))
    return g * half, slope


def nn(a, b):
    return jnp.dot(a, b, preferred_element_type=F32)


def nt(a, b):
    return lax.dot_general(a, b, (((1,), (1,)), ((), ())), preferred_element_type=F32)


def rope_norm_back(v, g, cos, sin, w):
    r = lax.rsqrt(jnp.mean(v * v, axis=0, keepdims=True) + NORM_EPS)
    a, b = w[: HD // 2], w[HD // 2 :]
    dn = jnp.concatenate([a * cos + b * sin, b * cos - a * sin], axis=0)
    dg = jnp.sum(dn * (v * r), axis=1, keepdims=True)
    u = dn * g
    dv = r * u - v * (r * r * r * jnp.mean(u * v, axis=0, keepdims=True))
    return dv, dg


def rows_add(dst, srcs, n):
    def step(i, carry):
        t = dst[i].astype(F32)
        for s in srcs:
            t = t + s[i].astype(F32)
        dst[i] = t.astype(BF)
        return carry

    lax.fori_loop(0, n, step, 0)


ORDER = (0, 3, 1, 2)
JS = (2, 1, 3, 0)
FFW = FFT * SLICE
ROWS = TOK // SLICE


def layer_body(
    doc_ref, own_ref, m_ref, x_ref, y_ref, g_ref,
    lo_ref, ig_ref, gsum_ref, grad_ref, xa_hbm,
    tile, grp, tile_of, tile_ref, wall, wf, xf, dd, dap_all, ab, bb, sbuf, near, far, t1, t2, u1, u2, fin,
    wo, ptl, qt, kb, vt, raw, oto, osl, sq, watt, dst, dot_, hsend, hrec, dqk, drec, dsl,
    da, a1, amid, a2, att, gl, gin, gmid, gin2,
    load_sem, ts, tr, n1s, n1r, n2s, n2r, n3s, n3r, n4s, n4r, xxs, xxr, xcs, xcr, c1s, c1r, c2s, c2r, c3s, c3r, c4s, c4r,
    as_, ar, wxs, wxr, wcs, wcr, hs, hr, os_, or_, fxs, fxr, fcs, fcr, bxs, bxr, bcs, bcr,
    ss, sr, rs_, rr, axs, axr, acs, acr, hbs, hbr, qs, qr, g1s, g1r, g2s, g2r, k1s, k1r, k2s, k2r,
    fs, fr, gas, gar, gbs, gbr,
):
    y, z, x, c = here()
    me = x * 2 + c
    twin = place(y, z, x, 1 - c)
    s = seq_index()
    chips = {d: turn(x, d) for d in range(4)}
    peers = {d: place(y, z, chips[d], c) for d in (1, 2, 3)}
    others = [(d, cc) for d in (1, 2, 3) for cc in range(2)]
    field = [(o - 1, place(turn(y, o // 4), turn(z, o % 4), x, c)) for o in range(1, 16)]
    mine_k = y * 4 + z
    at = (y, z)
    ring = (
        {d: place(turn(y, d), z, x, c) for d in (1, 2, 3)},
        {d: place(y, turn(z, d), x, c) for d in (1, 2, 3)},
    )
    partners = (
        [place(y, z, chips[d], cc) for d, cc in others]
        + [twin]
        + [seq_place(lax.rem(s + 64 + d, 64)) for d in (-4, -3, -2, -1, 1, 2, 3, 4)]
        + [f[1] for f in field]
    )
    sem = pltpu.get_barrier_semaphore()
    for p in partners:
        pl.semaphore_signal(sem, inc=1, device_id=p, device_id_type=MESH)
    for h in range(2):
        tile[4 * h : 4 * h + 4] = m_ref[:, h * 128 : (h + 1) * 128].T.astype(BF).reshape(4, SLICE, D)
    pl.semaphore_wait(sem, len(partners))
    sent = []

    def go(step):
        step.start()
        sent.append(step)
        return step

    def settle(steps):
        for step in steps:
            step.wait_send()
        sent[:] = [a for a in sent if not any(a is b for b in steps)]

    mm = member(x, c)
    base = mine_k * GROUP
    for d, cc in [(2, 0), (2, 1), (1, 0), (1, 1), (3, 0), (3, 1)]:
        go(remote(tile.at[chips[d] * 2 + cc], grp.at[mm], ts.at[d, cc], tr.at[d, c], place(y, z, chips[d], cc)))
    go(remote(tile.at[x * 2 + 1 - c], grp.at[mm], ts.at[0, 0], tr.at[0, c], twin))
    grp[mm] = tile[me]
    dd[x, c] = norm_of(x_ref[...].astype(F32), g_ref[:, 0:D]).astype(BF)
    mine = dd.at[x, c]
    x_far = {d: go(remote(mine, mine, xxs.at[d - 1], xxr.at[d - 1], peers[d])) for d in (1, 3, 2)}
    x_near = {0: go(remote(mine, mine, xcs.at[0], xcr.at[0], twin))}
    pos = s * TOK + lax.broadcasted_iota(jnp.int32, (HD // 2, TOK), 1)
    freq = lax.broadcasted_iota(jnp.int32, (HD // 2, TOK), 0).astype(F32)
    angle = pos.astype(F32) * jnp.exp(-jnp.log(THETA) * freq * 2.0 / HD)
    cos, sin = jnp.cos(angle), jnp.sin(angle)
    lane = lax.broadcasted_iota(jnp.int32, (1, 128), 1)
    tile_of[...] = lax.fori_loop(
        0,
        ATT + 3 * FFT,
        lambda t, acc: jnp.where(lane == own_ref[t], t, acc),
        jnp.zeros((1, 128), jnp.int32),
    )
    to_scalars = pltpu.make_async_copy(tile_of, tile_ref, load_sem.at[0])
    to_scalars.start()
    for d, cc in others:
        remote(tile.at[0], grp.at[mm], ts.at[d, cc], tr.at[d, cc], twin).wait_recv()
    remote(tile.at[0], grp.at[mm], ts.at[0, 0], tr.at[0, 1 - c], twin).wait_recv()
    def halves(h):
        return slice(h * 16, h * 16 + 16)

    def lay(t, v):
        for k in range(9):
            da[t * 9 + k] = v[:, k * 128 : (k + 1) * 128]

    def taken(t):
        return jnp.concatenate([att[t * 9 + k] for k in range(9)], axis=1)

    def set_out(ph):
        steps = []
        for d in (2, 1, 3):
            for h in (0, 1):
                src = da.at[pl.ds(24 * turn(at[h], d), 24), halves(h)]
                steps.append(go(remote(src, a1.at[ph, h, d - 1], c1s.at[ph, h, d - 1], c1r.at[ph, h, d - 1], ring[h][d])))
        return steps

    def add_up(ph, first):
        for step in first:
            step.wait_recv()
        for h in (0, 1):
            tot = da[pl.ds(24 * at[h], 24), halves(h)].astype(F32)
            for i in range(3):
                tot = tot + a1[ph, h, i].astype(F32)
            amid[h] = tot.astype(BF)
        steps = []
        for d in (2, 1, 3):
            for h in (0, 1):
                src = amid.at[h, pl.ds(6 * turn(at[1 - h], d), 6)]
                dst = a2.at[ph, h, d - 1]
                steps.append(go(remote(src, dst, c2s.at[ph, h, d - 1], c2r.at[ph, h, d - 1], ring[1 - h][d])))
        return steps

    def give(ph, second):
        for step in second:
            step.wait_recv()
        steps = []
        for h in (0, 1):
            tot = amid[h, pl.ds(6 * at[1 - h], 6)].astype(F32)
            for i in range(3):
                tot = tot + a2[ph, h, i].astype(F32)
            att[pl.ds(24 * at[h] + 6 * at[1 - h], 6), halves(h)] = tot.astype(BF)
            src = att.at[pl.ds(24 * at[h] + 6 * at[1 - h], 6), halves(h)]
            for d in (2, 1, 3):
                steps.append(go(remote(src, src, c3s.at[ph, h, d - 1], c3r.at[ph, h, d - 1], ring[1 - h][d])))
        return steps

    def give_on(ph, third):
        for step in third:
            step.wait_recv()
        steps = []
        for h in (0, 1):
            src = att.at[pl.ds(24 * at[h], 24), halves(h)]
            for d in (2, 1, 3):
                steps.append(go(remote(src, src, c4s.at[ph, h, d - 1], c4r.at[ph, h, d - 1], ring[h][d])))
        return steps

    for t in range(ATT):
        rel = own_ref[t] - base
        v = grp[jnp.clip(rel, 0, GROUP - 1)]
        lay(t, jnp.where((rel >= 0) & (rel < GROUP), v, jnp.zeros_like(v)))

    routed = set_out(0)
    wall[pl.ds(base, GROUP)] = grp[...]

    w_at = (z, y)
    f_at = {h: {d: turn(w_at[h], d) for d in range(4)} for h in (0, 1)}
    s_at = {h: {d: turn(w_at[1 - h], d) for d in range(4)} for h in (0, 1)}
    ways = ((0, 1, 3), (1, 3, 1))

    def block(h, first, second):
        yy, zz = (second, first) if h == 0 else (first, second)
        return wall.at[pl.ds(((yy * 4 + zz) * 2 + h) * 4, 4)]

    one, two, far1 = {}, {}, {}
    for h in (0, 1):
        for n, up, _ in ways:
            src = grp.at[4 * h : 4 * h + 4]
            one[h, n] = go(remote(src, block(h, f_at[h][0], s_at[h][0]), n1s.at[h, n], n1r.at[h, n], ring[1 - h][up]))

    def second(k):
        for h in (0, 1):
            b = block(h, f_at[h][k], s_at[h][0])
            src = b if k else grp.at[4 * h : 4 * h + 4]
            for n, up, _ in ways:
                two[h, k, n] = go(remote(src, b, n2s.at[h, k, n], n2r.at[h, k, n], ring[h][up]))

    def onward(k):
        for h in (0, 1):
            for n, up, down in ways:
                two[h, k, n].wait_recv()
                b = block(h, f_at[h][k], s_at[h][down]).at[2 * n : 2 * n + 2]
                last.append(go(remote(b, b, n4s.at[h, k, n], n4r.at[h, k, n], ring[h][up])))

    last = []
    for d in (1, 3, 2):
        x_far[d].wait_recv()
        src = dd.at[chips[4 - d], c]
        x_near[d] = go(remote(src, src, xcs.at[d], xcr.at[d], twin))
    added = add_up(0, routed)
    second(0)
    for h in (0, 1):
        for n, up, down in ways:
            one[h, n].wait_recv()
            b = block(h, f_at[h][down], s_at[h][0]).at[2 * n : 2 * n + 2]
            far1[h, n] = go(remote(b, b, n3s.at[h, n], n3r.at[h, n], ring[1 - h][up]))
    given = give(0, added)
    for step in x_near.values():
        step.wait_recv()
    save_x = pltpu.make_async_copy(dd, xa_hbm, load_sem.at[1])
    save_x.start()
    second(3)
    given_on = give_on(0, given)
    second(1)
    for step in given_on:
        step.wait_recv()

    for t in range(HEADS + 2):
        watt[t * SLICE : (t + 1) * SLICE] = taken(t)
    for h in range(HEADS):
        wo[h, me] = taken(HEADS + 2 + h)
    for d in (2, 1, 3, 0):
        part = nt(watt[...], dd[chips[d]].reshape(2 * TOK, D)).astype(BF)
        for cc in range(2):
            sq[d, cc] = part[:, cc * TOK : (cc + 1) * TOK].reshape(HEADS + 2, SLICE, TOK)
        if d:
            for cc in range(2):
                go(remote(sq.at[d, cc], raw.at[:, me], as_.at[d, cc], ar.at[d, c], place(y, z, chips[d], cc)))
    go(remote(sq.at[0, 1 - c], raw.at[:, me], as_.at[0, 0], ar.at[0, c], twin))
    raw[:, me] = sq[0, c]
    mine = wo.at[:, me]
    w_far = {d: go(remote(mine, mine, wxs.at[d - 1], wxr.at[d - 1], peers[d])) for d in (1, 3)}
    w_near = {0: go(remote(mine, mine, wcs.at[0], wcr.at[0], twin))}
    onward(0)
    for d, cc in others:
        remote(sq.at[d, cc], raw.at[:, me], as_.at[d, cc], ar.at[d, cc], twin).wait_recv()
    remote(sq.at[0, 0], raw.at[:, me], as_.at[0, 0], ar.at[0, 1 - c], twin).wait_recv()

    gain_q, gain_k = column(g_ref, 0), column(g_ref, 1)
    kt = rope_norm(raw[HEADS].reshape(HD, TOK).astype(F32), gain_k, cos, sin)
    kb[4] = kt.T.astype(BF)
    vt[:, 4 * TOK :] = raw[HEADS + 1].reshape(HD, TOK)
    halo = []
    for d in (4, 3, 2, 1):
        to = seq_place(lax.rem(s + d, 64))
        lanes = slice((4 - d) * TOK, (5 - d) * TOK)
        halo.append(go(remote(kb.at[4], kb.at[4 - d], hs.at[0, d - 1], hr.at[0, d - 1], to)))
        halo.append(go(remote(vt.at[:, 4 * TOK :], vt.at[:, lanes], hs.at[1, d - 1], hr.at[1, d - 1], to)))
    w_far[2] = go(remote(mine, mine, wxs.at[1], wxr.at[1], peers[2]))
    for step in far1.values():
        step.wait_recv()
    second(2)
    onward(3)
    onward(1)
    for h in range(HEADS):
        q = rope_norm(raw[h].reshape(HD, TOK).astype(F32), gain_q, cos, sin)
        qt[:, h * TOK : (h + 1) * TOK] = q.astype(BF)
    row = lax.broadcasted_iota(jnp.int32, (WINDOW + TOK, TOK), 0)
    col = lax.broadcasted_iota(jnp.int32, (WINDOW + TOK, TOK), 1)
    seen = (row <= col + WINDOW) & (row > col) & (row >= WINDOW - s * TOK)
    half = lax.broadcasted_iota(jnp.int32, (BLK, TOK), 1) < BLK
    q_doc = jnp.where(half, doc_ref[0, 2 * s], doc_ref[0, 2 * s + 1])
    k_doc = jnp.concatenate(
        [jnp.full((BLK, TOK), doc_ref[0, jnp.maximum(2 * s - 8 + b, 0)], jnp.int32) for b in range(10)],
        axis=0,
    )
    seen = seen & (k_doc == jnp.concatenate([q_doc] * 10, axis=0))
    for step in halo:
        step.wait_recv()
    keys = kb[...].reshape(WINDOW + TOK, HD)
    for h in range(HEADS):
        lanes = slice(h * TOK, (h + 1) * TOK)
        sc = nn(keys, qt[:, lanes]) * (HD**-0.5)
        sc = jnp.where(seen, sc, -1e30)
        ex = jnp.exp(sc - jnp.max(sc, axis=0, keepdims=True))
        ptl[:, lanes] = (ex / jnp.sum(ex, axis=0, keepdims=True)).astype(BF)
    ot = nn(vt[...], ptl[...])
    oto[...] = ot.astype(BF)
    for d, cc in others:
        rows = pl.ds(pl.multiple_of((chips[d] * 2 + cc) * SLICE, SLICE), SLICE)
        go(remote(oto.at[rows], osl.at[me], os_.at[d, cc], or_.at[d, c], place(y, z, chips[d], cc)))
    rows = pl.ds(pl.multiple_of((x * 2 + 1 - c) * SLICE, SLICE), SLICE)
    go(remote(oto.at[rows], osl.at[me], os_.at[0, 0], or_.at[0, c], twin))
    osl[me] = oto[pl.ds(pl.multiple_of(me * SLICE, SLICE), SLICE)]

    onward(2)
    for d in (1, 3, 2):
        w_far[d].wait_recv()
        src = wo.at[:, chips[4 - d] * 2 + c]
        w_near[d] = go(remote(src, src, wcs.at[d], wcr.at[d], twin))
    for step in w_near.values():
        step.wait_recv()
    ap = jnp.zeros((TOK, D), F32)
    for h in range(HEADS):
        o = ot[:, h * TOK : (h + 1) * TOK].T.astype(BF)
        ap = ap + nn(o, wo[h].reshape(HD, D))
    act = x_ref[...].astype(F32)
    r1 = act + norm_of(ap, g_ref[:, 1 * D : 2 * D])
    xf[x, c] = norm_of(r1, g_ref[:, 2 * D : 3 * D]).astype(BF)

    def gather_start(buf, xs, xr, cs, cr, first=(1, 3, 2)):
        own = buf.at[x, c]
        near_ = {0: go(remote(own, own, cs.at[0], cr.at[0], twin))}
        sends = {d: go(remote(own, own, xs.at[d - 1], xr.at[d - 1], peers[d])) for d in first}
        return sends, near_

    def gather_wait(buf, e, sends, near_, cs, cr):
        if e:
            d = 4 - e
            sends[d].wait_recv()
            src = buf.at[chips[e], c]
            near_[d] = go(remote(src, src, cs.at[d], cr.at[d], twin))
            near_[d].wait_recv()
        else:
            near_[0].wait_recv()

    def pbuf(ph, e, cc):
        return (wall if ph < 2 else wf).at[pl.ds((2 * e + cc) * ROWS, ROWS)]

    def sum_swap(ph, n, e):
        return go(remote(pbuf(ph, e, 1 - c), near.at[n, e], ss.at[ph, e], sr.at[ph, e], twin))

    def sum_send(ph, n, e, swap):
        swap.wait_recv()
        both = pbuf(ph, e, c)[...].astype(F32) + near[n, e].astype(F32)
        if not e:
            return None, both
        sbuf[e - 1] = both.astype(BF)
        return go(remote(sbuf.at[e - 1], far.at[n, e - 1], rs_.at[ph, e - 1], rr.at[ph, e - 1], peers[e])), None

    def finish(n, swaps, outs, ph, total=None):
        if total is None:
            _, total = sum_send(ph, n, 0, swaps[0])
            settle(list(swaps.values()))
        for step in outs:
            step.wait_recv()
        total = ((total + far[n, 0].astype(F32)) + far[n, 1].astype(F32)) + far[n, 2].astype(F32)
        settle(outs)
        return total.reshape(TOK, D)

    def pipeline(ph, order, ready, block):
        swaps, outs = {}, []
        for n, e in enumerate(order):
            ready(e)
            part = block(e).astype(BF).reshape(2, ROWS, SLICE, D)
            for cc in range(2):
                pbuf(ph, e, cc)[...] = part[cc]
            swaps[e] = sum_swap(ph, ph % 2, e)
            if n and order[n - 1]:
                outs.append(sum_send(ph, ph % 2, order[n - 1], swaps[order[n - 1]])[0])
        if order[3]:
            outs.append(sum_send(ph, ph % 2, order[3], swaps[order[3]])[0])
        return swaps, outs, ph

    def put(k, e, v):
        cols = pl.ds(pl.multiple_of(chips[e] * 2 * TOK, 2 * TOK), 2 * TOK)
        wall[32 + k * FFT : 32 + (k + 1) * FFT, :, cols] = v.T.reshape(FFT, SLICE, 2 * TOK)

    def tiles(k):
        return wf[k * FFT : (k + 1) * FFT].reshape(FFW, D)

    def forward(e):
        v = xf[chips[e]].reshape(2 * TOK, D)
        g = nt(v, tiles(0))
        u = nt(v, tiles(1))
        h, slope = gelu_parts(g)
        ab[e] = (u * slope).astype(BF)
        bb[e] = h.astype(BF)
        hid = (h * u).astype(BF)
        put(2, e, hid)
        return nn(hid, tiles(2))

    sends, near_ = gather_start(xf, fxs, fxr, fcs, fcr)
    for step in last:
        step.wait_recv()

    def pack(t, carry):
        wf[t] = wall[own_ref[ATT + t]]
        return carry

    lax.fori_loop(0, 3 * FFT, pack, 0)
    settle(list(two.values()) + list(far1.values()) + last + list(x_far.values()) + list(x_near.values()))
    save_x.wait()
    to_scalars.wait()
    settle(routed + added + given + given_on)
    state = pipeline(0, ORDER, lambda e: gather_wait(xf, e, sends, near_, fcs, fcr), forward)
    dn = finish(0, *state)
    lo_ref[...] = (r1 + norm_of(dn, g_ref[:, 3 * D : 4 * D])).astype(BF)
    cot = y_ref[...].astype(F32)
    ddn, d_fpost = norm_back(dn, g_ref[:, 3 * D : 4 * D], cot)
    dd[x, c] = ddn.astype(BF)

    def backward(e):
        v = dd[chips[e]].reshape(2 * TOK, D)
        dh = nt(v, tiles(2))
        dg = (dh * ab[e].astype(F32)).astype(BF)
        du = (dh * bb[e].astype(F32)).astype(BF)
        put(0, e, dg)
        put(1, e, du)
        return nn(dg, tiles(0)) + nn(du, tiles(1))

    sends_b, near_b = gather_start(dd, bxs, bxr, bcs, bcr)
    state = pipeline(1, ORDER, lambda e: gather_wait(dd, e, sends_b, near_b, bcs, bcr), backward)

    for k, rhs in enumerate((xf, xf, dd)):
        left = wall[32 + k * FFT : 32 + (k + 1) * FFT, :, 0 : GROUP * TOK].reshape(FFW, GROUP * TOK)
        for n in range(3):
            cols = slice(n * 384, (n + 1) * 384)
            g = nn(left, rhs[:, :, :, cols].reshape(GROUP * TOK, 384)).astype(BF)
            wf[k * FFT : (k + 1) * FFT, :, cols] = g.reshape(FFT, SLICE, 384)
    _, rest = sum_send(1, 1, 0, state[0][0])
    settle(list(state[0].values()))

    def fill(i, carry):
        wall[i] = wf[jnp.clip(tile_ref[0, i] - ATT, 0, 3 * FFT - 1)]
        return carry

    lax.fori_loop(0, 128, fill, 0)

    def part(h, first, second):
        yy, zz = (first, second) if h == 0 else (second, first)
        return wall.at[pl.ds(((yy * 4 + zz) * 2 + h) * 4, 4)]

    here1 = {h: {d: turn(at[h], d) for d in range(4)} for h in (0, 1)}
    here2 = {h: {d: turn(at[1 - h], d) for d in range(4)} for h in (0, 1)}
    s1 = {}
    for j in JS:
        for h in (0, 1):
            blk = part(h, here1[h][2], here2[h][j])
            s1[h, j, 0] = go(remote(blk.at[0:2], t1.at[h, j, 0], g1s.at[h, j, 0], g1r.at[h, j, 0], ring[h][1]))
            s1[h, j, 1] = go(remote(blk.at[2:4], t1.at[h, j, 1], g1s.at[h, j, 1], g1r.at[h, j, 1], ring[h][3]))

    dxf = finish(1, *state, rest)
    e1, d_fpre = norm_back(r1, g_ref[:, 2 * D : 3 * D], dxf)
    dr1 = cot + e1
    ig_ref[...] = dr1
    dap, d_apost = norm_back(ap, g_ref[:, 1 * D : 2 * D], dr1)
    dap_all[x, c] = dap.astype(BF)
    sends_a, near_a = gather_start(dap_all, axs, axr, acs, acr, (1, 3))

    dmix = nt(wo[...].reshape(HEADS * HD, D), dap.astype(BF)).astype(BF)
    for h in range(HEADS):
        dot_[:, h * TOK : (h + 1) * TOK] = dmix[h * HD : (h + 1) * HD]
    values = jnp.concatenate([vt[:, b * TOK : (b + 1) * TOK].T for b in range(5)], axis=0)
    for h in range(HEADS):
        lanes = slice(h * TOK, (h + 1) * TOK)
        pr = ptl[:, lanes].astype(F32)
        dp = nn(values, dot_[:, lanes])
        inner = jnp.sum(pr * dp, axis=0, keepdims=True)
        dst[:, lanes] = (pr * (dp - inner) * (HD**-0.5)).astype(BF)
    dk = nt(qt[...], dst[...])
    dv = nt(dot_[...], ptl[...])
    back = []
    for d in (4, 3, 2, 1):
        lanes = slice((4 - d) * TOK, (5 - d) * TOK)
        hsend[d - 1, 0] = dk[:, lanes].astype(BF)
        hsend[d - 1, 1] = dv[:, lanes].astype(BF)
        to = seq_place(lax.rem(s + 64 - d, 64))
        back.append(go(remote(hsend.at[d - 1], hrec.at[d - 1], hbs.at[d - 1], hbr.at[d - 1], to)))
    dk = dk[:, 4 * TOK :]
    dv = dv[:, 4 * TOK :]
    own = dap_all.at[x, c]
    sends_a[2] = go(remote(own, own, axs.at[1], axr.at[1], peers[2]))

    s2 = {}

    def pass_on(j):
        for h in (0, 1):
            s1[h, j, 0].wait_recv()
            blk = part(h, here1[h][1], here2[h][j])
            rows_add(blk.at[0:2], [t1.at[h, j, 0]], 2)
            s2[h, j, 0] = go(remote(blk, t2.at[h, j, 0], g2s.at[h, j, 0], g2r.at[h, j, 0], ring[h][1]))
            s1[h, j, 1].wait_recv()
            blk = part(h, here1[h][3], here2[h][j])
            rows_add(blk.at[2:4], [t1.at[h, j, 1]], 2)
            s2[h, j, 1] = go(remote(blk, t2.at[h, j, 1], g2s.at[h, j, 1], g2r.at[h, j, 1], ring[h][3]))

    pass_on(2)
    settle(list(sends.values()) + list(near_.values()))
    load_x = pltpu.make_async_copy(xa_hbm, xf, load_sem.at[2])
    load_x.start()
    keys_t = jnp.concatenate([kb[b].T for b in range(5)], axis=1)
    dgq = jnp.zeros((HD, 1), F32)
    for h in range(HEADS):
        dq = nn(keys_t, dst[:, h * TOK : (h + 1) * TOK])
        dq, dg = rope_norm_back(raw[h].reshape(HD, TOK).astype(F32), gain_q, cos, sin, dq)
        dqk[h] = dq.astype(BF).reshape(GROUP, SLICE, TOK)
        dgq = dgq + dg

    pass_on(1)
    for step in back:
        step.wait_recv()
    for d in range(4):
        dk = dk + hrec[d, 0].astype(F32)
        dv = dv + hrec[d, 1].astype(F32)
    dk, dgk = rope_norm_back(raw[HEADS].reshape(HD, TOK).astype(F32), gain_k, cos, sin, dk)
    dqk[HEADS] = dk.astype(BF).reshape(GROUP, SLICE, TOK)
    dqk[HEADS + 1] = dv.astype(BF).reshape(GROUP, SLICE, TOK)
    for d, cc in others:
        to = chips[d] * 2 + cc
        go(remote(dqk.at[:, to], drec.at[me], qs.at[d, cc], qr.at[d, c], place(y, z, chips[d], cc)))
    go(remote(dqk.at[:, x * 2 + 1 - c], drec.at[me], qs.at[0, 0], qr.at[0, c], twin))
    drec[me] = dqk[:, me]

    pass_on(3)
    for e in (0, 3, 1, 2):
        gather_wait(dap_all, e, sends_a, near_a, acs, acr)
    for d, cc in others:
        remote(oto.at[0:SLICE], osl.at[me], os_.at[d, cc], or_.at[d, cc], twin).wait_recv()
    remote(oto.at[0:SLICE], osl.at[me], os_.at[0, 0], or_.at[0, 1 - c], twin).wait_recv()
    for h in range(HEADS):
        for p in range(GROUP):
            dsl[h * SLICE : (h + 1) * SLICE, p * TOK : (p + 1) * TOK] = osl[p, :, h * TOK : (h + 1) * TOK]
    g = nn(dsl[0 : HEADS * SLICE], dap_all[...].reshape(GROUP * TOK, D)).astype(BF)
    for h in range(HEADS):
        lay(HEADS + 2 + h, g[h * SLICE : (h + 1) * SLICE])

    pass_on(0)
    for d, cc in others:
        remote(dqk.at[:, 0], drec.at[me], qs.at[d, cc], qr.at[d, cc], twin).wait_recv()
    remote(dqk.at[:, 0], drec.at[me], qs.at[0, 0], qr.at[0, 1 - c], twin).wait_recv()
    for p in range(GROUP):
        dsl[:, p * TOK : (p + 1) * TOK] = drec[p].reshape((HEADS + 2) * SLICE, TOK)
    load_x.wait()
    g = nn(dsl[...], xf[...].reshape(GROUP * TOK, D)).astype(BF)
    for t in range(HEADS + 2):
        lay(t, g[t * SLICE : (t + 1) * SLICE])

    routed = set_out(1)

    def inputs_back(e):
        pair = [
            nn(drec[chips[e] * 2 + cc].reshape((HEADS + 2) * SLICE, TOK).T, watt[...]) for cc in range(2)
        ]
        return jnp.concatenate(pair, axis=0)

    state = pipeline(2, JS, lambda e: None, inputs_back)

    added = add_up(1, routed)

    def close(j):
        for h in (0, 1):
            s2[h, j, 0].wait_recv()
            s2[h, j, 1].wait_recv()
            rows_add(part(h, here1[h][0], here2[h][j]), [t2.at[h, j, 0], t2.at[h, j, 1]], 4)

    e1, e2 = {}, {}
    close(2)
    for h in (0, 1):
        blk = part(h, here1[h][0], here2[h][2])
        e1[h, 0] = go(remote(blk.at[0:2], u1.at[h, 0], k1s.at[h, 0], k1r.at[h, 0], ring[1 - h][1]))
        e1[h, 1] = go(remote(blk.at[2:4], u1.at[h, 1], k1s.at[h, 1], k1r.at[h, 1], ring[1 - h][3]))

    close(1)
    close(3)
    given = give(1, added)
    for n, j in ((0, 1), (1, 3)):
        for h in (0, 1):
            blk = part(h, here1[h][0], here2[h][j])
            e1[h, n].wait_recv()
            rows_add(blk.at[2 * n : 2 * n + 2], [u1.at[h, n]], 2)
            e2[h, n] = go(remote(blk, u2.at[h, n], k2s.at[h, n], k2r.at[h, n], ring[1 - h][j]))

    given_on = give_on(1, given)
    dxa = finish(0, *state)
    ein, d_apre = norm_back(x_ref[...].astype(F32), g_ref[:, 0 * D : 1 * D], dxa)
    ig_ref[...] = ig_ref[...] + ein
    for k in range(9):
        lanes = slice(k * 128, (k + 1) * 128)
        for m, dg in enumerate((d_apre, d_apost, d_fpre, d_fpost)):
            gl[9 * m + k : 9 * m + k + 1] = dg[:, lanes]
    for m, dg in enumerate((dgq, dgk)):
        flat = jnp.broadcast_to(dg, (HD, 128)).T
        for k in range(2):
            gl[36 + 2 * m + k : 37 + 2 * m + k] = flat[0:1, k * 128 : (k + 1) * 128]
    for d, cc in others:
        go(remote(gl, gin.at[x, c], gas.at[d, cc], gar.at[d, c], place(y, z, chips[d], cc)))
    go(remote(gl, gin.at[x, c], gas.at[0, 0], gar.at[0, c], twin))
    gin[x, c] = gl[...]

    for d, cc in others:
        remote(gl, gin.at[x, c], gas.at[d, cc], gar.at[d, cc], twin).wait_recv()
    remote(gl, gin.at[x, c], gas.at[0, 0], gar.at[0, 1 - c], twin).wait_recv()
    acc = gin[0, 0]
    for p in range(1, GROUP):
        acc = acc + gin[p // 2, p % 2]
    gmid[...] = acc
    gin2[mine_k] = acc
    all_gains = [go(remote(gmid, gin2.at[mine_k], gbs.at[o], gbr.at[o], to)) for o, to in field]
    close(0)

    for step in given_on:
        step.wait_recv()
    for h in (0, 1):
        e2[h, 0].wait_recv()
        e2[h, 1].wait_recv()
        blk = part(h, here1[h][0], here2[h][0])
        rows_add(blk, [u2.at[h, 0], u2.at[h, 1]], 4)
    for q in range(GROUP):
        t = tile_ref[0, base + q]
        low = taken(jnp.clip(t, 0, ATT - 1))
        fin[q] = jnp.where(t < ATT, low, wall[base + q])
    for d, cc in others:
        src = fin.at[member(chips[d], cc)]
        go(remote(src, grad_ref.at[me], fs.at[d, cc], fr.at[d, c], place(y, z, chips[d], cc)))
    go(remote(fin.at[member(x, 1 - c)], grad_ref.at[me], fs.at[0, 0], fr.at[0, c], twin))
    grad_ref[me] = fin[member(x, c)]
    for step in all_gains:
        step.wait_recv()
    acc = gin2[0]
    for k in range(1, 16):
        acc = acc + gin2[k]
    gsum_ref[...] = acc
    for d, cc in others:
        remote(fin.at[0], grad_ref.at[me], fs.at[d, cc], fr.at[d, cc], twin).wait_recv()
    remote(fin.at[0], grad_ref.at[me], fs.at[0, 0], fr.at[0, 1 - c], twin).wait_recv()
    for step in sent:
        step.wait_send()


def run_layer(doc, owners, master, x, y, gains, cid):
    f = jax.ShapeDtypeStruct
    smem = pl.BlockSpec(memory_space=pltpu.SMEM)
    vm = pltpu.VMEM
    blocks = (TOK // SLICE, SLICE, D)
    lanes = HEADS * TOK
    seen = WINDOW + TOK
    qkv = HEADS + 2
    return pl.pallas_call(
        layer_body,
        out_shape=(
            f((TOK, D), BF),
            f((TOK, D), F32),
            f((40, 128), F32),
            f((GROUP, SLICE, D), BF),
            f((4, 2, TOK, D), BF),
        ),
        in_specs=[smem, smem, INV, INV, INV, INV],
        out_specs=(INV, INV, INV, INV, ANY),
        scratch_shapes=[
            vm((GROUP, SLICE, D), BF),
            vm((GROUP, SLICE, D), BF),
            vm((1, 128), jnp.int32),
            pltpu.SMEM((1, 128), jnp.int32),
            vm((128, SLICE, D), BF),
            vm((3 * FFT, SLICE, D), BF),
            vm((4, 2, TOK, D), BF),
            vm((4, 2, TOK, D), BF),
            vm((4, 2, TOK, D), BF),
            vm((4, 2 * TOK, FFW), BF),
            vm((4, 2 * TOK, FFW), BF),
            vm((3,) + blocks, BF),
            vm((2, 4) + blocks, BF),
            vm((2, 3) + blocks, BF),
            vm((2, 4, 2, 2, SLICE, D), BF),
            vm((2, 4, 2, 4, SLICE, D), BF),
            vm((2, 2, 2, SLICE, D), BF),
            vm((2, 2, 4, SLICE, D), BF),
            vm((GROUP, SLICE, D), BF),
            vm((HEADS, GROUP, SLICE, D), BF),
            vm((seen, lanes), BF),
            vm((HD, lanes), BF),
            vm((5, TOK, HD), BF),
            vm((HD, seen), BF),
            vm((qkv, GROUP, SLICE, TOK), BF),
            vm((HD, lanes), BF),
            vm((GROUP, SLICE, lanes), BF),
            vm((4, 2, qkv, SLICE, TOK), BF),
            vm((qkv * SLICE, D), BF),
            vm((seen, lanes), BF),
            vm((HD, lanes), BF),
            vm((4, 2, HD, TOK), BF),
            vm((4, 2, HD, TOK), BF),
            vm((qkv, GROUP, SLICE, TOK), BF),
            vm((GROUP, qkv, SLICE, TOK), BF),
            vm((qkv * SLICE, GROUP * TOK), BF),
            vm((96, SLICE, 128), BF),
            vm((2, 2, 3, 24, 16, 128), BF),
            vm((2, 24, 16, 128), BF),
            vm((2, 2, 3, 6, 16, 128), BF),
            vm((96, SLICE, 128), BF),
            vm((40, 128), F32),
            vm((4, 2, 40, 128), F32),
            vm((40, 128), F32),
            vm((16, 40, 128), F32),
            DMA((3,)),
            DMA((4, 2)), DMA((4, 2)),
            DMA((2, 2)), DMA((2, 2)), DMA((2, 4, 2)), DMA((2, 4, 2)),
            DMA((2, 2)), DMA((2, 2)), DMA((2, 4, 2)), DMA((2, 4, 2)),
            DMA((3,)), DMA((3,)), DMA((4,)), DMA((4,)),
            DMA((2, 2, 3)), DMA((2, 2, 3)), DMA((2, 2, 3)), DMA((2, 2, 3)),
            DMA((2, 2, 3)), DMA((2, 2, 3)), DMA((2, 2, 3)), DMA((2, 2, 3)),
            DMA((4, 2)), DMA((4, 2)),
            DMA((3,)), DMA((3,)), DMA((4,)), DMA((4,)),
            DMA((2, 4)), DMA((2, 4)),
            DMA((4, 2)), DMA((4, 2)),
            DMA((3,)), DMA((3,)), DMA((4,)), DMA((4,)),
            DMA((3,)), DMA((3,)), DMA((4,)), DMA((4,)),
            DMA((3, 4)), DMA((3, 4)), DMA((3, 3)), DMA((3, 3)),
            DMA((3,)), DMA((3,)), DMA((4,)), DMA((4,)),
            DMA((4,)), DMA((4,)),
            DMA((4, 2)), DMA((4, 2)),
            DMA((2, 4, 2)), DMA((2, 4, 2)), DMA((2, 4, 2)), DMA((2, 4, 2)),
            DMA((2, 2)), DMA((2, 2)), DMA((2, 2)), DMA((2, 2)),
            DMA((4, 2)), DMA((4, 2)),
            DMA((4, 2)), DMA((4, 2)),
            DMA((15,)), DMA((15,)),
        ],
        compiler_params=params(cid),
    )(doc, owners, master, x, y, gains)


def step_body(
    own_ref, g_ref, gsum_ref, gain_ref, gf_ref, gs_ref, lo_ref, ig_ref, l_hbm, r_hbm, m_hbm, f_hbm, s_hbm,
    mo_hbm, fo_hbm, so_hbm, ng_ref, nf_ref, ns_ref, lo_out, ig_out, lv, rv, mv, fv, sv, lb, sem,
):
    y, z, x, c = here()
    slot = (y * 4 + z) * GROUP + member(x, c)
    third = D // 3
    cuts = [slice(k * third, (k + 1) * third) for k in range(3)]
    pieces = [pltpu.make_async_copy(l_hbm.at[r], lv.at[r], sem.at[8 + k]) for k, r in enumerate(cuts)]
    ins = [
        pltpu.make_async_copy(a, b, sem.at[i])
        for i, (a, b) in enumerate(((r_hbm, rv), (f_hbm, fv), (s_hbm, sv), (m_hbm, mv)))
    ]
    for step in pieces + ins:
        step.start()
    lo_out[...] = lo_ref[...]
    ig_out[...] = ig_ref[...]
    acc = gsum_ref[...]
    first = BETA_ONE * gf_ref[...] + (1.0 - BETA_ONE) * acc
    second = BETA_TWO * gs_ref[...] + (1.0 - BETA_TWO) * acc * acc
    nf_ref[...] = first
    ns_ref[...] = second
    u = first / (1.0 - BETA_ONE**STEP) / (jnp.sqrt(second / (1.0 - BETA_TWO**STEP)) + ADAM_EPS)
    ng_ref[...] = gain_ref[...] - GAIN_RATE * u
    owned = lax.fori_loop(0, ATT + 3 * FFT, lambda t, a: a + (own_ref[t] == slot).astype(jnp.int32), 0) > 0
    grad = g_ref[...].reshape(HD, D)
    rot = jnp.zeros((HD, D), F32)
    for step, r in zip(pieces, cuts):
        step.wait()
        lb[r] = lv[r].astype(BF)
        rot = rot + nn(grad[:, r], lb[r])
    ins[0].wait()
    right = rv[...].astype(BF)
    rot = nn(rot.T.astype(BF), right)
    ins[1].wait()
    ins[2].wait()
    first = BETA_ONE * fv[...] + (1.0 - BETA_ONE) * rot
    second = BETA_TWO * sv[...] + (1.0 - BETA_TWO) * rot * rot
    u = first / (1.0 - BETA_ONE**STEP) / (jnp.sqrt(second / (1.0 - BETA_TWO**STEP)) + ADAM_EPS)
    fv[...] = jnp.where(owned, first, fv[...])
    sv[...] = jnp.where(owned, second, sv[...])
    outs = [pltpu.make_async_copy(fv, fo_hbm, sem.at[5]), pltpu.make_async_copy(sv, so_hbm, sem.at[6])]
    for step in outs:
        step.start()
    turned = nt(u.astype(BF), right).astype(BF)
    ins[3].wait()
    for k, r in enumerate(cuts):
        back = nn(lb[r], turned)
        w = mv[r]
        mv[r] = jnp.where(owned, w - RATE * (back + DECAY * w), w)
        outs.append(pltpu.make_async_copy(mv.at[r], mo_hbm.at[r], sem.at[12 + k]))
        outs[-1].start()
    for step in outs:
        step.wait()


def run_step(owners, grad, gsum, gains, gain_first, gain_second, lo, ig, left, right, master, first, second):
    f = jax.ShapeDtypeStruct
    vm = pltpu.VMEM
    tile = f((D, HD), F32)
    row = f((40, 128), F32)
    return pl.pallas_call(
        step_body,
        out_shape=(tile, tile, tile, row, row, row, f((TOK, D), BF), f((TOK, D), F32)),
        in_specs=[pl.BlockSpec(memory_space=pltpu.SMEM)] + [INV] * 7 + [ANY] * 5,
        out_specs=(ANY, ANY, ANY, INV, INV, INV, INV, INV),
        scratch_shapes=[
            vm((D, D), F32), vm((HD, HD), F32), vm((D, HD), F32), vm((D, HD), F32), vm((D, HD), F32), vm((D, D), BF),
            DMA((16,)),
        ],
        compiler_params=pltpu.CompilerParams(vmem_limit_bytes=VMEM_LIMIT),
    )(owners, grad, gsum, gains, gain_first, gain_second, lo, ig, left, right, master, first, second)


def local(
    inputs,
    out_grad,
    doc_ids,
    owners,
    masters,
    first_old,
    second_old,
    left_basis,
    right_basis,
    gains,
    gain_first,
    gain_second,
):
    x = inputs[0]
    row = gains.reshape(1, 5120)
    lo, ig, gsum, grad, _ = run_layer(doc_ids, owners, masters[0], x, out_grad[0], row, 1)
    square = [a.reshape(40, 128) for a in (gains, gain_first, gain_second)]
    new_masters, new_first, new_second, new_gains, new_gain_first, new_gain_second, layer_out, input_grad = run_step(
        owners, grad, gsum, *square, lo, ig, left_basis[0], right_basis[0], masters[0], first_old[0], second_old[0]
    )
    return (
        layer_out[None],
        input_grad[None],
        new_masters[None],
        new_first[None],
        new_second[None],
        new_gains.reshape(5120),
        new_gain_first.reshape(5120),
        new_gain_second.reshape(5120),
    )


def solution(mesh):
    wide = Mesh(mesh.devices.reshape(4, 4, 2, 2, 2), AXES)
    tokens = P("xl", ("y", "z", "xh", "core"), None)
    held = P(AXES, None, None)
    return jax.shard_map(
        local,
        mesh=wide,
        in_specs=(tokens, tokens, P("xl", None), P(), held, held, held, held, held, P(), P(), P()),
        out_specs=(tokens, tokens, held, held, held, P(), P(), P()),
        check_vma=False,
    )
```

```python
import functools

import jax
import jax.numpy as jnp
from jax import lax
from jax.experimental import pallas as pl
from jax.experimental.pallas import tpu as pltpu
from jax.sharding import Mesh
from jax.sharding import PartitionSpec as P

FF = 6912
HEADS = 4
WINDOW = 512
BLK = 64
STEP = 10
D = 1152
HD = 256
TOK = 128
GROUP = 8
SLICE = HD // GROUP
ATT = 2 * HEADS + 2
FFT = FF // HD

NORM_EPS = 1e-06
THETA = 10000.0
BETA_ONE = 0.5
BETA_TWO = 0.5
RATE = 0.02
GAIN_RATE = 0.4
DECAY = 0.01
ADAM_EPS = 1e-08

MESH = pl.DeviceIdType.MESH
AXES = ("y", "z", "xh", "core", "xl")
VMEM_LIMIT = 63 * 1024 * 1024
BF = jnp.bfloat16
F32 = jnp.float32


def here():
    y, z, xh, c, xl = [lax.axis_index(a) for a in AXES]
    return y, z, xh * 2 + xl, c


def place(y, z, x, c):
    return (y, z, x // 2, c, lax.rem(x, 2))


def member(x, c):
    return (x // 2) * 4 + c * 2 + lax.rem(x, 2)


def turn(a, d):
    return lax.rem(a + d, 4)


def remote(src, dst, send, recv, where):
    return pltpu.make_async_remote_copy(src, dst, send, recv, device_id=where, device_id_type=MESH)


def params(cid):
    return pltpu.CompilerParams(
        collective_id=cid, has_side_effects=True, vmem_limit_bytes=VMEM_LIMIT
    )


ANY = pl.BlockSpec(memory_space=pl.ANY)
INV = pl.BlockSpec(memory_space=pltpu.VMEM)
DMA = pltpu.SemaphoreType.DMA


def seq_place(s):
    return (s // 16, lax.rem(s // 4, 4), lax.rem(s // 2, 2), lax.rem(s, 2), lax.axis_index("xl"))


def seq_index():
    y, z, xh, c, xl = [lax.axis_index(a) for a in AXES]
    return ((y * 4 + z) * 2 + xh) * 2 + c


def norm_of(v, g):
    return v * lax.rsqrt(jnp.mean(v * v, axis=-1, keepdims=True) + NORM_EPS) * g


def norm_back(v, g, w):
    r = lax.rsqrt(jnp.mean(v * v, axis=-1, keepdims=True) + NORM_EPS)
    u = w * g
    dg = jnp.sum(w * (v * r), axis=0, keepdims=True)
    dv = r * u - v * (r * r * r * jnp.mean(u * v, axis=-1, keepdims=True))
    return dv, dg


def column(g_ref, i):
    row = g_ref[:, 4 * D + i * HD : 4 * D + (i + 1) * HD]
    return jnp.broadcast_to(row, (128, HD)).T[:, 0:1]


def rope_norm(v, g, cos, sin):
    n = v * lax.rsqrt(jnp.mean(v * v, axis=0, keepdims=True) + NORM_EPS) * g
    a, b = n[: HD // 2], n[HD // 2 :]
    return jnp.concatenate([a * cos - b * sin, b * cos + a * sin], axis=0)


def gelu_parts(g):
    k, a = 0.7978845608028654, 0.044715
    sq = g * g
    th = jnp.tanh(k * g * (1.0 + a * sq))
    half = 0.5 * (1.0 + th)
    slope = half + 0.5 * g * (1.0 - th * th) * (k * (1.0 + 3.0 * a * sq))
    return g * half, slope


def nn(a, b):
    return jnp.dot(a, b, preferred_element_type=F32)


def nt(a, b):
    return lax.dot_general(a, b, (((1,), (1,)), ((), ())), preferred_element_type=F32)


def rope_norm_back(v, g, cos, sin, w):
    r = lax.rsqrt(jnp.mean(v * v, axis=0, keepdims=True) + NORM_EPS)
    a, b = w[: HD // 2], w[HD // 2 :]
    dn = jnp.concatenate([a * cos + b * sin, b * cos - a * sin], axis=0)
    dg = jnp.sum(dn * (v * r), axis=1, keepdims=True)
    u = dn * g
    dv = r * u - v * (r * r * r * jnp.mean(u * v, axis=0, keepdims=True))
    return dv, dg


def rows_add(dst, srcs, n):
    def step(i, carry):
        t = dst[i].astype(F32)
        for s in srcs:
            t = t + s[i].astype(F32)
        dst[i] = t.astype(BF)
        return carry

    lax.fori_loop(0, n, step, 0)


ORDER = (0, 3, 1, 2)
JS = (2, 1, 3, 0)
FFW = FFT * SLICE
ROWS = TOK // SLICE


def layer_body(
    doc_ref, own_ref, m_ref, x_ref, y_ref, g_ref,
    lo_ref, ig_ref, gsum_ref, grad_ref, xa_hbm,
    tile, grp, tile_of, tile_ref, wall, wf, xf, dd, dap_all, ab, bb, sbuf, near, far, t1, t2, u1, u2, fin,
    wo, ptl, qt, kb, vt, raw, oto, osl, sq, watt, dst, dot_, hsend, hrec, dqk, drec, dsl,
    da, a1, amid, a2, att, gl, gin, gmid, gin2,
    load_sem, ts, tr, n1s, n1r, n2s, n2r, n3s, n3r, n4s, n4r, xxs, xxr, xcs, xcr, c1s, c1r, c2s, c2r, c3s, c3r, c4s, c4r,
    as_, ar, wxs, wxr, wcs, wcr, hs, hr, os_, or_, fxs, fxr, fcs, fcr, bxs, bxr, bcs, bcr,
    ss, sr, rs_, rr, axs, axr, acs, acr, hbs, hbr, qs, qr, g1s, g1r, g2s, g2r, k1s, k1r, k2s, k2r,
    fs, fr, gas, gar, gbs, gbr,
):
    y, z, x, c = here()
    me = x * 2 + c
    twin = place(y, z, x, 1 - c)
    s = seq_index()
    chips = {d: turn(x, d) for d in range(4)}
    peers = {d: place(y, z, chips[d], c) for d in (1, 2, 3)}
    others = [(d, cc) for d in (2, 1, 3) for cc in range(2)]
    field = [(o - 1, place(turn(y, o // 4), turn(z, o % 4), x, c)) for o in range(1, 16)]
    mine_k = y * 4 + z
    at = (y, z)
    ring = (
        {d: place(turn(y, d), z, x, c) for d in (1, 2, 3)},
        {d: place(y, turn(z, d), x, c) for d in (1, 2, 3)},
    )
    partners = (
        [place(y, z, chips[d], cc) for d, cc in others]
        + [twin]
        + [seq_place(lax.rem(s + 64 + d, 64)) for d in (-4, -3, -2, -1, 1, 2, 3, 4)]
        + [f[1] for f in field]
    )
    sem = pltpu.get_barrier_semaphore()
    for p in partners:
        pl.semaphore_signal(sem, inc=1, device_id=p, device_id_type=MESH)
    for h in range(2):
        tile[4 * h : 4 * h + 4] = m_ref[:, h * 128 : (h + 1) * 128].T.astype(BF).reshape(4, SLICE, D)
    pl.semaphore_wait(sem, len(partners))
    sent = []

    def go(step):
        step.start()
        sent.append(step)
        return step

    def settle(steps):
        for step in steps:
            step.wait_send()
        sent[:] = [a for a in sent if not any(a is b for b in steps)]

    mm = member(x, c)
    base = mine_k * GROUP
    for d, cc in others:
        go(remote(tile.at[chips[d] * 2 + cc], grp.at[mm], ts.at[d, cc], tr.at[d, c], place(y, z, chips[d], cc)))
    go(remote(tile.at[x * 2 + 1 - c], grp.at[mm], ts.at[0, 0], tr.at[0, c], twin))
    grp[mm] = tile[me]
    dd[x, c] = norm_of(x_ref[...].astype(F32), g_ref[:, 0:D]).astype(BF)
    mine = dd.at[x, c]
    x_far = {d: go(remote(mine, mine, xxs.at[d - 1], xxr.at[d - 1], peers[d])) for d in (1, 3, 2)}
    x_near = {0: go(remote(mine, mine, xcs.at[0], xcr.at[0], twin))}
    pos = s * TOK + lax.broadcasted_iota(jnp.int32, (HD // 2, TOK), 1)
    freq = lax.broadcasted_iota(jnp.int32, (HD // 2, TOK), 0).astype(F32)
    angle = pos.astype(F32) * jnp.exp(-jnp.log(THETA) * freq * 2.0 / HD)
    cos, sin = jnp.cos(angle), jnp.sin(angle)
    lane = lax.broadcasted_iota(jnp.int32, (1, 128), 1)
    tile_of[...] = lax.fori_loop(
        0,
        ATT + 3 * FFT,
        lambda t, acc: jnp.where(lane == own_ref[t], t, acc),
        jnp.zeros((1, 128), jnp.int32),
    )
    to_scalars = pltpu.make_async_copy(tile_of, tile_ref, load_sem.at[0])
    to_scalars.start()
    for d, cc in others:
        remote(tile.at[0], grp.at[mm], ts.at[d, cc], tr.at[d, cc], twin).wait_recv()
    remote(tile.at[0], grp.at[mm], ts.at[0, 0], tr.at[0, 1 - c], twin).wait_recv()
    def halves(h):
        return slice(h * 16, h * 16 + 16)

    def lay(t, v):
        for k in range(9):
            da[t * 9 + k] = v[:, k * 128 : (k + 1) * 128]

    def taken(t):
        return jnp.concatenate([att[t * 9 + k] for k in range(9)], axis=1)

    def set_out(ph):
        steps = []
        for d in (2, 1, 3):
            for h in (0, 1):
                src = da.at[pl.ds(24 * turn(at[h], d), 24), halves(h)]
                steps.append(go(remote(src, a1.at[ph, h, d - 1], c1s.at[ph, h, d - 1], c1r.at[ph, h, d - 1], ring[h][d])))
        return steps

    def add_up(ph, first):
        for step in first:
            step.wait_recv()
        for h in (0, 1):
            tot = da[pl.ds(24 * at[h], 24), halves(h)].astype(F32)
            for i in range(3):
                tot = tot + a1[ph, h, i].astype(F32)
            amid[h] = tot.astype(BF)
        steps = []
        for d in (2, 1, 3):
            for h in (0, 1):
                src = amid.at[h, pl.ds(6 * turn(at[1 - h], d), 6)]
                dst = a2.at[ph, h, d - 1]
                steps.append(go(remote(src, dst, c2s.at[ph, h, d - 1], c2r.at[ph, h, d - 1], ring[1 - h][d])))
        return steps

    def give(ph, second):
        for step in second:
            step.wait_recv()
        steps = []
        for h in (0, 1):
            tot = amid[h, pl.ds(6 * at[1 - h], 6)].astype(F32)
            for i in range(3):
                tot = tot + a2[ph, h, i].astype(F32)
            att[pl.ds(24 * at[h] + 6 * at[1 - h], 6), halves(h)] = tot.astype(BF)
            src = att.at[pl.ds(24 * at[h] + 6 * at[1 - h], 6), halves(h)]
            for d in (2, 1, 3):
                steps.append(go(remote(src, src, c3s.at[ph, h, d - 1], c3r.at[ph, h, d - 1], ring[1 - h][d])))
        return steps

    def give_on(ph, third):
        for step in third:
            step.wait_recv()
        steps = []
        for h in (0, 1):
            src = att.at[pl.ds(24 * at[h], 24), halves(h)]
            for d in (2, 1, 3):
                steps.append(go(remote(src, src, c4s.at[ph, h, d - 1], c4r.at[ph, h, d - 1], ring[h][d])))
        return steps

    for t in range(ATT):
        rel = own_ref[t] - base
        v = grp[jnp.clip(rel, 0, GROUP - 1)]
        lay(t, jnp.where((rel >= 0) & (rel < GROUP), v, jnp.zeros_like(v)))

    routed = set_out(0)
    wall[pl.ds(base, GROUP)] = grp[...]

    w_at = (z, y)
    f_at = {h: {d: turn(w_at[h], d) for d in range(4)} for h in (0, 1)}
    s_at = {h: {d: turn(w_at[1 - h], d) for d in range(4)} for h in (0, 1)}
    ways = ((0, 1, 3), (1, 3, 1))

    def block(h, first, second):
        yy, zz = (second, first) if h == 0 else (first, second)
        return wall.at[pl.ds(((yy * 4 + zz) * 2 + h) * 4, 4)]

    one, two, far1 = {}, {}, {}
    for h in (0, 1):
        for n, up, _ in ways:
            src = grp.at[4 * h : 4 * h + 4]
            one[h, n] = go(remote(src, block(h, f_at[h][0], s_at[h][0]), n1s.at[h, n], n1r.at[h, n], ring[1 - h][up]))

    def second(k):
        for h in (0, 1):
            b = block(h, f_at[h][k], s_at[h][0])
            src = b if k else grp.at[4 * h : 4 * h + 4]
            for n, up, _ in ways:
                two[h, k, n] = go(remote(src, b, n2s.at[h, k, n], n2r.at[h, k, n], ring[h][up]))

    def onward(k):
        for h in (0, 1):
            for n, up, down in ways:
                two[h, k, n].wait_recv()
                b = block(h, f_at[h][k], s_at[h][down]).at[2 * n : 2 * n + 2]
                last.append(go(remote(b, b, n4s.at[h, k, n], n4r.at[h, k, n], ring[h][up])))

    last = []
    for d in (1, 3, 2):
        x_far[d].wait_recv()
        src = dd.at[chips[4 - d], c]
        x_near[d] = go(remote(src, src, xcs.at[d], xcr.at[d], twin))
    added = add_up(0, routed)
    second(0)
    for h in (0, 1):
        for n, up, down in ways:
            one[h, n].wait_recv()
            b = block(h, f_at[h][down], s_at[h][0]).at[2 * n : 2 * n + 2]
            far1[h, n] = go(remote(b, b, n3s.at[h, n], n3r.at[h, n], ring[1 - h][up]))
    given = give(0, added)
    for step in x_near.values():
        step.wait_recv()
    save_x = pltpu.make_async_copy(dd, xa_hbm, load_sem.at[1])
    save_x.start()
    second(3)
    given_on = give_on(0, given)
    second(1)
    for step in given_on:
        step.wait_recv()

    for t in range(HEADS + 2):
        watt[t * SLICE : (t + 1) * SLICE] = taken(t)
    for h in range(HEADS):
        wo[h, me] = taken(HEADS + 2 + h)
    for d in (2, 1, 3, 0):
        part = nt(watt[...], dd[chips[d]].reshape(2 * TOK, D)).astype(BF)
        for cc in range(2):
            sq[d, cc] = part[:, cc * TOK : (cc + 1) * TOK].reshape(HEADS + 2, SLICE, TOK)
        if d:
            for cc in range(2):
                go(remote(sq.at[d, cc], raw.at[:, me], as_.at[d, cc], ar.at[d, c], place(y, z, chips[d], cc)))
    go(remote(sq.at[0, 1 - c], raw.at[:, me], as_.at[0, 0], ar.at[0, c], twin))
    raw[:, me] = sq[0, c]
    mine = wo.at[:, me]
    w_far = {d: go(remote(mine, mine, wxs.at[d - 1], wxr.at[d - 1], peers[d])) for d in (1, 3)}
    w_near = {0: go(remote(mine, mine, wcs.at[0], wcr.at[0], twin))}
    onward(0)
    for d, cc in others:
        remote(sq.at[d, cc], raw.at[:, me], as_.at[d, cc], ar.at[d, cc], twin).wait_recv()
    remote(sq.at[0, 0], raw.at[:, me], as_.at[0, 0], ar.at[0, 1 - c], twin).wait_recv()

    gain_q, gain_k = column(g_ref, 0), column(g_ref, 1)
    kt = rope_norm(raw[HEADS].reshape(HD, TOK).astype(F32), gain_k, cos, sin)
    kb[4] = kt.T.astype(BF)
    vt[:, 4 * TOK :] = raw[HEADS + 1].reshape(HD, TOK)
    halo = []
    for d in (4, 3, 2, 1):
        to = seq_place(lax.rem(s + d, 64))
        lanes = slice((4 - d) * TOK, (5 - d) * TOK)
        halo.append(go(remote(kb.at[4], kb.at[4 - d], hs.at[0, d - 1], hr.at[0, d - 1], to)))
        halo.append(go(remote(vt.at[:, 4 * TOK :], vt.at[:, lanes], hs.at[1, d - 1], hr.at[1, d - 1], to)))
    w_far[2] = go(remote(mine, mine, wxs.at[1], wxr.at[1], peers[2]))
    for step in far1.values():
        step.wait_recv()
    second(2)
    onward(3)
    onward(1)
    for h in range(HEADS):
        q = rope_norm(raw[h].reshape(HD, TOK).astype(F32), gain_q, cos, sin)
        qt[:, h * TOK : (h + 1) * TOK] = q.astype(BF)
    row = lax.broadcasted_iota(jnp.int32, (WINDOW + TOK, TOK), 0)
    col = lax.broadcasted_iota(jnp.int32, (WINDOW + TOK, TOK), 1)
    seen = (row <= col + WINDOW) & (row > col) & (row >= WINDOW - s * TOK)
    half = lax.broadcasted_iota(jnp.int32, (BLK, TOK), 1) < BLK
    q_doc = jnp.where(half, doc_ref[0, 2 * s], doc_ref[0, 2 * s + 1])
    k_doc = jnp.concatenate(
        [jnp.full((BLK, TOK), doc_ref[0, jnp.maximum(2 * s - 8 + b, 0)], jnp.int32) for b in range(10)],
        axis=0,
    )
    seen = seen & (k_doc == jnp.concatenate([q_doc] * 10, axis=0))
    for step in halo:
        step.wait_recv()
    keys = kb[...].reshape(WINDOW + TOK, HD)
    for h in range(HEADS):
        lanes = slice(h * TOK, (h + 1) * TOK)
        sc = nn(keys, qt[:, lanes]) * (HD**-0.5)
        sc = jnp.where(seen, sc, -1e30)
        ex = jnp.exp(sc - jnp.max(sc, axis=0, keepdims=True))
        ptl[:, lanes] = (ex / jnp.sum(ex, axis=0, keepdims=True)).astype(BF)
    ot = nn(vt[...], ptl[...])
    oto[...] = ot.astype(BF)
    for d, cc in others:
        rows = pl.ds(pl.multiple_of((chips[d] * 2 + cc) * SLICE, SLICE), SLICE)
        go(remote(oto.at[rows], osl.at[me], os_.at[d, cc], or_.at[d, c], place(y, z, chips[d], cc)))
    rows = pl.ds(pl.multiple_of((x * 2 + 1 - c) * SLICE, SLICE), SLICE)
    go(remote(oto.at[rows], osl.at[me], os_.at[0, 0], or_.at[0, c], twin))
    osl[me] = oto[pl.ds(pl.multiple_of(me * SLICE, SLICE), SLICE)]

    onward(2)
    for d in (1, 3, 2):
        w_far[d].wait_recv()
        src = wo.at[:, chips[4 - d] * 2 + c]
        w_near[d] = go(remote(src, src, wcs.at[d], wcr.at[d], twin))
    for step in w_near.values():
        step.wait_recv()
    ap = jnp.zeros((TOK, D), F32)
    for h in range(HEADS):
        o = ot[:, h * TOK : (h + 1) * TOK].T.astype(BF)
        ap = ap + nn(o, wo[h].reshape(HD, D))
    act = x_ref[...].astype(F32)
    r1 = act + norm_of(ap, g_ref[:, 1 * D : 2 * D])
    xf[x, c] = norm_of(r1, g_ref[:, 2 * D : 3 * D]).astype(BF)

    def gather_start(buf, xs, xr, cs, cr, first=(1, 3, 2)):
        own = buf.at[x, c]
        near_ = {0: go(remote(own, own, cs.at[0], cr.at[0], twin))}
        sends = {d: go(remote(own, own, xs.at[d - 1], xr.at[d - 1], peers[d])) for d in first}
        return sends, near_

    def gather_wait(buf, e, sends, near_, cs, cr):
        if e:
            d = 4 - e
            sends[d].wait_recv()
            src = buf.at[chips[e], c]
            near_[d] = go(remote(src, src, cs.at[d], cr.at[d], twin))
            near_[d].wait_recv()
        else:
            near_[0].wait_recv()

    def pbuf(ph, e, cc):
        return (wall if ph < 2 else wf).at[pl.ds((2 * e + cc) * ROWS, ROWS)]

    def sum_swap(ph, n, e):
        return go(remote(pbuf(ph, e, 1 - c), near.at[n, e], ss.at[ph, e], sr.at[ph, e], twin))

    def sum_send(ph, n, e, swap):
        swap.wait_recv()
        both = pbuf(ph, e, c)[...].astype(F32) + near[n, e].astype(F32)
        if not e:
            return None, both
        sbuf[e - 1] = both.astype(BF)
        return go(remote(sbuf.at[e - 1], far.at[n, e - 1], rs_.at[ph, e - 1], rr.at[ph, e - 1], peers[e])), None

    def finish(n, swaps, outs, ph, total=None):
        if total is None:
            _, total = sum_send(ph, n, 0, swaps[0])
            settle(list(swaps.values()))
        for step in outs:
            step.wait_recv()
        total = ((total + far[n, 0].astype(F32)) + far[n, 1].astype(F32)) + far[n, 2].astype(F32)
        settle(outs)
        return total.reshape(TOK, D)

    def pipeline(ph, order, ready, block):
        swaps, outs = {}, []
        for n, e in enumerate(order):
            ready(e)
            part = block(e).astype(BF).reshape(2, ROWS, SLICE, D)
            for cc in range(2):
                pbuf(ph, e, cc)[...] = part[cc]
            swaps[e] = sum_swap(ph, ph % 2, e)
            if n and order[n - 1]:
                outs.append(sum_send(ph, ph % 2, order[n - 1], swaps[order[n - 1]])[0])
        if order[3]:
            outs.append(sum_send(ph, ph % 2, order[3], swaps[order[3]])[0])
        return swaps, outs, ph

    def put(k, e, v):
        cols = pl.ds(pl.multiple_of(chips[e] * 2 * TOK, 2 * TOK), 2 * TOK)
        wall[32 + k * FFT : 32 + (k + 1) * FFT, :, cols] = v.T.reshape(FFT, SLICE, 2 * TOK)

    def tiles(k):
        return wf[k * FFT : (k + 1) * FFT].reshape(FFW, D)

    def forward(e):
        v = xf[chips[e]].reshape(2 * TOK, D)
        g = nt(v, tiles(0))
        u = nt(v, tiles(1))
        h, slope = gelu_parts(g)
        ab[e] = (u * slope).astype(BF)
        bb[e] = h.astype(BF)
        hid = (h * u).astype(BF)
        put(2, e, hid)
        return nn(hid, tiles(2))

    sends, near_ = gather_start(xf, fxs, fxr, fcs, fcr)
    for step in last:
        step.wait_recv()

    def pack(t, carry):
        wf[t] = wall[own_ref[ATT + t]]
        return carry

    lax.fori_loop(0, 3 * FFT, pack, 0)
    settle(list(two.values()) + list(far1.values()) + last + list(x_far.values()) + list(x_near.values()))
    save_x.wait()
    to_scalars.wait()
    settle(routed + added + given + given_on)
    state = pipeline(0, ORDER, lambda e: gather_wait(xf, e, sends, near_, fcs, fcr), forward)
    dn = finish(0, *state)
    lo_ref[...] = (r1 + norm_of(dn, g_ref[:, 3 * D : 4 * D])).astype(BF)
    cot = y_ref[...].astype(F32)
    ddn, d_fpost = norm_back(dn, g_ref[:, 3 * D : 4 * D], cot)
    dd[x, c] = ddn.astype(BF)

    def backward(e):
        v = dd[chips[e]].reshape(2 * TOK, D)
        dh = nt(v, tiles(2))
        dg = (dh * ab[e].astype(F32)).astype(BF)
        du = (dh * bb[e].astype(F32)).astype(BF)
        put(0, e, dg)
        put(1, e, du)
        return nn(dg, tiles(0)) + nn(du, tiles(1))

    sends_b, near_b = gather_start(dd, bxs, bxr, bcs, bcr)
    state = pipeline(1, ORDER, lambda e: gather_wait(dd, e, sends_b, near_b, bcs, bcr), backward)

    for k, rhs in enumerate((xf, xf, dd)):
        left = wall[32 + k * FFT : 32 + (k + 1) * FFT, :, 0 : GROUP * TOK].reshape(FFW, GROUP * TOK)
        for n in range(3):
            cols = slice(n * 384, (n + 1) * 384)
            g = nn(left, rhs[:, :, :, cols].reshape(GROUP * TOK, 384)).astype(BF)
            wf[k * FFT : (k + 1) * FFT, :, cols] = g.reshape(FFT, SLICE, 384)
    _, rest = sum_send(1, 1, 0, state[0][0])
    settle(list(state[0].values()))

    def fill(i, carry):
        wall[i] = wf[jnp.clip(tile_ref[0, i] - ATT, 0, 3 * FFT - 1)]
        return carry

    lax.fori_loop(0, 128, fill, 0)

    def part(h, first, second):
        yy, zz = (first, second) if h == 0 else (second, first)
        return wall.at[pl.ds(((yy * 4 + zz) * 2 + h) * 4, 4)]

    here1 = {h: {d: turn(at[h], d) for d in range(4)} for h in (0, 1)}
    here2 = {h: {d: turn(at[1 - h], d) for d in range(4)} for h in (0, 1)}
    s1 = {}
    for j in JS:
        for h in (0, 1):
            blk = part(h, here1[h][2], here2[h][j])
            s1[h, j, 0] = go(remote(blk.at[0:2], t1.at[h, j, 0], g1s.at[h, j, 0], g1r.at[h, j, 0], ring[h][1]))
            s1[h, j, 1] = go(remote(blk.at[2:4], t1.at[h, j, 1], g1s.at[h, j, 1], g1r.at[h, j, 1], ring[h][3]))

    dxf = finish(1, *state, rest)
    e1, d_fpre = norm_back(r1, g_ref[:, 2 * D : 3 * D], dxf)
    dr1 = cot + e1
    ig_ref[...] = dr1
    dap, d_apost = norm_back(ap, g_ref[:, 1 * D : 2 * D], dr1)
    dap_all[x, c] = dap.astype(BF)
    sends_a, near_a = gather_start(dap_all, axs, axr, acs, acr, (1, 3))

    dmix = nt(wo[...].reshape(HEADS * HD, D), dap.astype(BF)).astype(BF)
    for h in range(HEADS):
        dot_[:, h * TOK : (h + 1) * TOK] = dmix[h * HD : (h + 1) * HD]
    values = jnp.concatenate([vt[:, b * TOK : (b + 1) * TOK].T for b in range(5)], axis=0)
    for h in range(HEADS):
        lanes = slice(h * TOK, (h + 1) * TOK)
        pr = ptl[:, lanes].astype(F32)
        dp = nn(values, dot_[:, lanes])
        inner = jnp.sum(pr * dp, axis=0, keepdims=True)
        dst[:, lanes] = (pr * (dp - inner) * (HD**-0.5)).astype(BF)
    dk = nt(qt[...], dst[...])
    dv = nt(dot_[...], ptl[...])
    back = []
    for d in (4, 3, 2, 1):
        lanes = slice((4 - d) * TOK, (5 - d) * TOK)
        hsend[d - 1, 0] = dk[:, lanes].astype(BF)
        hsend[d - 1, 1] = dv[:, lanes].astype(BF)
        to = seq_place(lax.rem(s + 64 - d, 64))
        back.append(go(remote(hsend.at[d - 1], hrec.at[d - 1], hbs.at[d - 1], hbr.at[d - 1], to)))
    dk = dk[:, 4 * TOK :]
    dv = dv[:, 4 * TOK :]
    own = dap_all.at[x, c]
    sends_a[2] = go(remote(own, own, axs.at[1], axr.at[1], peers[2]))

    s2 = {}

    def pass_on(j):
        for h in (0, 1):
            s1[h, j, 0].wait_recv()
            blk = part(h, here1[h][1], here2[h][j])
            rows_add(blk.at[0:2], [t1.at[h, j, 0]], 2)
            s2[h, j, 0] = go(remote(blk, t2.at[h, j, 0], g2s.at[h, j, 0], g2r.at[h, j, 0], ring[h][1]))
            s1[h, j, 1].wait_recv()
            blk = part(h, here1[h][3], here2[h][j])
            rows_add(blk.at[2:4], [t1.at[h, j, 1]], 2)
            s2[h, j, 1] = go(remote(blk, t2.at[h, j, 1], g2s.at[h, j, 1], g2r.at[h, j, 1], ring[h][3]))

    pass_on(2)
    settle(list(sends.values()) + list(near_.values()))
    load_x = pltpu.make_async_copy(xa_hbm, xf, load_sem.at[2])
    load_x.start()
    keys_t = jnp.concatenate([kb[b].T for b in range(5)], axis=1)
    dgq = jnp.zeros((HD, 1), F32)
    for h in range(HEADS):
        dq = nn(keys_t, dst[:, h * TOK : (h + 1) * TOK])
        dq, dg = rope_norm_back(raw[h].reshape(HD, TOK).astype(F32), gain_q, cos, sin, dq)
        dqk[h] = dq.astype(BF).reshape(GROUP, SLICE, TOK)
        dgq = dgq + dg

    pass_on(1)
    for step in back:
        step.wait_recv()
    for d in range(4):
        dk = dk + hrec[d, 0].astype(F32)
        dv = dv + hrec[d, 1].astype(F32)
    dk, dgk = rope_norm_back(raw[HEADS].reshape(HD, TOK).astype(F32), gain_k, cos, sin, dk)
    dqk[HEADS] = dk.astype(BF).reshape(GROUP, SLICE, TOK)
    dqk[HEADS + 1] = dv.astype(BF).reshape(GROUP, SLICE, TOK)
    for d, cc in others:
        to = chips[d] * 2 + cc
        go(remote(dqk.at[:, to], drec.at[me], qs.at[d, cc], qr.at[d, c], place(y, z, chips[d], cc)))
    go(remote(dqk.at[:, x * 2 + 1 - c], drec.at[me], qs.at[0, 0], qr.at[0, c], twin))
    drec[me] = dqk[:, me]

    pass_on(3)
    for e in (0, 3, 1, 2):
        gather_wait(dap_all, e, sends_a, near_a, acs, acr)
    for d, cc in others:
        remote(oto.at[0:SLICE], osl.at[me], os_.at[d, cc], or_.at[d, cc], twin).wait_recv()
    remote(oto.at[0:SLICE], osl.at[me], os_.at[0, 0], or_.at[0, 1 - c], twin).wait_recv()
    for h in range(HEADS):
        for p in range(GROUP):
            dsl[h * SLICE : (h + 1) * SLICE, p * TOK : (p + 1) * TOK] = osl[p, :, h * TOK : (h + 1) * TOK]
    g = nn(dsl[0 : HEADS * SLICE], dap_all[...].reshape(GROUP * TOK, D)).astype(BF)
    for h in range(HEADS):
        lay(HEADS + 2 + h, g[h * SLICE : (h + 1) * SLICE])

    pass_on(0)
    for d, cc in others:
        remote(dqk.at[:, 0], drec.at[me], qs.at[d, cc], qr.at[d, cc], twin).wait_recv()
    remote(dqk.at[:, 0], drec.at[me], qs.at[0, 0], qr.at[0, 1 - c], twin).wait_recv()
    for p in range(GROUP):
        dsl[:, p * TOK : (p + 1) * TOK] = drec[p].reshape((HEADS + 2) * SLICE, TOK)
    load_x.wait()
    g = nn(dsl[...], xf[...].reshape(GROUP * TOK, D)).astype(BF)
    for t in range(HEADS + 2):
        lay(t, g[t * SLICE : (t + 1) * SLICE])

    routed = set_out(1)

    def close(j):
        for h in (0, 1):
            s2[h, j, 0].wait_recv()
            s2[h, j, 1].wait_recv()
            rows_add(part(h, here1[h][0], here2[h][j]), [t2.at[h, j, 0], t2.at[h, j, 1]], 4)

    e1, e2 = {}, {}
    close(2)
    for h in (0, 1):
        blk = part(h, here1[h][0], here2[h][2])
        e1[h, 0] = go(remote(blk.at[0:2], u1.at[h, 0], k1s.at[h, 0], k1r.at[h, 0], ring[1 - h][1]))
        e1[h, 1] = go(remote(blk.at[2:4], u1.at[h, 1], k1s.at[h, 1], k1r.at[h, 1], ring[1 - h][3]))

    def inputs_back(e):
        pair = [
            nn(drec[chips[e] * 2 + cc].reshape((HEADS + 2) * SLICE, TOK).T, watt[...]) for cc in range(2)
        ]
        return jnp.concatenate(pair, axis=0)

    state = pipeline(2, JS, lambda e: None, inputs_back)

    added = add_up(1, routed)

    close(1)
    close(3)
    given = give(1, added)
    for n, j in ((0, 1), (1, 3)):
        for h in (0, 1):
            blk = part(h, here1[h][0], here2[h][j])
            e1[h, n].wait_recv()
            rows_add(blk.at[2 * n : 2 * n + 2], [u1.at[h, n]], 2)
            e2[h, n] = go(remote(blk, u2.at[h, n], k2s.at[h, n], k2r.at[h, n], ring[1 - h][j]))

    given_on = give_on(1, given)
    dxa = finish(0, *state)
    ein, d_apre = norm_back(x_ref[...].astype(F32), g_ref[:, 0 * D : 1 * D], dxa)
    ig_ref[...] = ig_ref[...] + ein
    for k in range(9):
        lanes = slice(k * 128, (k + 1) * 128)
        for m, dg in enumerate((d_apre, d_apost, d_fpre, d_fpost)):
            gl[9 * m + k : 9 * m + k + 1] = dg[:, lanes]
    for m, dg in enumerate((dgq, dgk)):
        flat = jnp.broadcast_to(dg, (HD, 128)).T
        for k in range(2):
            gl[36 + 2 * m + k : 37 + 2 * m + k] = flat[0:1, k * 128 : (k + 1) * 128]
    for d, cc in others:
        go(remote(gl, gin.at[x, c], gas.at[d, cc], gar.at[d, c], place(y, z, chips[d], cc)))
    go(remote(gl, gin.at[x, c], gas.at[0, 0], gar.at[0, c], twin))
    gin[x, c] = gl[...]

    for d, cc in others:
        remote(gl, gin.at[x, c], gas.at[d, cc], gar.at[d, cc], twin).wait_recv()
    remote(gl, gin.at[x, c], gas.at[0, 0], gar.at[0, 1 - c], twin).wait_recv()
    acc = gin[0, 0]
    for p in range(1, GROUP):
        acc = acc + gin[p // 2, p % 2]
    gmid[...] = acc
    gin2[mine_k] = acc
    all_gains = [go(remote(gmid, gin2.at[mine_k], gbs.at[o], gbr.at[o], to)) for o, to in field]
    close(0)

    for step in given_on:
        step.wait_recv()
    for h in (0, 1):
        e2[h, 0].wait_recv()
        e2[h, 1].wait_recv()
        blk = part(h, here1[h][0], here2[h][0])
        rows_add(blk, [u2.at[h, 0], u2.at[h, 1]], 4)
    for q in range(GROUP):
        t = tile_ref[0, base + q]
        low = taken(jnp.clip(t, 0, ATT - 1))
        fin[q] = jnp.where(t < ATT, low, wall[base + q])
    for d, cc in others:
        src = fin.at[member(chips[d], cc)]
        go(remote(src, grad_ref.at[me], fs.at[d, cc], fr.at[d, c], place(y, z, chips[d], cc)))
    go(remote(fin.at[member(x, 1 - c)], grad_ref.at[me], fs.at[0, 0], fr.at[0, c], twin))
    grad_ref[me] = fin[member(x, c)]
    for step in all_gains:
        step.wait_recv()
    acc = gin2[0]
    for k in range(1, 16):
        acc = acc + gin2[k]
    gsum_ref[...] = acc
    for d, cc in others:
        remote(fin.at[0], grad_ref.at[me], fs.at[d, cc], fr.at[d, cc], twin).wait_recv()
    remote(fin.at[0], grad_ref.at[me], fs.at[0, 0], fr.at[0, 1 - c], twin).wait_recv()
    for step in sent:
        step.wait_send()


def run_layer(doc, owners, master, x, y, gains, cid):
    f = jax.ShapeDtypeStruct
    smem = pl.BlockSpec(memory_space=pltpu.SMEM)
    vm = pltpu.VMEM
    blocks = (TOK // SLICE, SLICE, D)
    lanes = HEADS * TOK
    seen = WINDOW + TOK
    qkv = HEADS + 2
    return pl.pallas_call(
        layer_body,
        out_shape=(
            f((TOK, D), BF),
            f((TOK, D), F32),
            f((40, 128), F32),
            f((GROUP, SLICE, D), BF),
            f((4, 2, TOK, D), BF),
        ),
        in_specs=[smem, smem, INV, INV, INV, INV],
        out_specs=(INV, INV, INV, INV, ANY),
        scratch_shapes=[
            vm((GROUP, SLICE, D), BF),
            vm((GROUP, SLICE, D), BF),
            vm((1, 128), jnp.int32),
            pltpu.SMEM((1, 128), jnp.int32),
            vm((128, SLICE, D), BF),
            vm((3 * FFT, SLICE, D), BF),
            vm((4, 2, TOK, D), BF),
            vm((4, 2, TOK, D), BF),
            vm((4, 2, TOK, D), BF),
            vm((4, 2 * TOK, FFW), BF),
            vm((4, 2 * TOK, FFW), BF),
            vm((3,) + blocks, BF),
            vm((2, 4) + blocks, BF),
            vm((2, 3) + blocks, BF),
            vm((2, 4, 2, 2, SLICE, D), BF),
            vm((2, 4, 2, 4, SLICE, D), BF),
            vm((2, 2, 2, SLICE, D), BF),
            vm((2, 2, 4, SLICE, D), BF),
            vm((GROUP, SLICE, D), BF),
            vm((HEADS, GROUP, SLICE, D), BF),
            vm((seen, lanes), BF),
            vm((HD, lanes), BF),
            vm((5, TOK, HD), BF),
            vm((HD, seen), BF),
            vm((qkv, GROUP, SLICE, TOK), BF),
            vm((HD, lanes), BF),
            vm((GROUP, SLICE, lanes), BF),
            vm((4, 2, qkv, SLICE, TOK), BF),
            vm((qkv * SLICE, D), BF),
            vm((seen, lanes), BF),
            vm((HD, lanes), BF),
            vm((4, 2, HD, TOK), BF),
            vm((4, 2, HD, TOK), BF),
            vm((qkv, GROUP, SLICE, TOK), BF),
            vm((GROUP, qkv, SLICE, TOK), BF),
            vm((qkv * SLICE, GROUP * TOK), BF),
            vm((96, SLICE, 128), BF),
            vm((2, 2, 3, 24, 16, 128), BF),
            vm((2, 24, 16, 128), BF),
            vm((2, 2, 3, 6, 16, 128), BF),
            vm((96, SLICE, 128), BF),
            vm((40, 128), F32),
            vm((4, 2, 40, 128), F32),
            vm((40, 128), F32),
            vm((16, 40, 128), F32),
            DMA((3,)),
            DMA((4, 2)), DMA((4, 2)),
            DMA((2, 2)), DMA((2, 2)), DMA((2, 4, 2)), DMA((2, 4, 2)),
            DMA((2, 2)), DMA((2, 2)), DMA((2, 4, 2)), DMA((2, 4, 2)),
            DMA((3,)), DMA((3,)), DMA((4,)), DMA((4,)),
            DMA((2, 2, 3)), DMA((2, 2, 3)), DMA((2, 2, 3)), DMA((2, 2, 3)),
            DMA((2, 2, 3)), DMA((2, 2, 3)), DMA((2, 2, 3)), DMA((2, 2, 3)),
            DMA((4, 2)), DMA((4, 2)),
            DMA((3,)), DMA((3,)), DMA((4,)), DMA((4,)),
            DMA((2, 4)), DMA((2, 4)),
            DMA((4, 2)), DMA((4, 2)),
            DMA((3,)), DMA((3,)), DMA((4,)), DMA((4,)),
            DMA((3,)), DMA((3,)), DMA((4,)), DMA((4,)),
            DMA((3, 4)), DMA((3, 4)), DMA((3, 3)), DMA((3, 3)),
            DMA((3,)), DMA((3,)), DMA((4,)), DMA((4,)),
            DMA((4,)), DMA((4,)),
            DMA((4, 2)), DMA((4, 2)),
            DMA((2, 4, 2)), DMA((2, 4, 2)), DMA((2, 4, 2)), DMA((2, 4, 2)),
            DMA((2, 2)), DMA((2, 2)), DMA((2, 2)), DMA((2, 2)),
            DMA((4, 2)), DMA((4, 2)),
            DMA((4, 2)), DMA((4, 2)),
            DMA((15,)), DMA((15,)),
        ],
        compiler_params=params(cid),
    )(doc, owners, master, x, y, gains)


def step_body(
    own_ref, g_ref, gsum_ref, gain_ref, gf_ref, gs_ref, lo_ref, ig_ref, l_hbm, r_hbm, m_hbm, f_hbm, s_hbm,
    mo_hbm, fo_hbm, so_hbm, ng_ref, nf_ref, ns_ref, lo_out, ig_out, lv, rv, mv, fv, sv, lb, sem,
):
    y, z, x, c = here()
    slot = (y * 4 + z) * GROUP + member(x, c)
    third = D // 3
    cuts = [slice(k * third, (k + 1) * third) for k in range(3)]
    pieces = [pltpu.make_async_copy(l_hbm.at[r], lv.at[r], sem.at[8 + k]) for k, r in enumerate(cuts)]
    ins = [
        pltpu.make_async_copy(a, b, sem.at[i])
        for i, (a, b) in enumerate(((r_hbm, rv), (f_hbm, fv), (s_hbm, sv), (m_hbm, mv)))
    ]
    for step in pieces + ins:
        step.start()
    lo_out[...] = lo_ref[...]
    ig_out[...] = ig_ref[...]
    acc = gsum_ref[...]
    first = BETA_ONE * gf_ref[...] + (1.0 - BETA_ONE) * acc
    second = BETA_TWO * gs_ref[...] + (1.0 - BETA_TWO) * acc * acc
    nf_ref[...] = first
    ns_ref[...] = second
    u = first / (1.0 - BETA_ONE**STEP) / (jnp.sqrt(second / (1.0 - BETA_TWO**STEP)) + ADAM_EPS)
    ng_ref[...] = gain_ref[...] - GAIN_RATE * u
    owned = lax.fori_loop(0, ATT + 3 * FFT, lambda t, a: a + (own_ref[t] == slot).astype(jnp.int32), 0) > 0
    grad = g_ref[...].reshape(HD, D)
    rot = jnp.zeros((HD, D), F32)
    for step, r in zip(pieces, cuts):
        step.wait()
        lb[r] = lv[r].astype(BF)
        rot = rot + nn(grad[:, r], lb[r])
    ins[0].wait()
    right = rv[...].astype(BF)
    rot = nn(rot.T.astype(BF), right)
    ins[1].wait()
    ins[2].wait()
    first = BETA_ONE * fv[...] + (1.0 - BETA_ONE) * rot
    second = BETA_TWO * sv[...] + (1.0 - BETA_TWO) * rot * rot
    u = first / (1.0 - BETA_ONE**STEP) / (jnp.sqrt(second / (1.0 - BETA_TWO**STEP)) + ADAM_EPS)
    fv[...] = jnp.where(owned, first, fv[...])
    sv[...] = jnp.where(owned, second, sv[...])
    outs = [pltpu.make_async_copy(fv, fo_hbm, sem.at[5]), pltpu.make_async_copy(sv, so_hbm, sem.at[6])]
    for step in outs:
        step.start()
    turned = nt(u.astype(BF), right).astype(BF)
    ins[3].wait()
    for k, r in enumerate(cuts):
        back = nn(lb[r], turned)
        w = mv[r]
        mv[r] = jnp.where(owned, w - RATE * (back + DECAY * w), w)
        outs.append(pltpu.make_async_copy(mv.at[r], mo_hbm.at[r], sem.at[12 + k]))
        outs[-1].start()
    for step in outs:
        step.wait()


def run_step(owners, grad, gsum, gains, gain_first, gain_second, lo, ig, left, right, master, first, second):
    f = jax.ShapeDtypeStruct
    vm = pltpu.VMEM
    tile = f((D, HD), F32)
    row = f((40, 128), F32)
    return pl.pallas_call(
        step_body,
        out_shape=(tile, tile, tile, row, row, row, f((TOK, D), BF), f((TOK, D), F32)),
        in_specs=[pl.BlockSpec(memory_space=pltpu.SMEM)] + [INV] * 7 + [ANY] * 5,
        out_specs=(ANY, ANY, ANY, INV, INV, INV, INV, INV),
        scratch_shapes=[
            vm((D, D), F32), vm((HD, HD), F32), vm((D, HD), F32), vm((D, HD), F32), vm((D, HD), F32), vm((D, D), BF),
            DMA((16,)),
        ],
        compiler_params=pltpu.CompilerParams(vmem_limit_bytes=VMEM_LIMIT),
    )(owners, grad, gsum, gains, gain_first, gain_second, lo, ig, left, right, master, first, second)


def local(
    inputs,
    out_grad,
    doc_ids,
    owners,
    masters,
    first_old,
    second_old,
    left_basis,
    right_basis,
    gains,
    gain_first,
    gain_second,
):
    x = inputs[0]
    row = gains.reshape(1, 5120)
    lo, ig, gsum, grad, _ = run_layer(doc_ids, owners, masters[0], x, out_grad[0], row, 1)
    square = [a.reshape(40, 128) for a in (gains, gain_first, gain_second)]
    new_masters, new_first, new_second, new_gains, new_gain_first, new_gain_second, layer_out, input_grad = run_step(
        owners, grad, gsum, *square, lo, ig, left_basis[0], right_basis[0], masters[0], first_old[0], second_old[0]
    )
    return (
        layer_out[None],
        input_grad[None],
        new_masters[None],
        new_first[None],
        new_second[None],
        new_gains.reshape(5120),
        new_gain_first.reshape(5120),
        new_gain_second.reshape(5120),
    )


def solution(mesh):
    wide = Mesh(mesh.devices.reshape(4, 4, 2, 2, 2), AXES)
    tokens = P("xl", ("y", "z", "xh", "core"), None)
    held = P(AXES, None, None)
    return jax.shard_map(
        local,
        mesh=wide,
        in_specs=(tokens, tokens, P("xl", None), P(), held, held, held, held, held, P(), P(), P()),
        out_specs=(tokens, tokens, held, held, held, P(), P(), P()),
        check_vma=False,
    )
```
